32 devices in a mesh: dp: 16 (over z, y, core), inner: 2 (over x).
Axes of the slice: x: 2, y: 2, z: 4, core: 2. Of those that a mesh axis runs over, the one named last changes fastest.
Arguments:
- target: bfloat16 [32, 1024, 512], P(('dp', 'inner')), may hold values from -6 to 6
- source: bfloat16 [32, 344, 512], P(('dp', 'inner')), may hold values from -6 to 6
- target_segment: int32 [32, 1024], P(('dp', 'inner')), may hold values from 0 to 11, as said below
- source_segment: int32 [32, 344], P(('dp', 'inner')), may hold values from 0 to 11, as said below
- source_keep: int32 [32, 344], P(('dp', 'inner')), may hold values from 0 to 1, as said below
- self_query: bfloat16 [512, 512], P('dp', 'inner'), may hold values from -0.25 to 0.25
- self_key: bfloat16 [512, 512], P('dp', 'inner'), may hold values from -0.25 to 0.25
- self_value: bfloat16 [512, 512], P('dp', 'inner'), may hold values from -0.25 to 0.25
- self_output: bfloat16 [512, 512], P('dp', 'inner'), may hold values from -1 to 1
- cross_query: bfloat16 [512, 512], P('dp', 'inner'), may hold values from -0.25 to 0.25
- cross_key: bfloat16 [512, 512], P('dp', 'inner'), may hold values from -0.25 to 0.25
- cross_value: bfloat16 [512, 512], P('dp', 'inner'), may hold values from -0.25 to 0.25
- cross_output: bfloat16 [512, 512], P('dp', 'inner'), may hold values from -1 to 1
- expand_weight: bfloat16 [512, 2048], P('dp', 'inner'), may hold values from -0.25 to 0.25
- shrink_weight: bfloat16 [2048, 512], P('dp', 'inner'), may hold values from -0.125 to 0.125
- norm_affine: bfloat16 [6, 512], P('inner', 'dp'), may hold values from -2 to 2
- cotangent: bfloat16 [32, 1024, 512], P(('dp', 'inner')), may hold values from -6 to 6
Outputs:
- output: bfloat16 [32, 1024, 512], P(('dp', 'inner'))
- target_gradient: float32 [32, 1024, 512], P(('dp', 'inner'))
- source_gradient: float32 [32, 344, 512], P(('dp', 'inner'))
- self_query_gradient: float32 [512, 512], P('dp', 'inner')
- self_key_gradient: float32 [512, 512], P('dp', 'inner')
- self_value_gradient: float32 [512, 512], P('dp', 'inner')
- self_output_gradient: float32 [512, 512], P('dp', 'inner')
- cross_query_gradient: float32 [512, 512], P('dp', 'inner')
- cross_key_gradient: float32 [512, 512], P('dp', 'inner')
- cross_value_gradient: float32 [512, 512], P('dp', 'inner')
- cross_output_gradient: float32 [512, 512], P('dp', 'inner')
- expand_weight_gradient: float32 [512, 2048], P('dp', 'inner')
- shrink_weight_gradient: float32 [2048, 512], P('dp', 'inner')
- norm_affine_gradient: float32 [6, 512], P('inner', 'dp')
The draws below stay inside these ranges and needn't reach their ends.
Inputs may be any that keep to these rules, and one draw needn't show every extreme that they name: In every row the numbers never fall, start at 0 and take every value up to 11; a row's documents appear in the same order in target_segment and source_segment. `source_segment`: same documents as target_segment; every document has at least one source position. `source_keep`: the first source position of every document is kept.
All inputs are finite; a program needn't handle non-finite values.
Results may differ from the reference program's by a relative error of at most 0.018.
Values may be sent and summed in bfloat16 or wider, within the bound.
No kernel may reach another device: no remote copies, remote signals or barrier semaphores. Data moves between devices by JAX's collectives and lax.ppermute only.
A program may use at most 192 MiB of HBM per device.

```python
import jax
import jax.numpy as jnp
from jax import lax

D = 512
HEADS = 8
HEAD_DIM = 64
FF = 2048
L = 1024
S = 344
DOCS = 12
ROWS = 32


def source_cuts(key):
    keys = jax.random.split(key, ROWS)

    def one_row(row_key):
        order = jax.random.permutation(row_key, jnp.arange(S - 1, dtype=jnp.int32))
        return jnp.sort(order[:DOCS - 1] + 1).astype(jnp.int32)
    return jax.vmap(one_row)(keys)


def segments_from(cuts, count):
    places = jnp.arange(count, dtype=jnp.int32)
    return jnp.sum((places[None, :, None] >= cuts[:, None, :]).astype(jnp.int32), axis=2).astype(jnp.int32)


def draw_source_segment(key, part):
    cuts = source_cuts(key)
    return segments_from(cuts, S)


def draw_target_segment(key, part):
    cuts = source_cuts(key)
    scaled = cuts * L // S
    return segments_from(scaled.astype(jnp.int32), L)


def draw_source_keep(key, part):
    cuts = source_cuts(key)
    key = jax.random.fold_in(key, 5)
    segs = segments_from(cuts, S)
    starts = jnp.concatenate([jnp.ones((ROWS, 1), dtype=bool), segs[:, 1:] != segs[:, :-1]], axis=1)
    coins = jax.random.randint(key, (ROWS, S), 0, 8)
    return ((coins > 0) | starts).astype(jnp.int32)


def draw_norm_affine(key, part):
    key = jax.random.fold_in(key, 6)
    gains = jax.random.uniform(key, (6, D), jnp.float32, 0.5, 1.5)
    shifts = jnp.clip(0.5 * jax.random.normal(jax.random.fold_in(key, 1), (6, D), jnp.float32), -2.0, 2.0)
    even = (jnp.arange(6) % 2 == 0)[:, None]
    return jnp.where(even, gains, shifts).astype(jnp.bfloat16)


def spiked(array, own_key, source, target, blocks, factor):
    def block_of(dim):
        return (jnp.arange(array.shape[dim]) // (array.shape[dim] // blocks)).reshape((-1,) + (1,) * (array.ndim - 1 - dim))

    one_side = jax.random.permutation(own_key, blocks)[block_of(target)]
    far = (block_of(target) + blocks // 2) % blocks
    return jnp.where((block_of(source) == one_side) | (block_of(source) == far), factor * array, array)


def level_of(rng, extent, pieces, low, high):
    factor_of, own = 1.0, jax.random.fold_in(rng, 6)
    for axis_at, blocks in pieces:
        draws = jnp.exp(jax.random.uniform(jax.random.fold_in(own, axis_at), (blocks,), jnp.float32, low / len(pieces), high / len(pieces)))
        factor_of = factor_of * jnp.repeat(draws, extent[axis_at] // blocks).reshape([-1 if axis == axis_at else 1 for axis in range(len(extent))])
    return factor_of


def normal_values(key, shape, width, most, cuts=(), kind=jnp.bfloat16):
    level = level_of(key, shape, cuts, -0.22, 0.18) if cuts else 1.0
    values = jax.random.normal(key, shape, jnp.float32) * width * level
    return jnp.minimum(jnp.maximum(values, -most), most).astype(kind)


def noise_with(key, dims, width, limit, pieces, heavy, held_as=jnp.bfloat16):
    entries = width * jax.random.normal(key, dims, jnp.float32)
    if pieces:
        entries = entries * level_of(key, dims, pieces, -0.22, 0.18)
    return jnp.clip(spiked(entries, jax.random.fold_in(key, 3), *heavy), -limit, limit).astype(held_as)


def setup_inputs(seed: int = 0) -> dict:
    seeds = jax.random.split(jax.random.key(seed), 18)
    target = normal_values(seeds[0], (ROWS, L, D), 1.0, 6.0, ((0, 32),))
    source = normal_values(seeds[1], (ROWS, S, D), 1.0, 6.0, ((0, 32),))
    target_segment = draw_target_segment(jax.random.fold_in(seeds[17], 71), 0)
    source_segment = draw_source_segment(jax.random.fold_in(seeds[17], 71), 0)
    source_keep = draw_source_keep(jax.random.fold_in(seeds[17], 71), 0)
    self_query = normal_values(seeds[5], (D, D), D ** -0.5, 0.25, ((0, 16), (1, 2)))
    self_key = normal_values(seeds[6], (D, D), D ** -0.5, 0.25, ((0, 16), (1, 2)))
    self_value = normal_values(seeds[7], (D, D), D ** -0.5, 0.25, ((0, 16), (1, 2)))
    self_output = normal_values(seeds[8], (D, D), (D // 16) ** -0.5, 1.0, ((0, 16), (1, 2)))
    cross_query = normal_values(seeds[9], (D, D), D ** -0.5, 0.25, ((0, 16), (1, 2)))
    cross_key = normal_values(seeds[10], (D, D), D ** -0.5, 0.25, ((0, 16), (1, 2)))
    cross_value = normal_values(seeds[11], (D, D), D ** -0.5, 0.25, ((0, 16), (1, 2)))
    cross_output = normal_values(seeds[12], (D, D), (D // 16) ** -0.5, 1.0, ((0, 16), (1, 2)))
    expand_weight = normal_values(seeds[13], (D, FF), D ** -0.5, 0.25, ((0, 16), (1, 2)))
    shrink_weight = normal_values(seeds[14], (FF, D), FF ** -0.5, 0.125, ((0, 16), (1, 2)))
    norm_affine = draw_norm_affine(jax.random.fold_in(seeds[17], 71), 0)
    cotangent = noise_with(seeds[16], (ROWS, L, D), 1.0, 6.0, ((0, 32),), (0, 2, 32, 2.75))
    return dict(target=target, source=source, target_segment=target_segment, source_segment=source_segment, source_keep=source_keep, self_query=self_query, self_key=self_key, self_value=self_value, self_output=self_output, cross_query=cross_query, cross_key=cross_key, cross_value=cross_value, cross_output=cross_output, expand_weight=expand_weight, shrink_weight=shrink_weight, norm_affine=norm_affine, cotangent=cotangent)


EPS = 1e-05
NEG = -1e+30
HIGH = lax.Precision.HIGHEST

@jax.custom_vjp
def low(v):
    return lax.optimization_barrier(v.astype(jnp.bfloat16)).astype(jnp.float32)

@jax.custom_vjp
def low_back(v):
    return v

def low_keep(v):
    return (low(v), None)

def low_pass(kept, grad):
    return (grad,)

def back_keep(v):
    return (v, None)

def back_low(kept, grad):
    return (low(grad),)
low.defvjp(low_keep, low_pass)
low_back.defvjp(back_keep, back_low)

def layer_norm(stream, gain, bias):
    centre = stream - lax.optimization_barrier(jnp.mean(stream, -1, keepdims=True))
    spread = lax.optimization_barrier(jnp.mean(centre * centre, -1, keepdims=True))
    return centre * lax.rsqrt(spread + EPS) * gain + bias

def matmul(left, right):
    return jnp.dot(left, right, precision=HIGH)

def attention(query, keys, values, allowed):
    length = query.shape[0]
    count = keys.shape[0]
    query_heads = query.reshape(length, HEADS, HEAD_DIM)
    key_heads = keys.reshape(count, HEADS, HEAD_DIM)
    value_heads = values.reshape(count, HEADS, HEAD_DIM)
    raw = jnp.einsum('qhd,khd->hqk', query_heads, key_heads, precision=HIGH) * 0.125
    scores = low_back(jnp.where(allowed[None], raw, NEG))
    top = lax.optimization_barrier(jnp.max(scores, -1, keepdims=True))
    expo = jnp.exp(scores - top)
    probs = expo / lax.optimization_barrier(jnp.sum(expo, -1, keepdims=True))
    mixed = jnp.einsum('hqk,khd->qhd', low(probs), value_heads, precision=HIGH)
    return mixed.reshape(length, HEADS * HEAD_DIM)

def row_layer(entry, weights):
    stream, encoded, target_segs, source_segs, keep_row = entry
    w_sq, w_sk, w_sv, w_so, w_cq, w_ck, w_cv, w_co, expand, shrink, affine = weights
    normed_one = low(layer_norm(stream, affine[0], affine[1]))
    query = low_back(low(matmul(normed_one, w_sq)))
    keys = low_back(low(matmul(normed_one, w_sk)))
    values = low_back(low(matmul(normed_one, w_sv)))
    same = target_segs[:, None] == target_segs[None, :]
    mixed = low_back(low(attention(query, keys, values, same)))
    first_sum = stream + low_back(matmul(mixed, w_so))
    normed_two = low(layer_norm(first_sum, affine[2], affine[3]))
    cross_q = low_back(low(matmul(normed_two, w_cq)))
    cross_k = low_back(low(matmul(encoded, w_ck)))
    cross_v = low_back(low(matmul(encoded, w_cv)))
    reach = (target_segs[:, None] == source_segs[None, :]) & (keep_row[None, :] > 0)
    cross_mixed = low_back(low(attention(cross_q, cross_k, cross_v, reach)))
    second_sum = first_sum + low_back(matmul(cross_mixed, w_co))
    normed_three = low(layer_norm(second_sum, affine[4], affine[5]))
    hidden = low_back(matmul(normed_three, expand))
    active = low(jax.nn.gelu(hidden))
    return second_sum + low_back(matmul(active, shrink))

def reference(target, source, target_segment, source_segment, source_keep, self_query, self_key, self_value, self_output, cross_query, cross_key, cross_value, cross_output, expand_weight, shrink_weight, norm_affine, cotangent):
    weights = tuple((w.astype(jnp.float32) for w in (self_query, self_key, self_value, self_output, cross_query, cross_key, cross_value, cross_output, expand_weight, shrink_weight, norm_affine)))
    stream = target.astype(jnp.float32)
    encoded = source.astype(jnp.float32)
    upstream = cotangent.astype(jnp.float32)

    def forward(stream_in, encoded_in, weight_set):

        def one_row(entry):
            return row_layer(entry, weight_set)
        step = jax.checkpoint(one_row)
        return lax.map(step, (stream_in, encoded_in, target_segment, source_segment, source_keep))
    result, pull = jax.vjp(forward, stream, encoded, weights)
    stream_grad, encoded_grad, weight_grads = pull(upstream)
    return (result.astype(jnp.bfloat16), stream_grad, encoded_grad, weight_grads[0], weight_grads[1], weight_grads[2], weight_grads[3], weight_grads[4], weight_grads[5], weight_grads[6], weight_grads[7], weight_grads[8], weight_grads[9], weight_grads[10])
```

```python
import functools

import jax
import jax.numpy as jnp
from jax import lax
from jax.experimental import pallas as pl
from jax.experimental.pallas import tpu as pltpu
from jax.sharding import Mesh
from jax.sharding import PartitionSpec as P

HEAD_DIM = 64
BLOCK = 512


EPS = 1e-05
NEG = -1e30


def layer_norm(stream, gain, bias):
    centre = stream - jnp.mean(stream, -1, keepdims=True)
    spread = jnp.mean(centre * centre, -1, keepdims=True)
    return centre * lax.rsqrt(spread + EPS) * gain + bias


def forward_dot(left, weight):
    return jnp.dot(left, weight, preferred_element_type=jnp.float32)


def weight_dot(left, right):
    return lax.dot_general(
        left, right, (((0,), (0,)), ((), ())), preferred_element_type=jnp.float32
    )


def input_dot(upstream, weight):
    return lax.dot_general(
        upstream, weight, (((1,), (1,)), ((), ())), preferred_element_type=jnp.float32
    )


SWAP = [(0, 1), (1, 0)]
SHIFTS = [[(i, (i + k) % 4) for i in range(4)] for k in range(4)]
CROSS = [[(i, i ^ k) for i in range(4)] for k in range(4)]


def along_line(array):
    return [array] + [lax.ppermute(array, "a", SHIFTS[k]) for k in (1, 2, 3)]


def along_plane(array):
    return [array] + [lax.ppermute(array, ("b", "i"), CROSS[k]) for k in (1, 2, 3)]


def across_cores(arrays):
    return arrays + [lax.ppermute(array, "c", SWAP) for array in arrays]


def fetch_line_first(shard):
    return across_cores(along_plane(jnp.stack(along_line(shard), 0)))


def fetch_plane_first(shard):
    return across_cores(along_line(jnp.stack(along_plane(shard), 0)))


def place_of(coords, line_first, part, entry):
    core, first = part // 4, part % 4
    back, plane = (entry, first) if line_first else (first, entry)
    line = (coords[0] - back) & 3
    outer = coords[1] ^ (plane >> 1)
    inner = coords[3] ^ (plane & 1)
    dp = (line * 2 + outer) * 2 + (coords[2] ^ core)
    return dp, inner


def assemble_kernel(line_first, rows, cols, coords, *refs):
    pieces, out, sems = refs[:8], refs[8], refs[9]
    copies = []
    for part in range(8):
        for entry in range(4):
            dp, inner = place_of(coords, line_first, part, entry)
            spot = out.at[
                :, pl.ds(pl.multiple_of(dp * rows, rows), rows), pl.ds(pl.multiple_of(inner * cols, cols), cols)
            ]
            copy = pltpu.make_async_copy(pieces[part].at[entry], spot, sems.at[part * 4 + entry])
            copy.start()
            copies.append(copy)
    for copy in copies:
        copy.wait()


def assemble(coords, pieces, line_first):
    _, count, rows, cols = pieces[0].shape
    return pl.pallas_call(
        functools.partial(assemble_kernel, line_first, rows, cols),
        out_shape=jax.ShapeDtypeStruct((count, rows * 16, cols * 2), pieces[0].dtype),
        in_specs=[pl.BlockSpec(memory_space=pltpu.SMEM)] + [pl.BlockSpec(memory_space=pl.ANY)] * 8,
        out_specs=pl.BlockSpec(memory_space=pl.ANY),
        scratch_shapes=[pltpu.SemaphoreType.DMA((32,))],
        name="assemble",
    )(coords, *pieces)


def pick(array, index, axis):
    return lax.dynamic_index_in_dim(array, index, axis, keepdims=False)


def plane_block(array, coords, step, cols):
    outer = coords[1] ^ (step >> 1)
    inner = coords[3] ^ (step & 1)
    array = pick(array, outer, array.ndim - 3)
    return lax.dynamic_slice_in_dim(array, inner * cols, cols, array.ndim - 1)


def spread_line(total, coords, axis):
    mine = pick(total, coords[0], axis)
    for k in (1, 2, 3):
        block = pick(total, (coords[0] + k) & 3, axis).astype(jnp.bfloat16)
        mine = mine + lax.ppermute(block, "a", SHIFTS[k]).astype(jnp.float32)
    return mine


def spread_plane(total, coords, cols):
    mine = plane_block(total, coords, 0, cols)
    for k in (1, 2, 3):
        block = plane_block(total, coords, k, cols).astype(jnp.bfloat16)
        mine = mine + lax.ppermute(block, ("b", "i"), CROSS[k]).astype(jnp.float32)
    return mine


def reduce_group(grads, coords, rest, plane_first=True):
    count, rows, cols = grads.shape
    shard, half = rows // 16, cols // 2
    blocks = grads.reshape(count, 4, 2, 2, shard, cols)
    away = pick(blocks, 1 - coords[2], 3).astype(jnp.bfloat16)
    total = pick(blocks, coords[2], 3).astype(jnp.float32)
    total = total + lax.ppermute(away, "c", SWAP).astype(jnp.float32)
    if plane_first:
        total = spread_line(spread_plane(total, coords, half), coords, 1)
    else:
        total = spread_plane(spread_line(total, coords, 1), coords, half)
    if rest > 1:
        total = lax.psum_scatter(total, "r", scatter_dimension=1, tiled=True)
    return total


def sum_all(array):
    for names, perms in (("c", [SWAP]), (("b", "i"), CROSS[1:]), ("a", SHIFTS[1:])):
        array = sum([lax.ppermute(array, names, perm) for perm in perms], array)
    return array


def pair_mask(query_segs, key_segs, keep_row):
    return (query_segs[:, None] == key_segs[None, :]) & (keep_row[None, :] > 0)


def pair_scores(query_block, key_rows, allowed):
    raw = (
        jnp.einsum("qhd,khd->hqk", query_block, key_rows, preferred_element_type=jnp.float32)
        * 0.125
    )
    return jnp.where(allowed[None], raw, NEG)


def slice_pair(array, row, column):
    count = array.shape[1]
    piece = lax.dynamic_slice(array, (row, 0, column), (1, count, 2 * HEAD_DIM))
    return piece[0].reshape(count, 2, HEAD_DIM)


def merge_heads(pieces, rows, count, width):
    pairs = width // (2 * HEAD_DIM)
    return (
        pieces.reshape(rows, pairs, count, 2 * HEAD_DIM)
        .transpose(0, 2, 1, 3)
        .reshape(rows, count, width)
    )


def attend(query, keys, values, query_segment, key_segment, key_keep):
    rows, length, width = query.shape
    pairs = width // (2 * HEAD_DIM)
    blocks = length // BLOCK

    def one_pair(index):
        row = index // pairs
        column = index % pairs * (2 * HEAD_DIM)
        query_rows = slice_pair(query, row, column)
        key_rows = slice_pair(keys, row, column)
        value_rows = slice_pair(values, row, column)
        query_segs = query_segment[row]
        key_segs = key_segment[row]
        keep_row = key_keep[row]
        mixed_parts = []
        total_parts = []
        for part in range(blocks):
            lower = part * BLOCK
            allowed = pair_mask(query_segs[lower : lower + BLOCK], key_segs, keep_row)
            scores = pair_scores(query_rows[lower : lower + BLOCK], key_rows, allowed)
            top = jnp.max(scores, -1, keepdims=True)
            expo = jnp.exp(scores - top)
            total = jnp.sum(expo, -1, keepdims=True)
            probs = (expo / total).astype(jnp.bfloat16)
            mixed = jnp.einsum(
                "hqk,khd->qhd", probs, value_rows, preferred_element_type=jnp.float32
            )
            mixed_parts.append(mixed.reshape(BLOCK, 2 * HEAD_DIM))
            total_parts.append((top + jnp.log(total))[:, :, 0])
        return (jnp.concatenate(mixed_parts, 0), jnp.concatenate(total_parts, 1))

    mixed, log_total = lax.map(one_pair, jnp.arange(rows * pairs, dtype=jnp.int32))
    return (merge_heads(mixed, rows, length, width), log_total)


def attend_back(query, keys, values, mixed_back, log_total, query_segment, key_segment, key_keep):
    rows, length, width = query.shape
    count = keys.shape[1]
    pairs = width // (2 * HEAD_DIM)
    blocks = length // BLOCK

    def one_pair(index):
        row = index // pairs
        column = index % pairs * (2 * HEAD_DIM)
        query_rows = slice_pair(query, row, column)
        key_rows = slice_pair(keys, row, column)
        value_rows = slice_pair(values, row, column)
        back_rows = slice_pair(mixed_back, row, column)
        totals = log_total[index]
        query_segs = query_segment[row]
        key_segs = key_segment[row]
        keep_row = key_keep[row]
        key_total = jnp.zeros((count, 2, HEAD_DIM), jnp.float32)
        value_total = jnp.zeros((count, 2, HEAD_DIM), jnp.float32)
        query_parts = []
        for part in range(blocks):
            lower = part * BLOCK
            query_block = query_rows[lower : lower + BLOCK]
            back_block = back_rows[lower : lower + BLOCK]
            allowed = pair_mask(query_segs[lower : lower + BLOCK], key_segs, keep_row)
            scores = pair_scores(query_block, key_rows, allowed)
            probs = jnp.exp(scores - totals[:, lower : lower + BLOCK, None])
            value_total = value_total + jnp.einsum(
                "hqk,qhd->khd",
                probs.astype(jnp.bfloat16),
                back_block,
                preferred_element_type=jnp.float32,
            )
            spread_back = jnp.einsum(
                "qhd,khd->hqk", back_block, value_rows, preferred_element_type=jnp.float32
            )
            score_back = (
                probs * (spread_back - jnp.sum(probs * spread_back, -1, keepdims=True))
            ).astype(jnp.bfloat16)
            query_part = (
                jnp.einsum("hqk,khd->qhd", score_back, key_rows, preferred_element_type=jnp.float32)
                * 0.125
            )
            query_parts.append(query_part.reshape(BLOCK, 2 * HEAD_DIM))
            key_total = (
                key_total
                + jnp.einsum(
                    "hqk,qhd->khd", score_back, query_block, preferred_element_type=jnp.float32
                )
                * 0.125
            )
        return (
            jnp.concatenate(query_parts, 0),
            key_total.reshape(count, 2 * HEAD_DIM),
            value_total.reshape(count, 2 * HEAD_DIM),
        )

    query_back, key_back, value_back = lax.map(one_pair, jnp.arange(rows * pairs, dtype=jnp.int32))
    return (
        merge_heads(query_back, rows, length, width),
        merge_heads(key_back, rows, count, width),
        merge_heads(value_back, rows, count, width),
    )


def shards(
    target,
    source,
    target_segment,
    source_segment,
    source_keep,
    self_query,
    self_key,
    self_value,
    self_output,
    cross_query,
    cross_key,
    cross_value,
    cross_output,
    expand_weight,
    shrink_weight,
    norm_affine,
    cotangent,
):
    rows, length, width = target.shape
    src_length = source.shape[1]
    tokens = rows * length
    coords = jnp.stack([lax.axis_index(name) for name in "abci"]).astype(jnp.int32)
    rest = lax.axis_size("r")

    def whole_rows(shard):
        return lax.all_gather(shard, "r", axis=1, tiled=True) if rest > 1 else shard

    shard_one = whole_rows(jnp.stack([self_query, self_key, self_value]))
    shard_two = whole_rows(jnp.stack([self_output, cross_query, cross_key, cross_value, cross_output]))
    shard_three = whole_rows(expand_weight[None])
    shard_four = whole_rows(shrink_weight[None])
    w_sq, w_sk, w_sv = assemble(coords, fetch_line_first(shard_one), True)
    w_so, w_cq, w_ck, w_cv, w_co = assemble(coords, fetch_line_first(shard_two), True)
    expand = assemble(coords, fetch_plane_first(shard_three), False)[0]
    shrink = assemble(coords, fetch_line_first(shard_four), True)[0]
    wide = norm_affine.shape[1]
    column = (((coords[0] * 2 + coords[1]) * 2 + coords[2]) * rest + lax.axis_index("r")) * wide
    affine_low = lax.dynamic_update_slice(
        jnp.zeros((6, width), jnp.float32), norm_affine.astype(jnp.float32), (coords[3] * 3, column)
    )
    if rest > 1:
        affine_low = lax.psum(affine_low, "r")
    affine_low = sum_all(affine_low)
    affine = affine_low.astype(jnp.float32)
    all_keep = jnp.ones_like(target_segment)
    stream = target.reshape(tokens, width).astype(jnp.float32)
    normed_one, norm_one_pull = jax.vjp(layer_norm, stream, affine[0], affine[1])
    normed_one = normed_one.astype(jnp.bfloat16)
    query = forward_dot(normed_one, w_sq).astype(jnp.bfloat16).reshape(rows, length, width)
    keys = forward_dot(normed_one, w_sk).astype(jnp.bfloat16).reshape(rows, length, width)
    values = forward_dot(normed_one, w_sv).astype(jnp.bfloat16).reshape(rows, length, width)
    self_mixed, self_total = attend(query, keys, values, target_segment, target_segment, all_keep)
    self_mixed = self_mixed.reshape(tokens, width).astype(jnp.bfloat16)
    first_sum = stream + forward_dot(self_mixed, w_so)
    normed_two, norm_two_pull = jax.vjp(layer_norm, first_sum, affine[2], affine[3])
    normed_two = normed_two.astype(jnp.bfloat16)
    encoded = source.reshape(rows * src_length, width)
    cross_q = forward_dot(normed_two, w_cq).astype(jnp.bfloat16).reshape(rows, length, width)
    cross_k = forward_dot(encoded, w_ck).astype(jnp.bfloat16).reshape(rows, src_length, width)
    cross_v = forward_dot(encoded, w_cv).astype(jnp.bfloat16).reshape(rows, src_length, width)
    cross_mixed, cross_total = attend(
        cross_q, cross_k, cross_v, target_segment, source_segment, source_keep
    )
    cross_mixed = cross_mixed.reshape(tokens, width).astype(jnp.bfloat16)
    second_sum = first_sum + forward_dot(cross_mixed, w_co)
    normed_three, norm_three_pull = jax.vjp(layer_norm, second_sum, affine[4], affine[5])
    normed_three = normed_three.astype(jnp.bfloat16)
    hidden = forward_dot(normed_three, expand)
    active, gelu_pull = jax.vjp(jax.nn.gelu, hidden)
    active = active.astype(jnp.bfloat16)
    result = (second_sum + forward_dot(active, shrink)).astype(jnp.bfloat16)
    b_sq, b_sk, b_sv, b_so, b_cq, b_ck, b_cv, b_co = w_sq, w_sk, w_sv, w_so, w_cq, w_ck, w_cv, w_co
    b_expand, b_shrink = expand, shrink
    out_back = cotangent.reshape(tokens, width)
    shrink_grad = weight_dot(active, out_back)
    active_back = input_dot(out_back, b_shrink)
    hidden_back = gelu_pull(active_back)[0].astype(jnp.bfloat16)
    expand_grad = weight_dot(normed_three, hidden_back)
    normed_three_back = input_dot(hidden_back, b_expand)
    second_ln, gain_three, bias_three = norm_three_pull(normed_three_back)
    second_back = out_back.astype(jnp.float32) + second_ln
    second_low = second_back.astype(jnp.bfloat16)
    cross_out_grad = weight_dot(cross_mixed, second_low)
    cross_mixed_back = input_dot(second_low, b_co).astype(jnp.bfloat16).reshape(rows, length, width)
    cq_back, ck_back, cv_back = attend_back(
        cross_q,
        cross_k,
        cross_v,
        cross_mixed_back,
        cross_total,
        target_segment,
        source_segment,
        source_keep,
    )
    cq_back = cq_back.reshape(tokens, width).astype(jnp.bfloat16)
    ck_back = ck_back.reshape(rows * src_length, width).astype(jnp.bfloat16)
    cv_back = cv_back.reshape(rows * src_length, width).astype(jnp.bfloat16)
    cross_query_grad = weight_dot(normed_two, cq_back)
    cross_key_grad = weight_dot(encoded, ck_back)
    cross_value_grad = weight_dot(encoded, cv_back)
    source_back = input_dot(ck_back, b_ck) + input_dot(cv_back, b_cv)
    normed_two_back = input_dot(cq_back, b_cq)
    first_ln, gain_two, bias_two = norm_two_pull(normed_two_back)
    first_back = second_back + first_ln
    first_low = first_back.astype(jnp.bfloat16)
    self_out_grad = weight_dot(self_mixed, first_low)
    self_mixed_back = input_dot(first_low, b_so).astype(jnp.bfloat16).reshape(rows, length, width)
    query_back, key_back, value_back = attend_back(
        query, keys, values, self_mixed_back, self_total, target_segment, target_segment, all_keep
    )
    query_back = query_back.reshape(tokens, width).astype(jnp.bfloat16)
    key_back = key_back.reshape(tokens, width).astype(jnp.bfloat16)
    value_back = value_back.reshape(tokens, width).astype(jnp.bfloat16)
    self_query_grad = weight_dot(normed_one, query_back)
    self_key_grad = weight_dot(normed_one, key_back)
    self_value_grad = weight_dot(normed_one, value_back)
    normed_one_back = (
        input_dot(query_back, b_sq) + input_dot(key_back, b_sk) + input_dot(value_back, b_sv)
    )
    stream_ln, gain_one, bias_one = norm_one_pull(normed_one_back)
    stream_back = first_back + stream_ln
    affine_grad = jnp.stack([gain_one, bias_one, gain_two, bias_two, gain_three, bias_three], 0)
    g_shrink = reduce_group(shrink_grad[None], coords, rest, False)[0]
    g_expand = reduce_group(expand_grad[None], coords, rest)[0]
    g_two = reduce_group(
        jnp.stack([self_out_grad, cross_query_grad, cross_key_grad, cross_value_grad, cross_out_grad]), coords, rest
    )
    g_one = reduce_group(jnp.stack([self_query_grad, self_key_grad, self_value_grad]), coords, rest)
    if rest > 1:
        affine_grad = lax.psum(affine_grad, "r")
    g_affine = lax.dynamic_slice(sum_all(affine_grad), (coords[3] * 3, column), (3, wide))
    reduced = (*g_one, *g_two, g_expand, g_shrink, g_affine)
    return (
        result.reshape(rows, length, width),
        stream_back.reshape(rows, length, width),
        source_back.reshape(rows, src_length, width),
        reduced[0],
        reduced[1],
        reduced[2],
        reduced[3],
        reduced[4],
        reduced[5],
        reduced[6],
        reduced[7],
        reduced[8],
        reduced[9],
        reduced[10],
    )


def solution(mesh):
    dp, inner = mesh.shape["dp"], mesh.shape["inner"]
    fine = Mesh(mesh.devices.reshape(4, 2, 2, dp // 16, inner), ("a", "b", "c", "r", "i"))
    split = ("a", "b", "c", "r")
    in_specs = (
        P((*split, "i"), None, None),
        P((*split, "i"), None, None),
        P((*split, "i"), None),
        P((*split, "i"), None),
        P((*split, "i"), None),
        P(split, "i"),
        P(split, "i"),
        P(split, "i"),
        P(split, "i"),
        P(split, "i"),
        P(split, "i"),
        P(split, "i"),
        P(split, "i"),
        P(split, "i"),
        P(split, "i"),
        P("i", split),
        P((*split, "i"), None, None),
    )
    out_specs = (
        P((*split, "i"), None, None),
        P((*split, "i"), None, None),
        P((*split, "i"), None, None),
        P(split, "i"),
        P(split, "i"),
        P(split, "i"),
        P(split, "i"),
        P(split, "i"),
        P(split, "i"),
        P(split, "i"),
        P(split, "i"),
        P(split, "i"),
        P(split, "i"),
        P("i", split),
    )
    return jax.shard_map(shards, mesh=fine, in_specs=in_specs, out_specs=out_specs, check_vma=False)
```

```python
import functools
import types

import jax
import jax.numpy as jnp
from jax import lax
from jax.experimental import pallas as pl
from jax.experimental.pallas import tpu as pltpu
from jax.sharding import Mesh
from jax.sharding import PartitionSpec as P

EPS = 1e-05
NEG = -1e30
SCALE = 0.125 * 1.4426950408889634
TOKENS = 256
LINE = 4
SELF_BLOCK = 256
SELF_SIZES = (384, 512, 768, 1024)
CROSS_BLOCK = 256
CROSS_SIZES = (128, 256, 384)
MIB = 1024 * 1024
BF16 = jnp.bfloat16
SPACE = pltpu.HBM
LARGE = 64
SMALL = 64
F32 = jnp.float32


def dot(left, right):
    return jnp.dot(left, right, preferred_element_type=F32)


def dot_nt(left, right):
    return lax.dot_general(left, right, (((1,), (1,)), ((), ())), preferred_element_type=F32)


def tile(index, size):
    return pl.ds(pl.multiple_of(index * size, size), size)


class Named:
    def __init__(self, act):
        self._act = act

    def __getattr__(self, name):
        return functools.partial(self._act, name)


class Rows:
    def __init__(self, of):
        self.of = of


class Part:
    def __init__(self, array, shape, choose):
        self.array, self.shape, self.dtype, self.choose = array, shape, array.dtype, choose


class Stage:
    def __init__(self):
        self.scalars, self.own, self.ins, self.outs, self.raw = None, {}, {}, {}, []
        self.waited, self.sent = set(), {}
        self.at, self.send = Named(self._at), Named(self._send)

    def begin(self):
        for _, copies in self.ins.values():
            for copy in copies:
                copy.start()

    def _at(self, name, index):
        buffer, copies = self.ins[name]
        if (name, index) not in self.waited:
            self.waited.add((name, index))
            copies[index].wait()
        return buffer

    def __getitem__(self, name):
        if name in self.own:
            return self.own[name]
        if name in self.outs:
            return self.outs[name][0]
        for index in range(len(self.ins[name][1])):
            self._at(name, index)
        return self.ins[name][0]

    def __getattr__(self, name):
        return self[name]

    def _send(self, name, index=None):
        for place, copy in enumerate(self.outs[name][1]):
            if index in (None, place) and (name, place) not in self.sent:
                self.sent[name, place] = copy
                copy.start()

    def finish(self):
        for name in self.ins:
            self[name]
        for name in self.outs:
            self._send(name)
        for copy in self.sent.values():
            copy.wait()


def staged(name, body, scalars, ins, outs, scratch, raw=None, raw_sems=0, weight=0, limit=LARGE):
    raw = raw or []
    by_rows = [label for group in (ins, outs) for label, value in group.items() if isinstance(value, Rows)]
    ins = {label: value.of if isinstance(value, Rows) else value for label, value in ins.items()}
    outs = {label: value.of if isinstance(value, Rows) else value for label, value in outs.items()}

    def copies_of(label, source, target, sems):
        if label not in by_rows:
            return [pltpu.make_async_copy(source, target, sems.pop())]
        spans = [pl.ds(first, TOKENS) for first in range(0, target.shape[0], TOKENS)]
        return [pltpu.make_async_copy(source.at[span], target.at[span], sems.pop()) for span in spans]

    def count_of(label, shape):
        return shape[0] // TOKENS if label in by_rows else 1

    total = sum(count_of(n, v.shape) for n, v in ins.items()) + sum(count_of(n, v[0]) for n, v in outs.items())
    total += raw_sems

    def kernel(*refs):
        refs = list(refs)

        def take(count):
            head = refs[:count]
            del refs[:count]
            return head

        stage = Stage()
        stage.scalars = types.SimpleNamespace(**dict(zip(scalars, take(len(scalars)))))
        in_refs, stage.raw, out_refs = take(len(ins)), take(len(raw)), take(len(outs))
        in_vmem, out_vmem = take(len(ins)), take(len(outs))
        stage.own = dict(zip(scratch, take(len(scratch))))
        stage.own.update(vars(stage.scalars))
        sem_array = take(1)[0]
        sems = [sem_array.at[place] for place in range(total)]
        for label, source, target in zip(ins, in_refs, in_vmem):
            if isinstance(ins[label], Part):
                source = ins[label].choose(source, stage.scalars)
            stage.ins[label] = (target, copies_of(label, source, target, sems))
        for label, source, target in zip(outs, out_vmem, out_refs):
            stage.outs[label] = (source, copies_of(label, source, target, sems))
        stage.raw_sems = sems
        stage.begin()
        body(stage)
        stage.finish()

    results = pl.pallas_call(
        kernel,
        out_shape=[jax.ShapeDtypeStruct(*shape) for shape in outs.values()],
        in_specs=[pl.BlockSpec(memory_space=pltpu.SMEM)] * len(scalars)
        + [pl.BlockSpec(memory_space=SPACE)] * (len(ins) + len(raw)),
        out_specs=[pl.BlockSpec(memory_space=SPACE)] * len(outs),
        scratch_shapes=[pltpu.VMEM(array.shape, array.dtype) for array in ins.values()]
        + [pltpu.VMEM(*shape) for shape in outs.values()]
        + [pltpu.VMEM(*shape) for shape in scratch.values()]
        + [pltpu.SemaphoreType.DMA((total,))],
        compiler_params=pltpu.CompilerParams(vmem_limit_bytes=limit * MIB),
        cost_estimate=pl.CostEstimate(
            flops=1000 + weight * 10**9, bytes_accessed=1000 + weight * 3 * 10**6, transcendentals=0
        ),
        name=name,
    )(
        *scalars.values(),
        *[array.array if isinstance(array, Part) else array for array in ins.values()],
        *raw,
    )
    return types.SimpleNamespace(**{str(label): result for label, result in zip(outs, results)})


def place_of(coords, line_first, part, entry):
    core, first = part // 4, part % 4
    back, plane = (entry, first) if line_first else (first, entry)
    line = (coords[0] - back) & 3
    outer = coords[1] ^ (plane >> 1)
    inner = coords[3] ^ (plane & 1)
    dp = (line * 2 + outer) * 2 + (coords[2] ^ core)
    return dp, inner


def piece_copies(stage, pieces, sems, spot, line_first=True):
    copies = []
    for part in range(8):
        for entry in range(4):
            dp, inner = place_of(stage.coords, line_first, part, entry)
            for which, target in spot(dp, inner):
                copies.append(pltpu.make_async_copy(pieces[part].at[entry, which], target, sems[len(copies)]))
    for copy in copies:
        copy.start()
    return copies


def standard(value):
    centre = value - jnp.mean(value, -1, keepdims=True)
    rate = lax.rsqrt(jnp.mean(centre * centre, -1, keepdims=True) + EPS)
    return centre * rate, rate


def standard_back(value, gain, upstream):
    z, rate = standard(value)
    scaled = upstream * gain
    back = rate * (scaled - jnp.mean(scaled, -1, keepdims=True) - z * jnp.mean(scaled * z, -1, keepdims=True))
    return back, upstream * z


def blocks_of_tokens(length, run):
    for index in range(length // TOKENS):
        run(slice(index * TOKENS, (index + 1) * TOKENS), index)


def windowed(sizes, kind, run):
    for place, size in enumerate(sizes):
        pl.when(kind == place)(functools.partial(run, size))


def set_bias(bias, query_seg, key_seg, rows, keys, size):
    bias[:, :size] = jnp.where(query_seg[rows, :] == key_seg[:, keys], 0.0, NEG)


def attend(query, keys, values, query_seg, key_seg, window, mixed, total, bias, sizes, block):
    length, width = query.shape
    lane = lax.broadcasted_iota(jnp.int32, (block, 128), 1)
    low = lane < 64

    def one_block(index, carry):
        rows = tile(index, block)
        start = window[0, index]

        def run(size):
            span = pl.ds(pl.multiple_of(start, 128), size)
            set_bias(bias, query_seg, key_seg, rows, span, size)

            def one_pair(pair, stats):
                lanes = tile(pair, 128)
                q, k, v = query[rows, lanes], keys[span, lanes], values[span, lanes]
                zero = jnp.zeros_like(q)
                parts = []
                for half in range(2):
                    picked = jnp.where(low, q, zero) if half == 0 else jnp.where(low, zero, q)
                    scores = dot_nt(picked, k) * SCALE + bias[:, :size]
                    top = jnp.max(scores, -1, keepdims=True)
                    expo = jnp.exp2(scores - top)
                    sums = jnp.sum(expo, -1, keepdims=True)
                    parts.append(dot(expo.astype(BF16), v) * (1.0 / sums))
                    stats = jnp.where(lane == pair * 2 + half, top + jnp.log2(sums), stats)
                mixed[rows, lanes] = jnp.where(low, parts[0], parts[1]).astype(BF16)
                return stats

            total[rows, :] = lax.fori_loop(0, width // 128, one_pair, jnp.zeros((block, 128), F32), unroll=2)

        windowed(sizes, window[1, index], run)
        return carry

    lax.fori_loop(0, length // block, one_block, 0)


def attend_back(query, keys, values, back, mixed, total, query_seg, key_seg, window, query_back, key_acc, value_acc, bias, sizes, block):
    length, width = query.shape
    lane = lax.broadcasted_iota(jnp.int32, (block, 128), 1)
    low = lane < 64
    key_acc[...] = jnp.zeros(key_acc.shape, F32)
    value_acc[...] = jnp.zeros(value_acc.shape, F32)

    def one_block(index, carry):
        rows = tile(index, block)
        start = window[0, index]

        def run(size):
            span = pl.ds(pl.multiple_of(start, 128), size)
            set_bias(bias, query_seg, key_seg, rows, span, size)
            stats = total[rows, :]

            def one_pair(pair, carried):
                lanes = tile(pair, 128)
                q, k, v = query[rows, lanes], keys[span, lanes], values[span, lanes]
                up = back[rows, lanes]
                product = up.astype(F32) * mixed[rows, lanes].astype(F32)
                q_t, up_t = q.T, up.T
                zero = jnp.zeros_like(q)
                parts = []
                for half in range(2):
                    mine = low if half == 0 else jnp.logical_not(low)
                    scores = dot_nt(jnp.where(mine, q, zero), k) * SCALE + bias[:, :size]
                    level = jnp.sum(jnp.where(lane == pair * 2 + half, stats, 0.0), -1, keepdims=True)
                    probs = jnp.exp2(scores - level)
                    spread = dot_nt(jnp.where(mine, up, zero), v)
                    delta = jnp.sum(jnp.where(mine, product, 0.0), -1, keepdims=True)
                    scores_back = (probs * (spread - delta)).astype(BF16)
                    parts.append(dot(scores_back, k))
                    own = slice(half * 64, half * 64 + 64)
                    spot = pl.ds(pl.multiple_of(pair * 128 + half * 64, 64), 64)
                    value_acc[spot, span] += dot(up_t[own], probs.astype(BF16))
                    key_acc[spot, span] += dot(q_t[own], scores_back)
                query_back[rows, lanes] = (jnp.where(low, parts[0], parts[1]) * 0.125).astype(BF16)
                return carried

            lax.fori_loop(0, width // 128, one_pair, 0)

        windowed(sizes, window[1, index], run)
        return carry

    lax.fori_loop(0, length // block, one_block, 0)


def put_square(stage, grad, column, base):
    core = stage.coords[2]
    rows = grad.shape[0] // 16
    blocks = grad.astype(BF16).reshape(LINE, 2, 2, rows, grad.shape[1])
    for result, wanted in ((stage.keep, 0), (stage.send_, 1)):
        picked = jnp.where(core == wanted, blocks[:, :, 0], blocks[:, :, 1])
        for outer in range(2):
            for chunk in range(2):
                result[outer * 2 + column, :, base + chunk * rows : base + (chunk + 1) * rows, :] = picked[
                    :, outer, :, chunk * 128 : (chunk + 1) * 128
                ]


def self_forward_body(stage):
    affine, loose, weight = stage.affine, stage.loose, stage.weight
    copies = piece_copies(
        stage, stage.raw, stage.raw_sems, lambda dp, inner: [(slice(0, 7), loose.at[:, dp, :, tile(inner, 256)])]
    )
    for copy in copies:
        copy.wait()
    for w in range(3):
        for dp in range(16):
            for half in range(2):
                weight[w, dp * 32 + half * 16 : dp * 32 + half * 16 + 16, :] = loose[2 * w + half, dp]
    flat = jnp.sum(loose[6].astype(F32), 0)
    flat = flat[:, :256] + flat[:, 256:]
    affine[:, :256] = flat[:8]
    affine[:, 256:] = flat[8:]
    stage.send.weight()
    stage.send.affine()
    normed_t = stage.normed_t
    length = normed_t.shape[1]

    def project(rows, index):
        z, _ = standard(stage.at.target(index)[rows, :].astype(F32))
        n = (z * affine[0:1, :] + affine[1:2, :]).astype(BF16)
        normed_t[:, rows] = n.T
        for place, result in enumerate((stage.query, stage.key, stage.value)):
            result[rows, :] = dot(n, weight[place]).astype(BF16)
        stage.send.query(index)
        stage.send.key(index)
        stage.send.value(index)

    blocks_of_tokens(length, project)
    stage.send.normed_t()
    attend(
        stage.query, stage.key, stage.value, stage.seg_col, stage.seg_row, stage.window,
        stage.mixed, stage.total, stage.bias, SELF_SIZES, SELF_BLOCK,
    )
    stage.send.mixed()
    stage.send.total()

    def turn(rows, index):
        stage.mixed_t[:, rows] = stage.mixed[rows, :].T

    blocks_of_tokens(length, turn)


def self_forward(coords, window, target, seg_col, seg_row, pieces):
    length, width = target.shape
    low, turned = ((length, width), BF16), ((width, length), BF16)
    return staged(
        "self_forward", self_forward_body, dict(coords=coords, window=window),
        dict(target=Rows(target), seg_col=seg_col, seg_row=seg_row),
        dict(
            weight=((3, width, width), BF16), affine=((8, width), F32), normed_t=turned, query=Rows(low),
            key=Rows(low), value=Rows(low), mixed=low, mixed_t=turned, total=((length, 128), F32),
        ),
        dict(loose=((7, 16, 16, width), BF16), bias=((SELF_BLOCK, SELF_SIZES[-1]), F32)),
        raw=pieces, raw_sems=32,
        weight=20,
    )


def cross_forward_body(stage):
    weight = stage.weight
    copies = piece_copies(
        stage,
        stage.raw,
        stage.raw_sems,
        lambda dp, inner: [(slice(0, 5), weight.at[:, tile(dp, 32), tile(inner, 256)])],
    )
    for copy in copies:
        copy.wait()
    stage.send.weight()
    source, affine = stage.source, stage.affine
    first = stage.first
    length = first.shape[0]
    stage.key[...] = dot(source[...], weight[2]).astype(BF16)
    stage.value[...] = dot(source[...], weight[3]).astype(BF16)
    stage.send.key()
    stage.send.value()

    def project(rows, index):
        v = stage.at.target(index)[rows, :].astype(F32) + dot(stage.at.mixed1(index)[rows, :], weight[0])
        first[rows, :] = v
        stage.send.first(index)
        z, _ = standard(v)
        n = (z * affine[2:3, :] + affine[3:4, :]).astype(BF16)
        stage.normed2_t[:, rows] = n.T
        stage.query[rows, :] = dot(n, weight[1]).astype(BF16)
        stage.send.query(index)

    blocks_of_tokens(length, project)
    stage.send.normed2_t()
    attend(
        stage.query, stage.key, stage.value, stage.seg_col, stage.seg_row, stage.window,
        stage.mixed, stage.total, stage.bias, CROSS_SIZES, CROSS_BLOCK,
    )
    stage.send.mixed()
    stage.send.total()

    def finish(rows, index):
        m = stage.mixed[rows, :]
        stage.mixed_t[:, rows] = m.T
        v = first[rows, :] + dot(m, weight[4])
        stage.second[rows, :] = v
        z, _ = standard(v)
        n = (z * affine[4:5, :] + affine[5:6, :]).astype(BF16)
        stage.normed[rows, :] = n
        stage.normed_t[:, rows] = n.T
        stage.send.second(index)
        stage.send.normed(index)

    blocks_of_tokens(length, finish)


def cross_forward(coords, window, target, mixed1, affine, source, seg_col, seg_row, pieces):
    length, width = target.shape
    count = source.shape[0]
    low, turned, full = ((length, width), BF16), ((width, length), BF16), ((length, width), F32)
    return staged(
        "cross_forward", cross_forward_body, dict(coords=coords, window=window),
        dict(
            mixed1=Rows(mixed1), target=Rows(target), affine=affine, source=source, seg_col=seg_col, seg_row=seg_row
        ),
        dict(
            weight=((5, width, width), BF16), key=((count, width), BF16), value=((count, width), BF16),
            first=Rows(full), normed2_t=turned, query=Rows(low), mixed=low, mixed_t=turned,
            total=((length, 128), F32), second=Rows(full), normed=Rows(low), normed_t=turned,
        ),
        dict(bias=((CROSS_BLOCK, CROSS_SIZES[-1]), F32)),
        raw=pieces, raw_sems=32,
        weight=20,
    )


FF_BLOCK = 256


def feed_forward_body(stage):
    expand, shrink = stage.expand, stage.shrink
    copies = piece_copies(
        stage,
        stage.raw,
        stage.raw_sems,
        lambda dp, inner: [
            (slice(0, 4), expand.at[tile(inner, 4), tile(dp, 32), :]),
            (slice(4, 8), shrink.at[inner, tile(dp, 4)]),
        ],
    )
    normed, normed_t, back, back_t = stage.normed, stage.normed_t, stage.back, stage.back_t
    second, normed_back = stage.second, stage.normed_back
    total, active, hidden_back = stage.total, stage.active, stage.hidden_back
    core = stage.coords[2]
    length, width = normed.shape
    for copy in copies:
        copy.wait()
    total[...] = second[...]
    normed_back[...] = jnp.zeros(normed_back.shape, F32)

    def one_part(part, carry):
        wide = expand[part]
        halves = [shrink[side, tile(part, 8)].reshape(FF_BLOCK, width // 2) for side in range(2)]
        narrow = jnp.concatenate(halves, 1)
        for index in range(length // TOKENS):
            rows = slice(index * TOKENS, (index + 1) * TOKENS)
            v = dot(normed[rows, :], wide)
            up = dot_nt(back[rows, :], narrow)
            square = v * v
            half = 0.5 + 0.5 * jnp.tanh(v * (0.7978845608028654 + 0.035677408136300125 * square))
            value = v * half
            slope = half + value * (1.0 - half) * (1.5957691216057308 + 0.21406444881780075 * square)
            low, low_back = value.astype(BF16), (up * slope).astype(BF16)
            active[rows, :] = low
            hidden_back[rows, :] = low_back
            total[rows, :] += dot(low, narrow)
            normed_back[rows, :] += dot_nt(low_back, wide)
        grad = dot(normed_t[...], hidden_back[...]).astype(BF16)
        blocks = grad.reshape(LINE, 2, 2, width // 16, FF_BLOCK)
        inner, chunk = part // 4, part % 4 * 2
        for result, wanted in ((stage.keep, 0), (stage.send_, 1)):
            picked = jnp.where(core == wanted, blocks[:, :, 0], blocks[:, :, 1])
            for outer in range(2):
                for side in range(2):
                    result[outer * 2 + inner, :, tile(chunk + side, width // 16), :] = picked[
                        :, outer, :, side * 128 : (side + 1) * 128
                    ]
        grad = dot(back_t[...], active[...]).astype(BF16)
        line, outer = part // 2, part % 2
        for result, wanted in ((stage.keep, 0), (stage.send_, 1)):
            picked = jnp.where(core == wanted, grad[:, :128], grad[:, 128:])
            for side in range(2):
                result[outer * 2 + side, line, width // 2 :, :] = picked[side * width // 2 : (side + 1) * width // 2]
        return carry

    lax.fori_loop(0, expand.shape[0], one_part, 0)
    stage.send.send_()
    stage.send.keep()
    stage.send.normed_back()

    def finish(rows, index):
        stage.output[rows, :] = total[rows, :].astype(BF16)

    blocks_of_tokens(length, finish)


def feed_forward(coords, normed, normed_t, second, back, back_t, pieces):
    length, width = normed.shape
    hidden = 4 * width
    low = ((length, width), BF16)
    part = ((4, LINE, width, 128), BF16)
    return staged(
        "feed_forward", feed_forward_body, dict(coords=coords),
        dict(normed=normed, normed_t=normed_t, second=second, back=back, back_t=back_t),
        dict(keep=part, send_=part, normed_back=((length, width), F32), output=low),
        dict(
            expand=((hidden // FF_BLOCK, width, FF_BLOCK), BF16), shrink=((2, hidden // 32, 32, width // 2), BF16),
            total=((length, width), F32), active=((length, FF_BLOCK), BF16), hidden_back=((length, FF_BLOCK), BF16),
        ),
        raw=pieces, raw_sems=64,
        weight=20,
    )


def add_affine(stage, row, gain, bias):
    stage.affine_back[row : row + 1, :] += jnp.sum(gain, 0, keepdims=True)
    stage.affine_back[row + 1 : row + 2, :] += jnp.sum(bias, 0, keepdims=True)


def norm_back_body(stage):
    affine = stage.affine
    stage.affine_back[...] = jnp.zeros(stage.affine_back.shape, F32)

    def run(rows, index):
        upstream = stage.at.normed_back(index)[rows, :]
        grad, gain = standard_back(stage.at.second(index)[rows, :], affine[4:5, :], upstream)
        add_affine(stage, 4, gain, upstream)
        grad = grad + stage.at.back(index)[rows, :].astype(F32)
        stage.second_back[rows, :] = grad
        low = grad.astype(BF16)
        stage.out_back[rows, :] = low
        stage.mixed_back[rows, :] = dot_nt(low, stage.weight[...]).astype(BF16)
        stage.send.second_back(index)
        stage.send.out_back(index)
        stage.send.mixed_back(index)

    blocks_of_tokens(stage.second_back.shape[0], run)


def norm_back(affine, weight, second, normed_back, back):
    length, width = second.shape
    low, full = ((length, width), BF16), ((length, width), F32)
    return staged(
        "norm_back", norm_back_body, {},
        dict(
            affine=affine, normed_back=Rows(normed_back), second=Rows(second), back=Rows(back),
            weight=Part(weight, (width, width), lambda ref, scalars: ref.at[4]),
        ),
        dict(affine_back=((8, width), F32), mixed_back=Rows(low), second_back=Rows(full), out_back=Rows(low)),
        {},
        weight=3,
    )


def square_grads(stage, base, left_t, right, turned):
    for column in range(2):
        cols = slice(column * 256, (column + 1) * 256)
        grad = dot_nt(left_t[...], right[cols, :]) if turned else dot(left_t[...], right[:, cols])
        put_square(stage, grad, column, base)


def cross_back_body(stage):
    query, affine = stage.query, stage.affine
    key_acc, value_acc, query_back = stage.key_acc, stage.value_acc, stage.query_back
    attend_back(
        query, stage.key, stage.value, stage.mixed_back, stage.mixed, stage.total, stage.seg_col,
        stage.seg_row, stage.window, query_back, key_acc, value_acc, stage.bias, CROSS_SIZES, CROSS_BLOCK,
    )
    weight, key_back, value_back = stage.weight, stage.key_back, stage.value_back
    key_back[...] = (key_acc[...] * 0.125).astype(BF16)
    value_back[...] = value_acc[...].astype(BF16)
    turned = dot(weight[2], key_back[...]) + dot(weight[3], value_back[...])
    stage.source_back[...] = turned.T[: stage.source_back.shape[0]]
    stage.send.source_back()
    stage.affine_back[...] = stage.affine_before[...]
    first_low = stage.first_low

    def run(rows, index):
        upstream = dot_nt(query_back[rows, :], weight[1])
        grad, gain = standard_back(stage.first[rows, :], affine[2:3, :], upstream)
        add_affine(stage, 2, gain, upstream)
        grad = grad + stage.second_back[rows, :]
        stage.first_back[rows, :] = grad
        low = grad.astype(BF16)
        first_low[rows, :] = low
        stage.mixed1_back[rows, :] = dot_nt(low, weight[0]).astype(BF16)

    blocks_of_tokens(query.shape[0], run)
    stage.send.first_back()
    stage.send.mixed1_back()
    stage.send.affine_back()
    rows_of = weight.shape[1] // 16 * 2
    square_grads(stage, 0, stage.mixed1_t, first_low, False)
    square_grads(stage, rows_of, stage.normed_t, query_back, False)
    square_grads(stage, 2 * rows_of, stage.source_t, key_back, True)
    square_grads(stage, 3 * rows_of, stage.source_t, value_back, True)
    square_grads(stage, 4 * rows_of, stage.mixed_t, stage.out_back, False)


def cross_back(coords, window, ins, source_length):
    ins_ = types.SimpleNamespace(**ins)
    length, width = ins_.query.shape
    count = ins_.key.shape[0]
    low, full = ((length, width), BF16), ((length, width), F32)
    turned = ((width, count), BF16)
    part = ((4, LINE, 5 * width // 8, 128), BF16)
    return staged(
        "cross_back", cross_back_body, dict(coords=coords, window=window), ins,
        dict(
            keep=part, send_=part, first_back=full, mixed1_back=low, affine_back=((8, width), F32),
            source_back=((source_length, width), F32),
        ),
        dict(
            key_acc=((width, count), F32), value_acc=((width, count), F32), query_back=low, first_low=low,
            key_back=turned, value_back=turned, bias=((CROSS_BLOCK, CROSS_SIZES[-1]), F32),
        ),
        weight=20,
    )


AFFINE_ROWS = 16


def pack_first_body(wide, stage):
    for place in range(3):
        for half in range(2):
            stage.packed[2 * place + half] = stage[place][half * 16 : half * 16 + 16, :]
    coords = stage.coords
    own = stage.norms[...].astype(F32)
    width = 2 * stage.packed.shape[2]
    row_at, from_row = (lax.broadcasted_iota(jnp.int32, (8, own.shape[0]), axis) for axis in range(2))
    from_lane, lane_at = (lax.broadcasted_iota(jnp.int32, (wide, width), axis) for axis in range(2))
    down = (row_at == coords[3] * 3 + from_row).astype(F32)
    right = (lane_at == coords[4] + from_lane).astype(F32)
    placed = dot(down, dot(own, right)).astype(BF16)
    stage.packed[6] = jnp.concatenate([placed[:, : width // 2], placed[:, width // 2 :]], 0)


def pack_first(coords, weights, norms):
    ins = {**dict(enumerate(weights)), **dict(norms=norms)}
    outs = dict(packed=((7, 16, weights[0].shape[1]), BF16))
    body = functools.partial(pack_first_body, norms.shape[1])
    return staged("pack", body, dict(coords=coords), ins, outs, {}, limit=SMALL).packed


def pack_second_body(stage):
    for place in range(len(stage.ins)):
        stage.packed[place] = stage[place][...]


def pack_second(weights):
    outs = dict(packed=((len(weights), *weights[0].shape), BF16))
    return staged("pack", pack_second_body, {}, dict(enumerate(weights)), outs, {}, limit=SMALL).packed


def pack_third_body(stage):
    for place in range(4):
        stage.packed[place] = stage.expand[:, place * 256 : place * 256 + 256]
        stage.packed[4 + place] = stage.shrink[place * 32 : place * 32 + 32, :]


def pack_third(expand, shrink):
    outs = dict(packed=((8, 32, 256), BF16))
    return staged("pack", pack_third_body, {}, dict(expand=expand, shrink=shrink), outs, {}, limit=SMALL).packed


def self_back_body(stage):
    query = stage.query
    key_acc, value_acc, query_back = stage.key_acc, stage.value_acc, stage.query_back
    attend_back(
        query, stage.key, stage.value, stage.mixed_back, stage.mixed, stage.total, stage.seg_col,
        stage.seg_row, stage.window, query_back, key_acc, value_acc, stage.bias, SELF_SIZES, SELF_BLOCK,
    )
    weight, affine = stage.weight, stage.affine
    key_back, value_back = stage.key_back, stage.value_back
    key_back[...] = (key_acc[...] * 0.125).astype(BF16)
    value_back[...] = value_acc[...].astype(BF16)
    stage.affine_back[...] = stage.affine_before[...]

    def run(rows, index):
        turned = dot(weight[1], key_back[:, rows]) + dot(weight[2], value_back[:, rows])
        upstream = dot_nt(query_back[rows, :], weight[0]) + turned.T
        grad, gain = standard_back(stage.target[rows, :].astype(F32), affine[0:1, :], upstream)
        add_affine(stage, 0, gain, upstream)
        stage.target_back[rows, :] = grad + stage.first_back[rows, :]
        stage.send.target_back(index)

    blocks_of_tokens(query.shape[0], run)
    width = query.shape[1]
    rows_of = width // 16 * 2
    square_grads(stage, 0, stage.normed_t, query_back, False)
    square_grads(stage, rows_of, stage.normed_t, key_back, True)
    square_grads(stage, 2 * rows_of, stage.normed_t, value_back, True)
    norms = stage.affine_back[...]
    norms = jnp.concatenate([norms, jnp.zeros_like(norms)], 0)
    for inner in range(2):
        low = (norms if inner == 0 else jnp.concatenate([norms[3:], norms[:3]], 0)).astype(BF16)
        for line in range(LINE):
            for result in (stage.keep, stage.send_):
                for outer in range(2):
                    result[outer * 2 + inner, line, 3 * rows_of :, :] = low[:, line * 128 : (line + 1) * 128]


def self_back(coords, window, ins):
    ins_ = types.SimpleNamespace(**ins)
    length, width = ins_.query.shape
    low, turned = ((length, width), BF16), ((width, length), BF16)
    part = ((4, LINE, 3 * width // 8 + AFFINE_ROWS, 128), BF16)
    return staged(
        "self_back", self_back_body, dict(coords=coords, window=window), ins,
        dict(send_=part, keep=part, target_back=Rows(((length, width), F32))),
        dict(
            key_acc=((width, length), F32), value_acc=((width, length), F32), query_back=low, key_back=turned,
            value_back=turned, affine_back=((8, width), F32), bias=((SELF_BLOCK, SELF_SIZES[-1]), F32),
        ),
        weight=20,
    )


def sums_body(jobs, stage):
    place = 0
    for index, job in enumerate(jobs):
        total = stage[place, index][...].astype(F32)
        for more in range(1, len(job)):
            total = total + stage[place + more, index][...].astype(F32)
        place += len(job)
        stage.outs[index][0][...] = total.astype(BF16)
        stage._send(index)


def sums(coords, jobs):
    ins = {}
    for index, job in enumerate(jobs):
        for part in job:
            ins[len(ins), index] = part
    outs = {index: (job[0].shape, BF16) for index, job in enumerate(jobs)}
    body = functools.partial(sums_body, jobs)
    return list(vars(staged("sums", body, dict(coords=coords), ins, outs, {}, limit=SMALL)).values())


def plane_part(array, step):
    def choose(ref, scalars):
        coords = scalars.coords
        return ref.at[(coords[1] ^ (step >> 1)) * 2 + (coords[3] ^ (step & 1))]

    return Part(array, array.shape[1:], choose)


def line_part(array, step):
    return Part(array, array.shape[1:], lambda ref, scalars: ref.at[(scalars.coords[0] + step) & 3])


ORDER = (1, 2, 3, 0)


def chip_jobs(keep, away):
    return [[plane_part(keep, step), plane_part(away, step)] for step in ORDER]


def plane_jobs(arrays):
    return [[line_part(array, step) for array in arrays] for step in ORDER]


def last_sums_body(hidden, squares, wide, stage):
    def total_of(first):
        parts = [stage[first + place][...].astype(F32) for place in range(4)]
        return parts[0] + parts[1] + (parts[2] + parts[3])

    results = [value[0] for value in stage.outs.values()]
    if hidden:
        total = total_of(0)
        half = total.shape[0] // 2
        rows = half // 8
        for chunk in range(8):
            results[0][:, chunk * 128 : (chunk + 1) * 128] = total[chunk * rows : (chunk + 1) * rows]
        results[1][...] = total[half:].T
        results = results[2:]
    first = 4 if hidden else 0
    for count in squares:
        total = total_of(first)
        first += 4
        for place in range(count):
            for chunk in range(2):
                row = (2 * place + chunk) * 32
                results[place][:, chunk * 128 : (chunk + 1) * 128] = total[row : row + 32]
        results = results[count:]
        if total.shape[0] > count * 64:
            lane = (stage.coords[1] * 2 + stage.coords[2]) * 32 + stage.coords[5]
            norms = pltpu.roll(total[count * 64 : count * 64 + 8], (128 - lane) & 127, 1)
            results[0][...] = norms[:3, :wide]
            results = results[1:]


def last_sums(coords, hidden, squares, wide):
    arrays = [array for group in ([hidden] if hidden else []) + squares for array in group]
    outs = {}
    if hidden:
        rows = hidden[0].shape[0]
        outs[(0,)] = ((rows // 16, 1024), F32)
        outs[(1,)] = ((128, rows // 2), F32)
    counts = []
    for group in squares:
        counts.append(group[0].shape[0] // 64)
        for _ in range(counts[-1]):
            outs[(len(outs),)] = ((32, 256), F32)
        if group[0].shape[0] % 64:
            outs[(len(outs),)] = ((3, wide), F32)
    body = functools.partial(last_sums_body, bool(hidden), counts, wide)
    result = staged("last_sums", body, dict(coords=coords), dict(enumerate(arrays)), outs, {}, limit=SMALL)
    return list(vars(result).values())


def windows(query_seg, key_seg, sizes, block, count):
    first, last_one = query_seg.reshape(-1, block)[:, 0], query_seg.reshape(-1, block)[:, -1]
    low = jnp.sum((key_seg[None, :] < first[:, None]).astype(jnp.int32), 1) // 128
    high = (jnp.sum((key_seg[None, :] <= last_one[:, None]).astype(jnp.int32), 1) + 127) // 128
    need = (high - low) * 128
    kind = sum(((need > size).astype(jnp.int32) for size in sizes[:-1]), jnp.zeros_like(need))
    size = sum((jnp.where(kind == place, size, 0) for place, size in enumerate(sizes)), jnp.zeros_like(need))
    return jnp.stack([jnp.minimum(low * 128, count - size), kind]).astype(jnp.int32)


SWAP = [(0, 1), (1, 0)]
SHIFTS = [[(i, (i + k) % LINE) for i in range(LINE)] for k in range(LINE)]
CROSS = [[(i, i ^ k) for i in range(4)] for k in range(4)]
PLANE = ("b", "i")


def after(value, *earlier):
    return lax.optimization_barrier((value, earlier))[0]


def join(arrays):
    return jnp.concatenate(arrays, 0).reshape(len(arrays), *arrays[0].shape)


def along_line(array):
    return [array] + [lax.ppermute(array, "a", SHIFTS[k]) for k in (1, 2, 3)]


def along_plane(array):
    return [array] + [lax.ppermute(array, PLANE, CROSS[k]) for k in (1, 2, 3)]


def across_cores(arrays):
    return arrays + [lax.ppermute(array, "c", SWAP) for array in arrays]


def swap_cores(array):
    return lax.ppermute(array, "c", SWAP)


def to_plane(arrays):
    return [lax.ppermute(array, PLANE, CROSS[k]) for array, k in zip(arrays, (1, 2, 3))] + arrays[3:4]


def to_line(arrays):
    return [lax.ppermute(array, "a", SHIFTS[k]) for array, k in zip(arrays, (1, 2, 3))] + arrays[3:4]


def shards(
    target,
    source,
    target_segment,
    source_segment,
    source_keep,
    self_query,
    self_key,
    self_value,
    self_output,
    cross_query,
    cross_key,
    cross_value,
    cross_output,
    expand_weight,
    shrink_weight,
    norm_affine,
    cotangent,
):
    length, width = target.shape[1:]
    src_length = source.shape[1]
    count = CROSS_SIZES[-1]
    rest = lax.axis_size("r")
    wide = norm_affine.shape[1]
    a, b, c, r, i = (lax.axis_index(name) for name in "abcri")
    coords = jnp.stack([a, b, c, i, (((a * 2 + b) * 2 + c) * rest + r) * wide, r * wide]).astype(jnp.int32)

    def whole_rows(shard):
        return lax.all_gather(shard, "r", axis=0, tiled=True) if rest > 1 else shard

    shard_one = pack_first(coords, [whole_rows(w) for w in (self_query, self_key, self_value)], norm_affine)
    if rest > 1:
        norms = lax.psum(shard_one[6].astype(F32), "r").astype(BF16)
        shard_one = jnp.concatenate([shard_one[:6], norms[None]], 0)
    shard_two = pack_second(
        [whole_rows(w) for w in (self_output, cross_query, cross_key, cross_value, cross_output)]
    )
    shard_three = pack_third(whole_rows(expand_weight), whole_rows(shrink_weight))
    x = target[0]
    upstream = cotangent[0]
    padded = jnp.pad(source[0], ((0, count - src_length), (0, 0)))
    seg = target_segment[0]
    line_one = along_line(shard_one)
    held = (seg, source_segment, source_keep, padded, upstream)
    joined_one = join(line_one)
    shard_two, held = after((shard_two, held), joined_one)
    near_one = along_plane(joined_one)
    line_two = along_line(shard_two)
    line_three = along_line(after(shard_three, shard_two))
    pieces_one = across_cores(near_one)
    stage_two = along_plane(after(join(line_two), pieces_one))

    seg, source_segment, source_keep, padded, held_upstream = held
    padded_t, upstream_t = padded.T, held_upstream.T
    seg_col, seg_row = seg[:, None], seg[None, :]
    key_seg = jnp.where(source_keep > 0, source_segment, -1)
    key_row = jnp.pad(key_seg, ((0, 0), (0, count - src_length)), constant_values=-1)
    self_window = windows(seg, seg, SELF_SIZES, SELF_BLOCK, length)
    cross_window = windows(seg, source_segment[0], CROSS_SIZES, CROSS_BLOCK, count)

    ready = after(x, padded, padded_t, upstream_t, key_row, cross_window)
    one = self_forward(coords, self_window, ready, seg_col, seg_row, pieces_one)
    line_three = after(line_three, one.mixed)
    pieces_two = across_cores(after(stage_two, line_three))
    stage_three = along_plane(after(join(line_three), stage_two))
    two = cross_forward(coords, cross_window, x, one.mixed, one.affine, padded, seg_col, key_row, pieces_two)
    pieces_three = across_cores(after(stage_three, two.mixed))
    three = feed_forward(coords, two.normed, two.normed_t, two.second, upstream, upstream_t, pieces_three)
    away_three = swap_cores(three.send_)
    four = norm_back(one.affine, two.weight, two.second, three.normed_back, upstream)
    chip_three = sums(coords, chip_jobs(three.keep, after(away_three, four.mixed_back)))
    plane_three = to_plane(chip_three)
    five = cross_back(
        coords,
        cross_window,
        dict(
            query=two.query, key=two.key, seg_col=seg_col, seg_row=key_row, total=two.total, value=two.value,
            mixed_back=after(four.mixed_back, chip_three), mixed=two.mixed, weight=two.weight, affine=one.affine,
            affine_before=four.affine_back, first=two.first, second_back=four.second_back, mixed1_t=one.mixed_t,
            normed_t=two.normed2_t, source_t=padded_t, mixed_t=two.mixed_t, out_back=four.out_back,
        ),
        src_length,
    )
    away_two = swap_cores(after(five.send_, plane_three))
    middle = sums(coords, chip_jobs(five.keep, away_two) + plane_jobs(plane_three))
    plane_two, line_three = to_plane(middle[:4]), to_line(middle[4:])
    six = self_back(
        coords,
        self_window,
        dict(
            query=one.query, key=one.key, seg_col=seg_col, seg_row=seg_row, total=one.total, value=one.value,
            mixed_back=after(five.mixed1_back, middle), mixed=one.mixed, weight=one.weight, affine=one.affine,
            affine_before=five.affine_back, target=x, first_back=five.first_back, normed_t=one.normed_t,
        ),
    )
    away_one = swap_cores(after(six.send_, plane_two, line_three))
    tail = sums(coords, chip_jobs(six.keep, away_one) + plane_jobs(plane_two))
    plane_one = to_plane(tail[:4])
    line_two = to_line(tail[4:])
    hidden = last_sums(coords, after(line_three, line_two[3]), [], wide)
    line_one = to_line(sums(coords, plane_jobs(after(plane_one, hidden))))
    *squares, norms = last_sums(coords, [], [line_two, line_one], wide)
    if rest > 1:
        norms = lax.psum(norms, "r")

    def own_block(spread):
        return lax.psum_scatter(spread, "r", scatter_dimension=0, tiled=True) if rest > 1 else spread

    grads = [own_block(grad) for grad in (*squares[5:], *squares[:5], *hidden)]
    return (three.output[None], six.target_back[None], five.source_back[None], *grads, norms)


def solution(mesh):
    dp, inner = mesh.shape["dp"], mesh.shape["inner"]
    fine = Mesh(mesh.devices.reshape(4, 2, 2, dp // 16, inner), ("a", "b", "c", "r", "i"))
    split = ("a", "b", "c", "r")
    in_specs = (
        P((*split, "i"), None, None),
        P((*split, "i"), None, None),
        P((*split, "i"), None),
        P((*split, "i"), None),
        P((*split, "i"), None),
        P(split, "i"),
        P(split, "i"),
        P(split, "i"),
        P(split, "i"),
        P(split, "i"),
        P(split, "i"),
        P(split, "i"),
        P(split, "i"),
        P(split, "i"),
        P(split, "i"),
        P("i", split),
        P((*split, "i"), None, None),
    )
    out_specs = (
        P((*split, "i"), None, None),
        P((*split, "i"), None, None),
        P((*split, "i"), None, None),
        P(split, "i"),
        P(split, "i"),
        P(split, "i"),
        P(split, "i"),
        P(split, "i"),
        P(split, "i"),
        P(split, "i"),
        P(split, "i"),
        P(split, "i"),
        P(split, "i"),
        P("i", split),
    )
    return jax.shard_map(shards, mesh=fine, in_specs=in_specs, out_specs=out_specs, check_vma=False)
```

```python
import functools
import types

import jax
import jax.numpy as jnp
from jax import lax
from jax.experimental import pallas as pl
from jax.experimental.pallas import tpu as pltpu
from jax.sharding import Mesh
from jax.sharding import PartitionSpec as P

EPS = 1e-05
NEG = -1e30
SCALE = 0.125 * 1.4426950408889634
TOKENS = 256
LINE = 4
SELF_BLOCK = 256
SELF_SIZES = (384, 512, 768, 1024)
BACK_SIZES = (384, 512, 640, 768, 1024)
CROSS_BLOCK = 256
CROSS_SIZES = (128, 256, 384)
MIB = 1024 * 1024
BF16 = jnp.bfloat16
SPACE = pltpu.HBM
LARGE = 64
PAIRS = 4
SMALL = 64
F32 = jnp.float32


def dot(left, right):
    return jnp.dot(left, right, preferred_element_type=F32)


def dot_nt(left, right):
    return lax.dot_general(left, right, (((1,), (1,)), ((), ())), preferred_element_type=F32)


def tile(index, size):
    return pl.ds(pl.multiple_of(index * size, size), size)


class Named:
    def __init__(self, act):
        self._act = act

    def __getattr__(self, name):
        return functools.partial(self._act, name)


class Rows:
    def __init__(self, of):
        self.of = of


class Part:
    def __init__(self, array, shape, choose):
        self.array, self.shape, self.dtype, self.choose = array, shape, array.dtype, choose


class Stage:
    def __init__(self):
        self.scalars, self.own, self.ins, self.outs, self.raw = None, {}, {}, {}, []
        self.waited, self.sent = set(), {}
        self.at, self.send = Named(self._at), Named(self._send)

    def begin(self):
        for _, copies in self.ins.values():
            for copy in copies:
                copy.start()

    def _at(self, name, index):
        buffer, copies = self.ins[name]
        if (name, index) not in self.waited:
            self.waited.add((name, index))
            copies[index].wait()
        return buffer

    def __getitem__(self, name):
        if name in self.own:
            return self.own[name]
        if name in self.outs:
            return self.outs[name][0]
        for index in range(len(self.ins[name][1])):
            self._at(name, index)
        return self.ins[name][0]

    def __getattr__(self, name):
        return self[name]

    def _send(self, name, index=None):
        for place, copy in enumerate(self.outs[name][1]):
            if index in (None, place) and (name, place) not in self.sent:
                self.sent[name, place] = copy
                copy.start()

    def finish(self):
        for name in self.ins:
            self[name]
        for name in self.outs:
            self._send(name)
        for copy in self.sent.values():
            copy.wait()


def staged(name, body, scalars, ins, outs, scratch, raw=None, raw_sems=0, weight=0, limit=LARGE):
    raw = raw or []
    by_rows = [label for group in (ins, outs) for label, value in group.items() if isinstance(value, Rows)]
    ins = {label: value.of if isinstance(value, Rows) else value for label, value in ins.items()}
    outs = {label: value.of if isinstance(value, Rows) else value for label, value in outs.items()}

    def copies_of(label, source, target, sems):
        if label not in by_rows:
            return [pltpu.make_async_copy(source, target, sems.pop())]
        spans = [pl.ds(first, TOKENS) for first in range(0, target.shape[0], TOKENS)]
        return [pltpu.make_async_copy(source.at[span], target.at[span], sems.pop()) for span in spans]

    def count_of(label, shape):
        return shape[0] // TOKENS if label in by_rows else 1

    total = sum(count_of(n, v.shape) for n, v in ins.items()) + sum(count_of(n, v[0]) for n, v in outs.items())
    total += raw_sems

    def kernel(*refs):
        refs = list(refs)

        def take(count):
            head = refs[:count]
            del refs[:count]
            return head

        stage = Stage()
        stage.scalars = types.SimpleNamespace(**dict(zip(scalars, take(len(scalars)))))
        in_refs, stage.raw, out_refs = take(len(ins)), take(len(raw)), take(len(outs))
        in_vmem, out_vmem = take(len(ins)), take(len(outs))
        stage.own = dict(zip(scratch, take(len(scratch))))
        stage.own.update(vars(stage.scalars))
        sem_array = take(1)[0]
        sems = [sem_array.at[place] for place in range(total)]
        for label, source, target in zip(ins, in_refs, in_vmem):
            if isinstance(ins[label], Part):
                source = ins[label].choose(source, stage.scalars)
            stage.ins[label] = (target, copies_of(label, source, target, sems))
        for label, source, target in zip(outs, out_vmem, out_refs):
            stage.outs[label] = (source, copies_of(label, source, target, sems))
        stage.raw_sems = sems
        if not raw:
            stage.begin()
        body(stage)
        stage.finish()

    results = pl.pallas_call(
        kernel,
        out_shape=[jax.ShapeDtypeStruct(*shape) for shape in outs.values()],
        in_specs=[pl.BlockSpec(memory_space=pltpu.SMEM)] * len(scalars)
        + [pl.BlockSpec(memory_space=SPACE)] * (len(ins) + len(raw)),
        out_specs=[pl.BlockSpec(memory_space=SPACE)] * len(outs),
        scratch_shapes=[pltpu.VMEM(array.shape, array.dtype) for array in ins.values()]
        + [pltpu.VMEM(*shape) for shape in outs.values()]
        + [pltpu.VMEM(*shape) for shape in scratch.values()]
        + [pltpu.SemaphoreType.DMA((total,))],
        compiler_params=pltpu.CompilerParams(vmem_limit_bytes=limit * MIB),
        cost_estimate=pl.CostEstimate(
            flops=1000 + weight * 10**9, bytes_accessed=1000 + weight * 3 * 10**6, transcendentals=0
        ),
        name=name,
    )(
        *scalars.values(),
        *[array.array if isinstance(array, Part) else array for array in ins.values()],
        *raw,
    )
    return types.SimpleNamespace(**{str(label): result for label, result in zip(outs, results)})


def place_of(coords, line_first, part, entry):
    core, first = part // 4, part % 4
    back, plane = (entry, first) if line_first else (first, entry)
    line = (coords[0] - back) & 3
    outer = coords[1] ^ (plane >> 1)
    inner = coords[3] ^ (plane & 1)
    dp = (line * 2 + outer) * 2 + (coords[2] ^ core)
    return dp, inner


def piece_copies(stage, pieces, sems, spot, line_first=True):
    copies = []
    for part in range(8):
        for entry in range(4):
            dp, inner = place_of(stage.coords, line_first, part, entry)
            for which, target in spot(dp, inner):
                copies.append(pltpu.make_async_copy(pieces[part].at[entry, which], target, sems[len(copies)]))
    for copy in copies:
        copy.start()
    return copies


def standard(value):
    centre = value - jnp.mean(value, -1, keepdims=True)
    rate = lax.rsqrt(jnp.mean(centre * centre, -1, keepdims=True) + EPS)
    return centre * rate, rate


def standard_back(value, gain, upstream):
    z, rate = standard(value)
    scaled = upstream * gain
    back = rate * (scaled - jnp.mean(scaled, -1, keepdims=True) - z * jnp.mean(scaled * z, -1, keepdims=True))
    return back, upstream * z


def blocks_of_tokens(length, run):
    for index in range(length // TOKENS):
        run(slice(index * TOKENS, (index + 1) * TOKENS), index)


def windowed(sizes, kind, run):
    for place, size in enumerate(sizes):
        pl.when(kind == place)(functools.partial(run, size))


def column_of(row):
    return jnp.broadcast_to(row.astype(F32), (128, row.shape[1])).T[:, :1]


def own_lanes(array, half):
    low = lax.broadcasted_iota(jnp.int32, array.shape, 1) < 64
    zero = jnp.zeros_like(array)
    return jnp.where(low, array, zero) if half == 0 else jnp.where(low, zero, array)


def attend(query, keys_t, values_t, query_seg, key_seg, window, mixed, mixed_t, total, bias, sums_t, sizes, block, first):
    length, width = query.shape
    heads = total.shape[0]
    lane = lax.broadcasted_iota(jnp.int32, (block, 128), 1)

    def one_block(index, carry):
        rows = tile(index, block)
        start = window[first, index]

        def run(size):
            span = pl.ds(pl.multiple_of(start, 128), size)
            bias[:, :size] = jnp.where(column_of(query_seg[:, rows]) == key_seg[:, span].astype(F32), 0.0, NEG)
            ones = jnp.ones((16, size), BF16)

            def one_pair(pair, tops):
                lanes = tile(pair, 128)
                q, k = query[rows, lanes], keys_t[lanes, span]
                for half in range(2):
                    scores = dot(own_lanes(q, half), k) * SCALE + bias[:, :size]
                    top = jnp.max(scores, -1, keepdims=True)
                    expo = jnp.exp2(scores - top).astype(BF16)
                    spot = pl.ds(pl.multiple_of(pair * 128 + half * 64, 64), 64)
                    parts = dot_nt(jnp.concatenate([values_t[spot, span], ones], 0), expo)
                    sums = parts[64:65]
                    mixed_t[spot, rows] = (parts[:64] * (1.0 / sums)).astype(BF16)
                    sums_t[pl.ds(pair * 2 + half, 1), :] = sums
                    tops = jnp.where(lane == pair * 2 + half, top, tops)
                return tops

            tops = lax.fori_loop(0, width // 128, one_pair, jnp.zeros((block, 128), F32), unroll=PAIRS)
            total[:, rows] = tops.T[:heads] + jnp.log2(sums_t[...])

        windowed(sizes, window[first + 1, index], run)
        mixed[rows, :] = mixed_t[:, rows].T
        return carry

    lax.fori_loop(0, length // block, one_block, 0)


def attend_back(query, keys, keys_t, values, back, mixed_t, total, query_seg, key_seg, window, query_back_t, key_acc, value_acc, bias, sizes, block, first):
    length, width = query.shape
    key_acc[...] = jnp.zeros(key_acc.shape, F32)
    value_acc[...] = jnp.zeros(value_acc.shape, F32)

    def one_block(index, carry):
        rows = tile(index, block)
        start = window[first, index]

        def run(size):
            span = pl.ds(pl.multiple_of(start, 128), size)
            bias[:size, :] = jnp.where(column_of(key_seg[:, span]) == query_seg[:, rows].astype(F32), 0.0, NEG)
            low = lax.broadcasted_iota(jnp.int32, (size, 128), 1) < 64

            def one_pair(pair, carried):
                lanes = tile(pair, 128)
                q, k, v, up = query[rows, lanes], keys[span, lanes], values[span, lanes], back[rows, lanes]
                q_t, up_t = q.T, up.T
                product = up_t.astype(F32) * mixed_t[lanes, rows].astype(F32)
                key_parts, value_parts = [], []
                for half in range(2):
                    scores = dot(own_lanes(k, half), q_t) * SCALE + bias[:size, :]
                    probs = jnp.exp2(scores - total[pl.ds(pair * 2 + half, 1), rows])
                    spread = dot(own_lanes(v, half), up_t)
                    delta = jnp.sum(product[half * 64 : half * 64 + 64], 0, keepdims=True)
                    scores_back = (probs * (spread - delta)).astype(BF16)
                    value_parts.append(dot(probs.astype(BF16), up))
                    key_parts.append(dot(scores_back, q))
                    spot = pl.ds(pl.multiple_of(pair * 128 + half * 64, 64), 64)
                    query_back_t[spot, rows] = (dot(keys_t[spot, span], scores_back) * 0.125).astype(BF16)
                value_acc[span, lanes] += jnp.where(low, *value_parts)
                key_acc[span, lanes] += jnp.where(low, *key_parts)
                return carried

            lax.fori_loop(0, width // 128, one_pair, 0, unroll=PAIRS)

        windowed(sizes, window[first + 1, index], run)
        return carry

    lax.fori_loop(0, length // block, one_block, 0)


def put_square(stage, grad, column, base):
    core = stage.coords[2]
    rows = grad.shape[0] // 16
    blocks = grad.astype(BF16).reshape(LINE, 2, 2, rows, grad.shape[1])
    for result, wanted in ((stage.keep, 0), (stage.send_, 1)):
        picked = jnp.where(core == wanted, blocks[:, :, 0], blocks[:, :, 1])
        for outer in range(2):
            for chunk in range(2):
                result[outer * 2 + column, :, base + chunk * rows : base + (chunk + 1) * rows, :] = picked[
                    :, outer, :, chunk * 128 : (chunk + 1) * 128
                ]


def self_forward_body(stage):
    affine, loose, weight = stage.affine, stage.loose, stage.weight
    copies = piece_copies(
        stage, stage.raw, stage.raw_sems, lambda dp, inner: [(slice(0, 7), loose.at[:, dp, :, tile(inner, 256)])]
    )
    stage.begin()
    for copy in copies:
        copy.wait()
    for w in range(3):
        for dp in range(16):
            for half in range(2):
                weight[w, dp * 32 + half * 16 : dp * 32 + half * 16 + 16, :] = loose[2 * w + half, dp]
    flat = jnp.sum(loose[6].astype(F32), 0)
    flat = flat[:, :256] + flat[:, 256:]
    affine[:, :256] = flat[:8]
    affine[:, 256:] = flat[8:]
    stage.send.weight()
    stage.send.affine()
    normed_t = stage.normed_t
    length = normed_t.shape[1]

    def project(rows, index):
        z, _ = standard(stage.at.target(index)[rows, :].astype(F32))
        n = (z * affine[0:1, :] + affine[1:2, :]).astype(BF16)
        normed_t[:, rows] = n.T
        query, key, value = (dot(n, weight[place]).astype(BF16) for place in range(3))
        stage.query[rows, :] = query
        stage.key[rows, :] = key
        stage.value[rows, :] = value
        stage.send.query(index)
        stage.send.key(index)
        stage.send.value(index)
        stage.key_t[:, rows] = key.T
        stage.value_t[:, rows] = value.T

    blocks_of_tokens(length, project)
    stage.send.normed_t()
    stage.send.key_t()
    attend(
        stage.query, stage.key_t, stage.value_t, stage.seg, stage.seg, stage.window, stage.mixed, stage.mixed_t,
        stage.total, stage.bias, stage.sums_t, SELF_SIZES, SELF_BLOCK, 0,
    )


def self_forward(coords, window, target, seg, pieces):
    length, width = target.shape
    low, turned = ((length, width), BF16), ((width, length), BF16)
    return staged(
        "self_forward", self_forward_body, dict(coords=coords, window=window), dict(target=Rows(target), seg=seg),
        dict(
            weight=((3, width, width), BF16), affine=((8, width), F32), query=Rows(low), key=Rows(low),
            value=Rows(low), key_t=turned, normed_t=turned, mixed=low, mixed_t=turned,
            total=((width // 64, length), F32),
        ),
        dict(
            loose=((7, 16, 16, width), BF16), value_t=turned, bias=((SELF_BLOCK, SELF_SIZES[-1]), F32),
            sums_t=((width // 64, SELF_BLOCK), F32),
        ),
        raw=pieces, raw_sems=32,
        weight=20,
    )


def cross_forward_body(stage):
    weight = stage.weight
    copies = piece_copies(
        stage,
        stage.raw,
        stage.raw_sems,
        lambda dp, inner: [(slice(0, 5), weight.at[:, tile(dp, 32), tile(inner, 256)])],
    )
    stage.begin()
    for copy in copies:
        copy.wait()
    stage.send.weight()
    source, affine = stage.source, stage.affine
    first = stage.first
    length = first.shape[0]
    padded = stage.padded
    count = source.shape[0]
    padded[...] = jnp.zeros(padded.shape, BF16)
    padded[:count, :] = source[...]
    stage.key[...] = dot(padded[...], weight[2]).astype(BF16)
    stage.value[...] = dot(padded[...], weight[3]).astype(BF16)
    stage.key_t[...] = stage.key[...].T
    stage.value_t[...] = stage.value[...].T
    stage.send.key()
    stage.send.key_t()
    stage.send.value()

    def project(rows, index):
        v = stage.at.target(index)[rows, :].astype(F32) + dot(stage.at.mixed1(index)[rows, :], weight[0])
        first[rows, :] = v
        stage.send.first(index)
        z, _ = standard(v)
        n = (z * affine[2:3, :] + affine[3:4, :]).astype(BF16)
        stage.normed2_t[:, rows] = n.T
        stage.query[rows, :] = dot(n, weight[1]).astype(BF16)
        stage.send.query(index)

    blocks_of_tokens(length, project)
    stage.send.normed2_t()
    attend(
        stage.query, stage.key_t, stage.value_t, stage.seg, stage.key_seg, stage.window, stage.mixed,
        stage.mixed_t, stage.total, stage.bias, stage.sums_t, CROSS_SIZES, CROSS_BLOCK, 2,
    )
    stage.send.mixed_t()
    stage.send.total()

    def finish(rows, index):
        m = stage.mixed[rows, :]
        v = first[rows, :] + dot(m, weight[4])
        stage.second[rows, :] = v
        z, _ = standard(v)
        n = (z * affine[4:5, :] + affine[5:6, :]).astype(BF16)
        stage.normed[rows, :] = n
        stage.normed_t[:, rows] = n.T
        stage.send.second(index)
        stage.send.normed(index)

    blocks_of_tokens(length, finish)


def cross_forward(coords, window, target, mixed1, affine, source, seg, key_seg, pieces):
    length, width = target.shape
    count = key_seg.shape[1]
    low, turned, full = ((length, width), BF16), ((width, length), BF16), ((length, width), F32)
    return staged(
        "cross_forward", cross_forward_body, dict(coords=coords, window=window),
        dict(
            mixed1=Rows(mixed1), target=Rows(target), affine=affine, source=source, seg=seg, key_seg=key_seg
        ),
        dict(
            weight=((5, width, width), BF16), key=((count, width), BF16), key_t=((width, count), BF16), value=((count, width), BF16),
            first=Rows(full), normed2_t=turned, query=Rows(low), mixed_t=turned,
            total=((width // 64, length), F32), second=Rows(full), normed=Rows(low), normed_t=turned,
        ),
        dict(
            bias=((CROSS_BLOCK, CROSS_SIZES[-1]), F32), sums_t=((width // 64, CROSS_BLOCK), F32),
            value_t=((width, count), BF16), mixed=low, padded=((count, width), BF16),
        ),
        raw=pieces, raw_sems=32,
        weight=20,
    )


FF_BLOCK = 256
FF_TOKENS = 512


def feed_forward_body(stage):
    expand, shrink, active, hidden_back = stage.expand, stage.shrink, stage.active, stage.hidden_back
    loose_expand, loose_shrink = stage.loose_expand, stage.loose_shrink
    copies = piece_copies(
        stage,
        stage.raw,
        stage.raw_sems,
        lambda dp, inner: [
            (slice(0, 4), loose_expand.at[tile(inner, 4), tile(dp, 32), :]),
            (slice(4, 8), loose_shrink.at[inner, tile(dp, 4)]),
        ],
    )
    stage.begin()
    core = stage.coords[2]
    width, hidden = expand.shape
    for copy in copies:
        copy.wait()
    for part in range(hidden // FF_BLOCK):
        expand[:, part * FF_BLOCK : (part + 1) * FF_BLOCK] = loose_expand[part]
    for side in range(2):
        shrink[:, side * width // 2 : (side + 1) * width // 2] = loose_shrink[side].reshape(hidden, width // 2)
    normed, back = stage.normed, stage.back
    normed_t, back_t = stage.normed_t, stage.back_t
    length = normed.shape[0]
    back_t[...] = back[...].T

    def one_part(part):
        lanes = slice(part * FF_BLOCK, (part + 1) * FF_BLOCK)
        for index in range(length // FF_TOKENS):
            rows = slice(index * FF_TOKENS, (index + 1) * FF_TOKENS)
            v = dot(normed[rows, :], expand[:, lanes])
            up = dot_nt(back[rows, :], shrink[lanes, :])
            square = v * v
            half = 0.5 + 0.5 * jnp.tanh(v * (0.7978845608028654 + 0.035677408136300125 * square))
            value = v * half
            slope = half + value * (1.0 - half) * (1.5957691216057308 + 0.21406444881780075 * square)
            active[rows, lanes] = value.astype(BF16)
            hidden_back[rows, lanes] = (up * slope).astype(BF16)
        grad = dot(normed_t[...], hidden_back[:, lanes]).astype(BF16)
        blocks = grad.reshape(LINE, 2, 2, width // 16, FF_BLOCK)
        inner, chunk = part // 4, part % 4 * 2
        for result, wanted in ((stage.keep, 0), (stage.send_, 1)):
            picked = jnp.where(core == wanted, blocks[:, :, 0], blocks[:, :, 1])
            for outer in range(2):
                for side in range(2):
                    first = (chunk + side) * width // 16
                    result[outer * 2 + inner, :, first : first + width // 16, :] = picked[
                        :, outer, :, side * 128 : (side + 1) * 128
                    ]
        grad = dot(back_t[...], active[:, lanes]).astype(BF16)
        line, outer = part // 2, part % 2
        for result, wanted in ((stage.keep, 0), (stage.send_, 1)):
            picked = jnp.where(core == wanted, grad[:, :128], grad[:, 128:])
            for side in range(2):
                result[outer * 2 + side, line, width // 2 :, :] = picked[side * width // 2 : (side + 1) * width // 2]

    for part in range(hidden // FF_BLOCK):
        one_part(part)
    stage.send.send_()
    stage.send.keep()

    def finish(rows, index):
        stage.normed_back[rows, :] = dot_nt(hidden_back[rows, :], expand[...])
        stage.send.normed_back(index)
        stage.output[rows, :] = (stage.at.second(index)[rows, :] + dot(active[rows, :], shrink[...])).astype(BF16)
        stage.send.output(index)

    blocks_of_tokens(length, finish)


def feed_forward(coords, normed, normed_t, second, back, pieces):
    length, width = normed.shape
    hidden = 4 * width
    part = ((4, LINE, width, 128), BF16)
    wide = ((length, hidden), BF16)
    return staged(
        "feed_forward", feed_forward_body, dict(coords=coords),
        dict(normed=normed, back=back, normed_t=normed_t, second=Rows(second)),
        dict(
            send_=part, keep=part, normed_back=Rows(((length, width), F32)), output=Rows(((length, width), BF16))
        ),
        dict(
            loose_expand=((hidden // FF_BLOCK, width, FF_BLOCK), BF16),
            loose_shrink=((2, hidden // 32, 32, width // 2), BF16),
            expand=((width, hidden), BF16), shrink=((hidden, width), BF16), active=wide, hidden_back=wide,
            back_t=((width, length), BF16),
        ),
        raw=pieces, raw_sems=64,
        weight=20,
    )


def add_affine(stage, row, gain, bias):
    stage.affine_back[row : row + 1, :] += jnp.sum(gain, 0, keepdims=True)
    stage.affine_back[row + 1 : row + 2, :] += jnp.sum(bias, 0, keepdims=True)


def norm_back_body(stage):
    affine = stage.affine
    stage.affine_back[...] = jnp.zeros(stage.affine_back.shape, F32)

    def run(rows, index):
        upstream = stage.at.normed_back(index)[rows, :]
        grad, gain = standard_back(stage.at.second(index)[rows, :], affine[4:5, :], upstream)
        add_affine(stage, 4, gain, upstream)
        grad = grad + stage.at.back(index)[rows, :].astype(F32)
        stage.second_back[rows, :] = grad
        low = grad.astype(BF16)
        stage.out_back[rows, :] = low
        stage.mixed_back[rows, :] = dot_nt(low, stage.weight[...]).astype(BF16)
        stage.send.second_back(index)
        stage.send.out_back(index)
        stage.send.mixed_back(index)

    blocks_of_tokens(stage.second_back.shape[0], run)


def norm_back(affine, weight, second, normed_back, back):
    length, width = second.shape
    low, full = ((length, width), BF16), ((length, width), F32)
    return staged(
        "norm_back", norm_back_body, {},
        dict(
            affine=affine, normed_back=Rows(normed_back), second=Rows(second), back=Rows(back),
            weight=Part(weight, (width, width), lambda ref, scalars: ref.at[4]),
        ),
        dict(affine_back=((8, width), F32), mixed_back=Rows(low), second_back=Rows(full), out_back=Rows(low)),
        {},
        weight=3,
    )


def square_grads(stage, base, left_t, right, turned):
    for column in range(2):
        cols = slice(column * 256, (column + 1) * 256)
        grad = dot_nt(left_t[...], right[cols, :]) if turned else dot(left_t[...], right[:, cols])
        put_square(stage, grad, column, base)


def cross_back_body(stage):
    query = stage.query
    key_acc, value_acc, query_back = stage.key_acc, stage.value_acc, stage.query_back
    attend_back(
        query, stage.key, stage.key_t, stage.value, stage.mixed_back, stage.mixed_t, stage.total, stage.seg,
        stage.key_seg, stage.window, query_back, key_acc, value_acc, stage.bias, CROSS_SIZES, CROSS_BLOCK, 2,
    )
    affine, weight, key_back, value_back = stage.affine, stage.weight, stage.key_back, stage.value_back
    key_back[...] = (key_acc[...] * 0.125).astype(BF16)
    value_back[...] = value_acc[...].astype(BF16)
    source_back = dot_nt(key_back[...], weight[2]) + dot_nt(value_back[...], weight[3])
    stage.source_back[...] = source_back[: stage.source_back.shape[0]]
    stage.send.source_back()
    stage.affine_back[...] = stage.affine_before[...]
    first_low = stage.first_low

    def run(rows, index):
        upstream = dot(weight[1], query_back[:, rows]).T
        grad, gain = standard_back(stage.first[rows, :], affine[2:3, :], upstream)
        add_affine(stage, 2, gain, upstream)
        grad = grad + stage.second_back[rows, :]
        stage.first_back[rows, :] = grad
        low = grad.astype(BF16)
        first_low[rows, :] = low
        stage.mixed1_back[rows, :] = dot_nt(low, weight[0]).astype(BF16)

    blocks_of_tokens(query.shape[0], run)
    stage.send.first_back()
    stage.send.mixed1_back()
    stage.send.affine_back()
    rows_of = weight.shape[1] // 16 * 2
    square_grads(stage, 0, stage.mixed1_t, first_low, False)
    square_grads(stage, rows_of, stage.normed_t, query_back, True)
    padded, source_t = stage.padded, stage.source_t
    padded[...] = jnp.zeros(padded.shape, BF16)
    padded[: stage.source.shape[0], :] = stage.source[...]
    source_t[...] = padded[...].T
    square_grads(stage, 2 * rows_of, source_t, key_back, False)
    square_grads(stage, 3 * rows_of, source_t, value_back, False)
    square_grads(stage, 4 * rows_of, stage.mixed_t, stage.out_back, False)


def cross_back(coords, window, ins, source_length):
    ins_ = types.SimpleNamespace(**ins)
    length, width = ins_.query.shape
    count = ins_.key.shape[0]
    low, full = ((length, width), BF16), ((length, width), F32)
    keyed = (count, width)
    part = ((4, LINE, 5 * width // 8, 128), BF16)
    return staged(
        "cross_back", cross_back_body, dict(coords=coords, window=window), ins,
        dict(
            keep=part, send_=part, first_back=full, mixed1_back=low, affine_back=((8, width), F32),
            source_back=((source_length, width), F32),
        ),
        dict(
            key_acc=(keyed, F32), value_acc=(keyed, F32), query_back=((width, length), BF16), first_low=low,
            key_back=(keyed, BF16), value_back=(keyed, BF16), bias=((CROSS_SIZES[-1], CROSS_BLOCK), F32),
            padded=(keyed, BF16), source_t=((width, count), BF16),
        ),
        weight=20,
    )


AFFINE_ROWS = 16


def pack_first_body(wide, stage):
    for place in range(3):
        for half in range(2):
            stage.packed[2 * place + half] = stage[place][half * 16 : half * 16 + 16, :]
    coords = stage.coords
    own = stage.norms[...].astype(F32)
    width = 2 * stage.packed.shape[2]
    row_at, from_row = (lax.broadcasted_iota(jnp.int32, (8, own.shape[0]), axis) for axis in range(2))
    from_lane, lane_at = (lax.broadcasted_iota(jnp.int32, (wide, width), axis) for axis in range(2))
    down = (row_at == coords[3] * 3 + from_row).astype(F32)
    right = (lane_at == coords[4] + from_lane).astype(F32)
    placed = dot(down, dot(own, right)).astype(BF16)
    stage.packed[6] = jnp.concatenate([placed[:, : width // 2], placed[:, width // 2 :]], 0)


def pack_first(coords, weights, norms):
    ins = {**dict(enumerate(weights)), **dict(norms=norms)}
    outs = dict(packed=((7, 16, weights[0].shape[1]), BF16))
    body = functools.partial(pack_first_body, norms.shape[1])
    return staged("pack", body, dict(coords=coords), ins, outs, {}, limit=SMALL).packed


def find_windows(seg, keys, sizes, block, count):
    lane = lax.broadcasted_iota(jnp.int32, (1, 128), 1)
    starts, kinds = jnp.zeros((1, 128), jnp.int32), jnp.zeros((1, 128), jnp.int32)
    for index in range(seg.shape[1] // block):
        first, last = seg[:, index * block : index * block + 1], seg[:, (index + 1) * block - 1 : (index + 1) * block]
        low = jnp.sum((keys < first).astype(F32), 1, keepdims=True).astype(jnp.int32) // 128 * 128
        high = (jnp.sum((keys <= last).astype(F32), 1, keepdims=True).astype(jnp.int32) + 127) // 128 * 128
        need = high - low
        kind = sum(((need > size).astype(jnp.int32) for size in sizes[:-1]), jnp.zeros_like(need))
        size = sum((jnp.where(kind == place, size, 0) for place, size in enumerate(sizes)), jnp.zeros_like(need))
        starts = jnp.where(lane == index, jnp.minimum(low, count - size), starts)
        kinds = jnp.where(lane == index, kind, kinds)
    return starts, kinds


def pack_rest_body(stage):
    for place in range(5):
        stage.second[place] = stage[place][...]
    for place in range(4):
        stage.third[place] = stage.expand[:, place * 256 : place * 256 + 256]
        stage.third[4 + place] = stage.shrink[place * 32 : place * 32 + 32, :]
    seg, source_seg = stage.seg[...], stage.source_seg[...]
    count = stage.key_seg.shape[1]
    stage.key_seg[...] = jnp.full(stage.key_seg.shape, -1, jnp.int32)
    stage.key_seg[:, : source_seg.shape[1]] = jnp.where(stage.source_keep[...] > 0, source_seg, -1)
    rows = (
        *find_windows(seg, seg, SELF_SIZES, SELF_BLOCK, seg.shape[1]),
        *find_windows(seg, source_seg, CROSS_SIZES, CROSS_BLOCK, count),
        *find_windows(seg, seg, BACK_SIZES, SELF_BLOCK, seg.shape[1]),
    )
    stage.window[...] = jnp.zeros(stage.window.shape, jnp.int32)
    for place, row in enumerate(rows):
        stage.window[place : place + 1, :] = row


def pack_rest(weights, expand, shrink, seg, source_seg, source_keep):
    ins = {
        **dict(enumerate(weights)),
        **dict(expand=expand, shrink=shrink, seg=seg, source_seg=source_seg, source_keep=source_keep),
    }
    outs = dict(
        second=((5, 32, 256), BF16), third=((8, 32, 256), BF16), window=((8, 128), jnp.int32),
        key_seg=((1, CROSS_SIZES[-1]), jnp.int32),
    )
    return staged("pack", pack_rest_body, {}, ins, outs, {})


def self_back_body(stage):
    query = stage.query
    key_acc, value_acc, query_back = stage.key_acc, stage.value_acc, stage.query_back
    attend_back(
        query, stage.key, stage.key_t, stage.value, stage.mixed_back, stage.mixed_t, stage.total, stage.seg,
        stage.seg, stage.window, query_back, key_acc, value_acc, stage.bias, BACK_SIZES, SELF_BLOCK, 4,
    )
    weight, affine = stage.weight, stage.affine
    key_back, value_back = stage.key_back, stage.value_back
    key_back[...] = (key_acc[...] * 0.125).astype(BF16)
    value_back[...] = value_acc[...].astype(BF16)
    stage.affine_back[...] = stage.affine_before[...]

    def run(rows, index):
        upstream = dot_nt(key_back[rows, :], weight[1]) + dot_nt(value_back[rows, :], weight[2])
        upstream = upstream + dot(weight[0], query_back[:, rows]).T
        grad, gain = standard_back(stage.target[rows, :].astype(F32), affine[0:1, :], upstream)
        add_affine(stage, 0, gain, upstream)
        stage.target_back[rows, :] = grad + stage.first_back[rows, :]
        stage.send.target_back(index)

    blocks_of_tokens(query.shape[0], run)
    width = query.shape[1]
    rows_of = width // 16 * 2
    square_grads(stage, 0, stage.normed_t, query_back, True)
    square_grads(stage, rows_of, stage.normed_t, key_back, False)
    square_grads(stage, 2 * rows_of, stage.normed_t, value_back, False)
    norms = stage.affine_back[...]
    norms = jnp.concatenate([norms, jnp.zeros_like(norms)], 0)
    for inner in range(2):
        low = (norms if inner == 0 else jnp.concatenate([norms[3:], norms[:3]], 0)).astype(BF16)
        for line in range(LINE):
            for result in (stage.keep, stage.send_):
                for outer in range(2):
                    result[outer * 2 + inner, line, 3 * rows_of :, :] = low[:, line * 128 : (line + 1) * 128]


def self_back(coords, window, ins):
    ins_ = types.SimpleNamespace(**ins)
    length, width = ins_.query.shape
    low, turned = ((length, width), BF16), ((width, length), BF16)
    part = ((4, LINE, 3 * width // 8 + AFFINE_ROWS, 128), BF16)
    return staged(
        "self_back", self_back_body, dict(coords=coords, window=window), ins,
        dict(send_=part, keep=part, target_back=Rows(((length, width), F32))),
        dict(
            key_acc=((length, width), F32), value_acc=((length, width), F32), query_back=turned, key_back=low,
            value_back=low, affine_back=((8, width), F32), bias=((BACK_SIZES[-1], SELF_BLOCK), F32),
        ),
        weight=20,
    )


def sums_body(jobs, stage):
    place = 0
    for index, job in enumerate(jobs):
        total = stage[place, index][...].astype(F32)
        for more in range(1, len(job)):
            total = total + stage[place + more, index][...].astype(F32)
        place += len(job)
        stage.outs[index][0][...] = total.astype(BF16)
        stage._send(index)


def sums(coords, jobs):
    ins = {}
    for index, job in enumerate(jobs):
        for part in job:
            ins[len(ins), index] = part
    outs = {index: (job[0].shape, BF16) for index, job in enumerate(jobs)}
    body = functools.partial(sums_body, jobs)
    return list(vars(staged("sums", body, dict(coords=coords), ins, outs, {}, limit=SMALL)).values())


def plane_part(array, step):
    def choose(ref, scalars):
        coords = scalars.coords
        return ref.at[(coords[1] ^ (step >> 1)) * 2 + (coords[3] ^ (step & 1))]

    return Part(array, array.shape[1:], choose)


def line_part(array, step):
    return Part(array, array.shape[1:], lambda ref, scalars: ref.at[(scalars.coords[0] + step) & 3])


ORDER = (1, 2, 3, 0)


def chip_jobs(keep, away):
    return [[plane_part(keep, step), plane_part(away, step)] for step in ORDER]


def plane_jobs(arrays):
    return [[line_part(array, step) for array in arrays] for step in ORDER]


def last_sums_body(hidden, squares, wide, stage):
    def total_of(first):
        parts = [stage[first + place][...].astype(F32) for place in range(4)]
        return parts[0] + parts[1] + (parts[2] + parts[3])

    results = [value[0] for value in stage.outs.values()]
    if hidden:
        total = total_of(0)
        half = total.shape[0] // 2
        rows = half // 8
        for chunk in range(8):
            results[0][:, chunk * 128 : (chunk + 1) * 128] = total[chunk * rows : (chunk + 1) * rows]
        results[1][...] = total[half:].T
        results = results[2:]
    first = 4 if hidden else 0
    for count in squares:
        total = total_of(first)
        first += 4
        for place in range(count):
            for chunk in range(2):
                row = (2 * place + chunk) * 32
                results[place][:, chunk * 128 : (chunk + 1) * 128] = total[row : row + 32]
        results = results[count:]
        if total.shape[0] > count * 64:
            lane = (stage.coords[1] * 2 + stage.coords[2]) * 32 + stage.coords[5]
            norms = pltpu.roll(total[count * 64 : count * 64 + 8], (128 - lane) & 127, 1)
            results[0][...] = norms[:3, :wide]
            results = results[1:]


def last_sums(coords, hidden, squares, wide):
    arrays = [array for group in ([hidden] if hidden else []) + squares for array in group]
    outs = {}
    if hidden:
        rows = hidden[0].shape[0]
        outs[(0,)] = ((rows // 16, 1024), F32)
        outs[(1,)] = ((128, rows // 2), F32)
    counts = []
    for group in squares:
        counts.append(group[0].shape[0] // 64)
        for _ in range(counts[-1]):
            outs[(len(outs),)] = ((32, 256), F32)
        if group[0].shape[0] % 64:
            outs[(len(outs),)] = ((3, wide), F32)
    body = functools.partial(last_sums_body, bool(hidden), counts, wide)
    result = staged("last_sums", body, dict(coords=coords), dict(enumerate(arrays)), outs, {}, limit=SMALL)
    return list(vars(result).values())


SWAP = [(0, 1), (1, 0)]
SHIFTS = [[(i, (i + k) % LINE) for i in range(LINE)] for k in range(LINE)]
CROSS = [[(i, i ^ k) for i in range(4)] for k in range(4)]
PLANE = ("b", "i")


def tie(*values):
    return lax.optimization_barrier(values)


def join(arrays):
    return jnp.concatenate(arrays, 0).reshape(len(arrays), *arrays[0].shape)


def along_line(array):
    return [array] + [lax.ppermute(array, "a", SHIFTS[k]) for k in (1, 2, 3)]


def along_plane(array):
    return [array] + [lax.ppermute(array, PLANE, CROSS[k]) for k in (1, 2, 3)]


def across_cores(arrays):
    return arrays + [lax.ppermute(array, "c", SWAP) for array in arrays]


def swap_cores(array):
    return lax.ppermute(array, "c", SWAP)


def to_plane(arrays):
    return [lax.ppermute(array, PLANE, CROSS[k]) for array, k in zip(arrays, (1, 2, 3))] + arrays[3:4]


def to_line(arrays):
    return [lax.ppermute(array, "a", SHIFTS[k]) for array, k in zip(arrays, (1, 2, 3))] + arrays[3:4]


def shards(
    target,
    source,
    target_segment,
    source_segment,
    source_keep,
    self_query,
    self_key,
    self_value,
    self_output,
    cross_query,
    cross_key,
    cross_value,
    cross_output,
    expand_weight,
    shrink_weight,
    norm_affine,
    cotangent,
):
    src_length = source.shape[1]
    rest = lax.axis_size("r")
    wide = norm_affine.shape[1]
    a, b, c, r, i = (lax.axis_index(name) for name in "abcri")
    coords = jnp.stack([a, b, c, i, (((a * 2 + b) * 2 + c) * rest + r) * wide, r * wide]).astype(jnp.int32)

    def whole_rows(shard):
        return lax.all_gather(shard, "r", axis=0, tiled=True) if rest > 1 else shard

    shard_one = pack_first(coords, [whole_rows(w) for w in (self_query, self_key, self_value)], norm_affine)
    if rest > 1:
        norms = lax.psum(shard_one[6].astype(F32), "r").astype(BF16)
        shard_one = jnp.concatenate([shard_one[:6], norms[None]], 0)
    x, upstream, sent = target[0], cotangent[0], source[0]
    line_one = along_line(shard_one)
    others = [whole_rows(w) for w in (self_output, cross_query, cross_key, cross_value, cross_output)]
    rest_of = pack_rest(
        others, whole_rows(expand_weight), whole_rows(shrink_weight), target_segment, source_segment, source_keep
    )
    seg, key_seg, window = target_segment, rest_of.key_seg, rest_of.window
    joined_one, shard_two = tie(join(line_one), rest_of.second)
    near_one = along_plane(joined_one)
    line_two = along_line(shard_two)
    near_one, line_two = tie(near_one, line_two)
    pieces_one = across_cores(near_one)
    stage_two = along_plane(join(line_two))
    line_three = along_line(rest_of.third)
    one = self_forward(coords, window, x, seg, pieces_one)
    line_three, one.mixed = tie(line_three, one.mixed)
    pieces_two = across_cores([tie(array, one.mixed)[0] for array in stage_two])
    stage_three = along_plane(join(line_three))
    two = cross_forward(coords, window, x, one.mixed, one.affine, sent, seg, key_seg, pieces_two)
    pieces_three = across_cores([tie(array, two.normed)[0] for array in stage_three])
    three = feed_forward(coords, two.normed, two.normed_t, two.second, upstream, pieces_three)
    away_three = swap_cores(three.send_)
    four = norm_back(one.affine, two.weight, two.second, three.normed_back, upstream)
    away_three, four.mixed_back = tie(away_three, four.mixed_back)
    chip_three = sums(coords, chip_jobs(three.keep, away_three))
    chip_three, four.mixed_back = tie(chip_three, four.mixed_back)
    plane_three = to_plane(chip_three)
    five = cross_back(
        coords,
        window,
        dict(
            query=two.query, key=two.key, seg=seg, key_seg=key_seg, mixed_t=two.mixed_t, total=two.total,
            value=two.value, mixed_back=four.mixed_back, key_t=two.key_t, weight=two.weight,
            affine=one.affine, affine_before=four.affine_back, first=two.first, second_back=four.second_back,
            mixed1_t=one.mixed_t, normed_t=two.normed2_t, source=sent, out_back=four.out_back,
        ),
        src_length,
    )
    five.send_, plane_three = tie(five.send_, plane_three)
    away_two = swap_cores(five.send_)
    line_three = to_line(sums(coords, plane_jobs(plane_three)))
    away_two, line_three[3] = tie(away_two, line_three[3])
    chip_two = sums(coords, chip_jobs(five.keep, away_two))
    chip_two, five.mixed1_back = tie(chip_two, five.mixed1_back)
    plane_two = to_plane(chip_two)
    six = self_back(
        coords,
        window,
        dict(
            query=one.query, key=one.key, seg=seg, total=one.total,
            value=one.value, mixed_back=five.mixed1_back, mixed_t=one.mixed_t, key_t=one.key_t,
            weight=one.weight, affine=one.affine, affine_before=five.affine_back, target=x,
            first_back=five.first_back, normed_t=one.normed_t,
        ),
    )
    six.send_, plane_two, line_three = tie(six.send_, plane_two, line_three)
    away_one = swap_cores(six.send_)
    tail = sums(coords, chip_jobs(six.keep, away_one) + plane_jobs(plane_two))
    plane_one = to_plane(tail[:4])
    line_two = to_line(tail[4:])
    line_three, line_two[3] = tie(line_three, line_two[3])
    hidden = last_sums(coords, line_three, [], wide)
    plane_one, hidden = tie(plane_one, hidden)
    line_one = to_line(sums(coords, plane_jobs(plane_one)))
    *squares, norms = last_sums(coords, [], [line_two, line_one], wide)
    if rest > 1:
        norms = lax.psum(norms, "r")

    def own_block(spread):
        return lax.psum_scatter(spread, "r", scatter_dimension=0, tiled=True) if rest > 1 else spread

    grads = [own_block(grad) for grad in (*squares[5:], *squares[:5], *hidden)]
    return (three.output[None], six.target_back[None], five.source_back[None], *grads, norms)


def solution(mesh):
    dp, inner = mesh.shape["dp"], mesh.shape["inner"]
    fine = Mesh(mesh.devices.reshape(4, 2, 2, dp // 16, inner), ("a", "b", "c", "r", "i"))
    split = ("a", "b", "c", "r")
    in_specs = (
        P((*split, "i"), None, None),
        P((*split, "i"), None, None),
        P((*split, "i"), None),
        P((*split, "i"), None),
        P((*split, "i"), None),
        P(split, "i"),
        P(split, "i"),
        P(split, "i"),
        P(split, "i"),
        P(split, "i"),
        P(split, "i"),
        P(split, "i"),
        P(split, "i"),
        P(split, "i"),
        P(split, "i"),
        P("i", split),
        P((*split, "i"), None, None),
    )
    out_specs = (
        P((*split, "i"), None, None),
        P((*split, "i"), None, None),
        P((*split, "i"), None, None),
        P(split, "i"),
        P(split, "i"),
        P(split, "i"),
        P(split, "i"),
        P(split, "i"),
        P(split, "i"),
        P(split, "i"),
        P(split, "i"),
        P(split, "i"),
        P(split, "i"),
        P("i", split),
    )
    return jax.shard_map(shards, mesh=fine, in_specs=in_specs, out_specs=out_specs, check_vma=False)
```

```python
import functools
import types

import jax
import jax.numpy as jnp
from jax import lax
from jax.experimental import pallas as pl
from jax.experimental.pallas import tpu as pltpu
from jax.sharding import Mesh
from jax.sharding import PartitionSpec as P

EPS = 1e-05
NEG = -1e30
SCALE = 0.125 * 1.4426950408889634
TOKENS = 256
LINE = 4
SELF_BLOCK = 256
SELF_SIZES = (384, 512, 768, 1024)
BACK_SIZES = (384, 512, 640, 768, 1024)
CROSS_BLOCK = 256
CROSS_SIZES = (128, 256, 384)
MIB = 1024 * 1024
BF16 = jnp.bfloat16
SPACE = pltpu.HBM
LARGE = 64
PAIRS = 4
SMALL = 64
F32 = jnp.float32


def dot(left, right):
    return jnp.dot(left, right, preferred_element_type=F32)


def dot_nt(left, right):
    return lax.dot_general(left, right, (((1,), (1,)), ((), ())), preferred_element_type=F32)


def tile(index, size):
    return pl.ds(pl.multiple_of(index * size, size), size)


class Named:
    def __init__(self, act):
        self._act = act

    def __getattr__(self, name):
        return functools.partial(self._act, name)


class Rows:
    def __init__(self, of):
        self.of = of


class Part:
    def __init__(self, array, shape, choose):
        self.array, self.shape, self.dtype, self.choose = array, shape, array.dtype, choose


class Stage:
    def __init__(self):
        self.scalars, self.own, self.ins, self.outs, self.raw = None, {}, {}, {}, []
        self.waited, self.sent = set(), {}
        self.at, self.send = Named(self._at), Named(self._send)

    def begin(self):
        for _, copies in self.ins.values():
            for copy in copies:
                copy.start()

    def _at(self, name, index):
        buffer, copies = self.ins[name]
        if (name, index) not in self.waited:
            self.waited.add((name, index))
            copies[index].wait()
        return buffer

    def __getitem__(self, name):
        if name in self.own:
            return self.own[name]
        if name in self.outs:
            return self.outs[name][0]
        for index in range(len(self.ins[name][1])):
            self._at(name, index)
        return self.ins[name][0]

    def __getattr__(self, name):
        return self[name]

    def _send(self, name, index=None):
        for place, copy in enumerate(self.outs[name][1]):
            if index in (None, place) and (name, place) not in self.sent:
                self.sent[name, place] = copy
                copy.start()

    def finish(self):
        for name in self.ins:
            self[name]
        for name in self.outs:
            self._send(name)
        for copy in self.sent.values():
            copy.wait()


def staged(name, body, scalars, ins, outs, scratch, raw=None, raw_sems=0, weight=0, limit=LARGE):
    raw = raw or []
    by_rows = [label for group in (ins, outs) for label, value in group.items() if isinstance(value, Rows)]
    ins = {label: value.of if isinstance(value, Rows) else value for label, value in ins.items()}
    outs = {label: value.of if isinstance(value, Rows) else value for label, value in outs.items()}

    def copies_of(label, source, target, sems):
        if label not in by_rows:
            return [pltpu.make_async_copy(source, target, sems.pop())]
        spans = [pl.ds(first, TOKENS) for first in range(0, target.shape[0], TOKENS)]
        return [pltpu.make_async_copy(source.at[span], target.at[span], sems.pop()) for span in spans]

    def count_of(label, shape):
        return shape[0] // TOKENS if label in by_rows else 1

    total = sum(count_of(n, v.shape) for n, v in ins.items()) + sum(count_of(n, v[0]) for n, v in outs.items())
    total += raw_sems

    def kernel(*refs):
        refs = list(refs)

        def take(count):
            head = refs[:count]
            del refs[:count]
            return head

        stage = Stage()
        stage.scalars = types.SimpleNamespace(**dict(zip(scalars, take(len(scalars)))))
        in_refs, stage.raw, out_refs = take(len(ins)), take(len(raw)), take(len(outs))
        in_vmem, out_vmem = take(len(ins)), take(len(outs))
        stage.own = dict(zip(scratch, take(len(scratch))))
        stage.own.update(vars(stage.scalars))
        sem_array = take(1)[0]
        sems = [sem_array.at[place] for place in range(total)]
        for label, source, target in zip(ins, in_refs, in_vmem):
            if isinstance(ins[label], Part):
                source = ins[label].choose(source, stage.scalars)
            stage.ins[label] = (target, copies_of(label, source, target, sems))
        for label, source, target in zip(outs, out_vmem, out_refs):
            stage.outs[label] = (source, copies_of(label, source, target, sems))
        stage.raw_sems = sems
        if not raw:
            stage.begin()
        body(stage)
        stage.finish()

    results = pl.pallas_call(
        kernel,
        out_shape=[jax.ShapeDtypeStruct(*shape) for shape in outs.values()],
        in_specs=[pl.BlockSpec(memory_space=pltpu.SMEM)] * len(scalars)
        + [pl.BlockSpec(memory_space=SPACE)] * (len(ins) + len(raw)),
        out_specs=[pl.BlockSpec(memory_space=SPACE)] * len(outs),
        scratch_shapes=[pltpu.VMEM(array.shape, array.dtype) for array in ins.values()]
        + [pltpu.VMEM(*shape) for shape in outs.values()]
        + [pltpu.VMEM(*shape) for shape in scratch.values()]
        + [pltpu.SemaphoreType.DMA((total,))],
        compiler_params=pltpu.CompilerParams(vmem_limit_bytes=limit * MIB),
        cost_estimate=pl.CostEstimate(
            flops=1000 + weight * 10**9, bytes_accessed=1000 + weight * 3 * 10**6, transcendentals=0
        ),
        name=name,
    )(
        *scalars.values(),
        *[array.array if isinstance(array, Part) else array for array in ins.values()],
        *raw,
    )
    return types.SimpleNamespace(**{str(label): result for label, result in zip(outs, results)})


def place_of(coords, doubled, part, entry):
    core, plane = part // 4, part % 4
    line = coords[0] ^ entry if doubled else (coords[0] - entry) & 3
    outer = coords[1] ^ (plane >> 1)
    inner = coords[3] ^ (plane & 1)
    return (line * 2 + outer) * 2 + (coords[2] ^ core), inner


def piece_copies(stage, pieces, sems, spot, doubled=False):
    copies = []
    for part in range(8):
        for entry in range(4):
            dp, inner = place_of(stage.coords, doubled, part, entry)
            for which, target in spot(dp, inner):
                copies.append(pltpu.make_async_copy(pieces[part].at[entry, which], target, sems[len(copies)]))
    for copy in copies:
        copy.start()
    return copies


def standard(value):
    centre = value - jnp.mean(value, -1, keepdims=True)
    rate = lax.rsqrt(jnp.mean(centre * centre, -1, keepdims=True) + EPS)
    return centre * rate, rate


def standard_back(value, gain, upstream):
    z, rate = standard(value)
    scaled = upstream * gain
    back = rate * (scaled - jnp.mean(scaled, -1, keepdims=True) - z * jnp.mean(scaled * z, -1, keepdims=True))
    return back, upstream * z


def blocks_of_tokens(length, run):
    for index in range(length // TOKENS):
        run(slice(index * TOKENS, (index + 1) * TOKENS), index)


def windowed(sizes, kind, run):
    for place, size in enumerate(sizes):
        pl.when(kind == place)(functools.partial(run, size))


def column_of(row):
    return jnp.broadcast_to(row.astype(F32), (128, row.shape[1])).T[:, :1]


def own_lanes(array, half):
    low = lax.broadcasted_iota(jnp.int32, array.shape, 1) < 64
    zero = jnp.zeros_like(array)
    return jnp.where(low, array, zero) if half == 0 else jnp.where(low, zero, array)


def attend(query, keys_t, values_t, query_seg, key_seg, window, mixed, mixed_t, total, bias, sums_t, sizes, block, first):
    length, width = query.shape
    heads = total.shape[0]
    lane = lax.broadcasted_iota(jnp.int32, (block, 128), 1)

    def one_block(index, carry):
        rows = tile(index, block)
        start = window[first, index]

        def run(size):
            span = pl.ds(pl.multiple_of(start, 128), size)
            bias[:, :size] = jnp.where(column_of(query_seg[:, rows]) == key_seg[:, span].astype(F32), 0.0, NEG)
            ones = jnp.ones((16, size), BF16)

            def one_pair(pair, tops):
                lanes = tile(pair, 128)
                q, k = query[rows, lanes], keys_t[lanes, span]
                for half in range(2):
                    scores = dot(own_lanes(q, half), k) * SCALE + bias[:, :size]
                    top = jnp.max(scores, -1, keepdims=True)
                    expo = jnp.exp2(scores - top).astype(BF16)
                    spot = pl.ds(pl.multiple_of(pair * 128 + half * 64, 64), 64)
                    parts = dot_nt(jnp.concatenate([values_t[spot, span], ones], 0), expo)
                    sums = parts[64:65]
                    mixed_t[spot, rows] = (parts[:64] * (1.0 / sums)).astype(BF16)
                    sums_t[pl.ds(pair * 2 + half, 1), :] = sums
                    tops = jnp.where(lane == pair * 2 + half, top, tops)
                return tops

            tops = lax.fori_loop(0, width // 128, one_pair, jnp.zeros((block, 128), F32), unroll=PAIRS)
            total[:, rows] = tops.T[:heads] + jnp.log2(sums_t[...])

        windowed(sizes, window[first + 1, index], run)
        mixed[rows, :] = mixed_t[:, rows].T
        return carry

    lax.fori_loop(0, length // block, one_block, 0)


def attend_back(query, keys, keys_t, values, back, mixed_t, total, query_seg, key_seg, window, query_back_t, key_acc, value_acc, bias, sizes, block, first):
    length, width = query.shape
    key_acc[...] = jnp.zeros(key_acc.shape, F32)
    value_acc[...] = jnp.zeros(value_acc.shape, F32)

    def one_block(index, carry):
        rows = tile(index, block)
        start = window[first, index]

        def run(size):
            span = pl.ds(pl.multiple_of(start, 128), size)
            bias[:size, :] = jnp.where(column_of(key_seg[:, span]) == query_seg[:, rows].astype(F32), 0.0, NEG)
            low = lax.broadcasted_iota(jnp.int32, (size, 128), 1) < 64

            def one_pair(pair, carried):
                lanes = tile(pair, 128)
                q, k, v, up = query[rows, lanes], keys[span, lanes], values[span, lanes], back[rows, lanes]
                q_t, up_t = q.T, up.T
                product = up_t.astype(F32) * mixed_t[lanes, rows].astype(F32)
                key_parts, value_parts = [], []
                for half in range(2):
                    scores = dot(own_lanes(k, half), q_t) * SCALE + bias[:size, :]
                    probs = jnp.exp2(scores - total[pl.ds(pair * 2 + half, 1), rows])
                    spread = dot(own_lanes(v, half), up_t)
                    delta = jnp.sum(product[half * 64 : half * 64 + 64], 0, keepdims=True)
                    scores_back = (probs * (spread - delta)).astype(BF16)
                    value_parts.append(dot(probs.astype(BF16), up))
                    key_parts.append(dot(scores_back, q))
                    spot = pl.ds(pl.multiple_of(pair * 128 + half * 64, 64), 64)
                    query_back_t[spot, rows] = (dot(keys_t[spot, span], scores_back) * 0.125).astype(BF16)
                value_acc[span, lanes] += jnp.where(low, *value_parts)
                key_acc[span, lanes] += jnp.where(low, *key_parts)
                return carried

            lax.fori_loop(0, width // 128, one_pair, 0, unroll=PAIRS)

        windowed(sizes, window[first + 1, index], run)
        return carry

    lax.fori_loop(0, length // block, one_block, 0)


def put_square(stage, grad, column, base):
    core = stage.coords[2]
    rows = grad.shape[0] // 16
    blocks = grad.astype(BF16).reshape(LINE, 2, 2, rows, grad.shape[1])
    for result, wanted in ((stage.keep, 0), (stage.send_, 1)):
        picked = jnp.where(core == wanted, blocks[:, :, 0], blocks[:, :, 1])
        for outer in range(2):
            for chunk in range(2):
                result[outer * 2 + column, :, base + chunk * rows : base + (chunk + 1) * rows, :] = picked[
                    :, outer, :, chunk * 128 : (chunk + 1) * 128
                ]


def self_forward_body(stage):
    affine, loose, weight = stage.affine, stage.loose, stage.weight
    copies = piece_copies(
        stage, stage.raw, stage.raw_sems, lambda dp, inner: [(slice(0, 7), loose.at[:, dp, :, tile(inner, 256)])]
    )
    stage.begin()
    for copy in copies:
        copy.wait()
    for w in range(3):
        for dp in range(16):
            for half in range(2):
                weight[w, dp * 32 + half * 16 : dp * 32 + half * 16 + 16, :] = loose[2 * w + half, dp]
    flat = jnp.sum(loose[6].astype(F32), 0)
    flat = flat[:, :256] + flat[:, 256:]
    affine[:, :256] = flat[:8]
    affine[:, 256:] = flat[8:]
    stage.send.weight()
    stage.send.affine()
    normed_t = stage.normed_t
    length = normed_t.shape[1]

    def project(rows, index):
        z, _ = standard(stage.at.target(index)[rows, :].astype(F32))
        n = (z * affine[0:1, :] + affine[1:2, :]).astype(BF16)
        normed_t[:, rows] = n.T
        query, key, value = (dot(n, weight[place]).astype(BF16) for place in range(3))
        stage.query[rows, :] = query
        stage.key[rows, :] = key
        stage.value[rows, :] = value
        stage.send.query(index)
        stage.send.key(index)
        stage.send.value(index)
        stage.key_t[:, rows] = key.T
        stage.value_t[:, rows] = value.T

    blocks_of_tokens(length, project)
    stage.send.normed_t()
    stage.send.key_t()
    attend(
        stage.query, stage.key_t, stage.value_t, stage.seg, stage.seg, stage.window, stage.mixed, stage.mixed_t,
        stage.total, stage.bias, stage.sums_t, SELF_SIZES, SELF_BLOCK, 0,
    )


def self_forward(coords, window, target, seg, pieces):
    length, width = target.shape
    low, turned = ((length, width), BF16), ((width, length), BF16)
    return staged(
        "self_forward", self_forward_body, dict(coords=coords, window=window), dict(target=Rows(target), seg=seg),
        dict(
            weight=((3, width, width), BF16), affine=((8, width), F32), query=Rows(low), key=Rows(low),
            value=Rows(low), key_t=turned, normed_t=turned, mixed=low, mixed_t=turned,
            total=((width // 64, length), F32),
        ),
        dict(
            loose=((7, 16, 16, width), BF16), value_t=turned, bias=((SELF_BLOCK, SELF_SIZES[-1]), F32),
            sums_t=((width // 64, SELF_BLOCK), F32),
        ),
        raw=pieces, raw_sems=32,
        weight=20,
    )


def cross_forward_body(stage):
    weight = stage.weight
    copies = piece_copies(
        stage,
        stage.raw,
        stage.raw_sems,
        lambda dp, inner: [(slice(0, 5), weight.at[:, tile(dp, 32), tile(inner, 256)])],
        doubled=True,
    )
    stage.begin()
    for copy in copies:
        copy.wait()
    stage.send.weight()
    source, affine = stage.source, stage.affine
    first = stage.first
    length = first.shape[0]
    padded = stage.padded
    count = source.shape[0]
    padded[...] = jnp.zeros(padded.shape, BF16)
    padded[:count, :] = source[...]
    stage.key[...] = dot(padded[...], weight[2]).astype(BF16)
    stage.value[...] = dot(padded[...], weight[3]).astype(BF16)
    stage.key_t[...] = stage.key[...].T
    stage.value_t[...] = stage.value[...].T
    stage.send.key()
    stage.send.key_t()
    stage.send.value()

    def project(rows, index):
        v = stage.at.target(index)[rows, :].astype(F32) + dot(stage.at.mixed1(index)[rows, :], weight[0])
        first[rows, :] = v
        stage.send.first(index)
        z, _ = standard(v)
        n = (z * affine[2:3, :] + affine[3:4, :]).astype(BF16)
        stage.normed2_t[:, rows] = n.T
        stage.query[rows, :] = dot(n, weight[1]).astype(BF16)
        stage.send.query(index)

    blocks_of_tokens(length, project)
    stage.send.normed2_t()
    attend(
        stage.query, stage.key_t, stage.value_t, stage.seg, stage.key_seg, stage.window, stage.mixed,
        stage.mixed_t, stage.total, stage.bias, stage.sums_t, CROSS_SIZES, CROSS_BLOCK, 2,
    )
    stage.send.mixed_t()
    stage.send.total()

    def finish(rows, index):
        m = stage.mixed[rows, :]
        v = first[rows, :] + dot(m, weight[4])
        stage.second[rows, :] = v
        z, _ = standard(v)
        n = (z * affine[4:5, :] + affine[5:6, :]).astype(BF16)
        stage.normed[rows, :] = n
        stage.normed_t[:, rows] = n.T
        stage.send.second(index)
        stage.send.normed(index)

    blocks_of_tokens(length, finish)


def cross_forward(coords, window, target, mixed1, affine, source, seg, key_seg, pieces):
    length, width = target.shape
    count = key_seg.shape[1]
    low, turned, full = ((length, width), BF16), ((width, length), BF16), ((length, width), F32)
    return staged(
        "cross_forward", cross_forward_body, dict(coords=coords, window=window),
        dict(
            mixed1=Rows(mixed1), target=Rows(target), affine=affine, source=source, seg=seg, key_seg=key_seg
        ),
        dict(
            weight=((5, width, width), BF16), key=((count, width), BF16), key_t=((width, count), BF16), value=((count, width), BF16),
            first=Rows(full), normed2_t=turned, query=Rows(low), mixed_t=turned,
            total=((width // 64, length), F32), second=Rows(full), normed=Rows(low), normed_t=turned,
        ),
        dict(
            bias=((CROSS_BLOCK, CROSS_SIZES[-1]), F32), sums_t=((width // 64, CROSS_BLOCK), F32),
            value_t=((width, count), BF16), mixed=low, padded=((count, width), BF16),
        ),
        raw=pieces, raw_sems=32,
        weight=20,
    )


FF_BLOCK = 256
FF_TOKENS = 512


def feed_forward_body(stage):
    expand, shrink, active, hidden_back = stage.expand, stage.shrink, stage.active, stage.hidden_back
    loose_expand, loose_shrink = stage.loose_expand, stage.loose_shrink
    coords, copies = stage.coords, []
    for part in range(8):
        core, kind = part // 4, part % 4
        for entry in range(8):
            first, line = entry // 4, coords[0] ^ (entry % 4)
            outer, inner = (kind, first) if kind < 2 else (first, kind - 2)
            outer, inner = coords[1] ^ outer, coords[3] ^ inner
            dp = (line * 2 + outer) * 2 + (coords[2] ^ core)
            if kind < 2:
                spot = loose_expand.at[tile(inner, 4), tile(dp, 32), :]
            else:
                spot = loose_shrink.at[inner, tile(dp, 4)]
            source = stage.raw[part].at[first, entry % 4]
            copies.append(pltpu.make_async_copy(source, spot, stage.raw_sems[len(copies)]))
            copies[-1].start()
    stage.begin()
    core = coords[2]
    width, hidden = expand.shape
    for copy in copies:
        copy.wait()
    for part in range(hidden // FF_BLOCK):
        expand[:, part * FF_BLOCK : (part + 1) * FF_BLOCK] = loose_expand[part]
    for side in range(2):
        shrink[:, side * width // 2 : (side + 1) * width // 2] = loose_shrink[side].reshape(hidden, width // 2)
    normed, back = stage.normed, stage.back
    normed_t, back_t = stage.normed_t, stage.back_t
    length = normed.shape[0]
    back_t[...] = back[...].T

    def one_part(part):
        lanes = slice(part * FF_BLOCK, (part + 1) * FF_BLOCK)
        for index in range(length // FF_TOKENS):
            rows = slice(index * FF_TOKENS, (index + 1) * FF_TOKENS)
            v = dot(normed[rows, :], expand[:, lanes])
            up = dot_nt(back[rows, :], shrink[lanes, :])
            square = v * v
            half = 0.5 + 0.5 * jnp.tanh(v * (0.7978845608028654 + 0.035677408136300125 * square))
            value = v * half
            slope = half + value * (1.0 - half) * (1.5957691216057308 + 0.21406444881780075 * square)
            active[rows, lanes] = value.astype(BF16)
            hidden_back[rows, lanes] = (up * slope).astype(BF16)
        grad = dot(normed_t[...], hidden_back[:, lanes]).astype(BF16)
        blocks = grad.reshape(LINE, 2, 2, width // 16, FF_BLOCK)
        inner, chunk = part // 4, part % 4 * 2
        for result, wanted in ((stage.keep, 0), (stage.send_, 1)):
            picked = jnp.where(core == wanted, blocks[:, :, 0], blocks[:, :, 1])
            for outer in range(2):
                for side in range(2):
                    first = (chunk + side) * width // 16
                    result[outer * 2 + inner, :, first : first + width // 16, :] = picked[
                        :, outer, :, side * 128 : (side + 1) * 128
                    ]
        grad = dot(back_t[...], active[:, lanes]).astype(BF16)
        line, outer = part // 2, part % 2
        for result, wanted in ((stage.keep, 0), (stage.send_, 1)):
            picked = jnp.where(core == wanted, grad[:, :128], grad[:, 128:])
            for side in range(2):
                result[outer * 2 + side, line, width // 2 :, :] = picked[side * width // 2 : (side + 1) * width // 2]

    for part in range(hidden // FF_BLOCK):
        one_part(part)
    stage.send.send_()
    stage.send.keep()

    def finish(rows, index):
        stage.normed_back[rows, :] = dot_nt(hidden_back[rows, :], expand[...])
        stage.send.normed_back(index)
        stage.output[rows, :] = (stage.at.second(index)[rows, :] + dot(active[rows, :], shrink[...])).astype(BF16)
        stage.send.output(index)

    blocks_of_tokens(length, finish)


def feed_forward(coords, normed, normed_t, second, back, pieces):
    length, width = normed.shape
    hidden = 4 * width
    part = ((4, LINE, width, 128), BF16)
    wide = ((length, hidden), BF16)
    return staged(
        "feed_forward", feed_forward_body, dict(coords=coords),
        dict(normed=normed, back=back, normed_t=normed_t, second=Rows(second)),
        dict(
            send_=part, keep=part, normed_back=Rows(((length, width), F32)), output=Rows(((length, width), BF16))
        ),
        dict(
            loose_expand=((hidden // FF_BLOCK, width, FF_BLOCK), BF16),
            loose_shrink=((2, hidden // 32, 32, width // 2), BF16),
            expand=((width, hidden), BF16), shrink=((hidden, width), BF16), active=wide, hidden_back=wide,
            back_t=((width, length), BF16),
        ),
        raw=pieces, raw_sems=64,
        weight=20,
    )


def add_affine(stage, row, gain, bias):
    stage.affine_back[row : row + 1, :] += jnp.sum(gain, 0, keepdims=True)
    stage.affine_back[row + 1 : row + 2, :] += jnp.sum(bias, 0, keepdims=True)


def norm_back_body(stage):
    affine = stage.affine
    stage.affine_back[...] = jnp.zeros(stage.affine_back.shape, F32)

    def run(rows, index):
        upstream = stage.at.normed_back(index)[rows, :]
        grad, gain = standard_back(stage.at.second(index)[rows, :], affine[4:5, :], upstream)
        add_affine(stage, 4, gain, upstream)
        grad = grad + stage.at.back(index)[rows, :].astype(F32)
        stage.second_back[rows, :] = grad
        low = grad.astype(BF16)
        stage.out_back[rows, :] = low
        stage.mixed_back[rows, :] = dot_nt(low, stage.weight[...]).astype(BF16)
        stage.send.second_back(index)
        stage.send.out_back(index)
        stage.send.mixed_back(index)

    blocks_of_tokens(stage.second_back.shape[0], run)


def norm_back(affine, weight, second, normed_back, back):
    length, width = second.shape
    low, full = ((length, width), BF16), ((length, width), F32)
    return staged(
        "norm_back", norm_back_body, {},
        dict(
            affine=affine, normed_back=Rows(normed_back), second=Rows(second), back=Rows(back),
            weight=Part(weight, (width, width), lambda ref, scalars: ref.at[4]),
        ),
        dict(affine_back=((8, width), F32), mixed_back=Rows(low), second_back=Rows(full), out_back=Rows(low)),
        {},
        weight=3,
    )


def square_grads(stage, base, left_t, right, turned):
    for column in range(2):
        cols = slice(column * 256, (column + 1) * 256)
        grad = dot_nt(left_t[...], right[cols, :]) if turned else dot(left_t[...], right[:, cols])
        put_square(stage, grad, column, base)


def cross_back_body(stage):
    query = stage.query
    key_acc, value_acc, query_back = stage.key_acc, stage.value_acc, stage.query_back
    attend_back(
        query, stage.key, stage.key_t, stage.value, stage.mixed_back, stage.mixed_t, stage.total, stage.seg,
        stage.key_seg, stage.window, query_back, key_acc, value_acc, stage.bias, CROSS_SIZES, CROSS_BLOCK, 2,
    )
    affine, weight, key_back, value_back = stage.affine, stage.weight, stage.key_back, stage.value_back
    key_back[...] = (key_acc[...] * 0.125).astype(BF16)
    value_back[...] = value_acc[...].astype(BF16)
    source_back = dot_nt(key_back[...], weight[2]) + dot_nt(value_back[...], weight[3])
    stage.source_back[...] = source_back[: stage.source_back.shape[0]]
    stage.send.source_back()
    stage.affine_back[...] = stage.affine_before[...]
    first_low = stage.first_low

    def run(rows, index):
        upstream = dot(weight[1], query_back[:, rows]).T
        grad, gain = standard_back(stage.first[rows, :], affine[2:3, :], upstream)
        add_affine(stage, 2, gain, upstream)
        grad = grad + stage.second_back[rows, :]
        stage.first_back[rows, :] = grad
        low = grad.astype(BF16)
        first_low[rows, :] = low
        stage.mixed1_back[rows, :] = dot_nt(low, weight[0]).astype(BF16)

    blocks_of_tokens(query.shape[0], run)
    stage.send.first_back()
    stage.send.mixed1_back()
    stage.send.affine_back()
    rows_of = weight.shape[1] // 16 * 2
    square_grads(stage, 0, stage.mixed1_t, first_low, False)
    square_grads(stage, rows_of, stage.normed_t, query_back, True)
    padded, source_t = stage.padded, stage.source_t
    padded[...] = jnp.zeros(padded.shape, BF16)
    padded[: stage.source.shape[0], :] = stage.source[...]
    source_t[...] = padded[...].T
    square_grads(stage, 2 * rows_of, source_t, key_back, False)
    square_grads(stage, 3 * rows_of, source_t, value_back, False)
    square_grads(stage, 4 * rows_of, stage.mixed_t, stage.out_back, False)


def cross_back(coords, window, ins, source_length):
    ins_ = types.SimpleNamespace(**ins)
    length, width = ins_.query.shape
    count = ins_.key.shape[0]
    low, full = ((length, width), BF16), ((length, width), F32)
    keyed = (count, width)
    part = ((4, LINE, 5 * width // 8, 128), BF16)
    return staged(
        "cross_back", cross_back_body, dict(coords=coords, window=window), ins,
        dict(
            keep=part, send_=part, first_back=full, mixed1_back=low, affine_back=((8, width), F32),
            source_back=((source_length, width), F32),
        ),
        dict(
            key_acc=(keyed, F32), value_acc=(keyed, F32), query_back=((width, length), BF16), first_low=low,
            key_back=(keyed, BF16), value_back=(keyed, BF16), bias=((CROSS_SIZES[-1], CROSS_BLOCK), F32),
            padded=(keyed, BF16), source_t=((width, count), BF16),
        ),
        weight=20,
    )


AFFINE_ROWS = 16


def pack_first_body(wide, stage):
    for place in range(3):
        for half in range(2):
            stage.packed[2 * place + half] = stage[place][half * 16 : half * 16 + 16, :]
    coords = stage.coords
    own = stage.norms[...].astype(F32)
    width = 2 * stage.packed.shape[2]
    row_at, from_row = (lax.broadcasted_iota(jnp.int32, (8, own.shape[0]), axis) for axis in range(2))
    from_lane, lane_at = (lax.broadcasted_iota(jnp.int32, (wide, width), axis) for axis in range(2))
    down = (row_at == coords[3] * 3 + from_row).astype(F32)
    right = (lane_at == coords[4] + from_lane).astype(F32)
    placed = dot(down, dot(own, right)).astype(BF16)
    stage.packed[6] = jnp.concatenate([placed[:, : width // 2], placed[:, width // 2 :]], 0)


def pack_first(coords, weights, norms):
    ins = {**dict(enumerate(weights)), **dict(norms=norms)}
    outs = dict(packed=((7, 16, weights[0].shape[1]), BF16))
    body = functools.partial(pack_first_body, norms.shape[1])
    return staged("pack", body, dict(coords=coords), ins, outs, {}, limit=SMALL).packed


def find_windows(seg, keys, sizes, block, count):
    lane = lax.broadcasted_iota(jnp.int32, (1, 128), 1)
    starts, kinds = jnp.zeros((1, 128), jnp.int32), jnp.zeros((1, 128), jnp.int32)
    for index in range(seg.shape[1] // block):
        first, last = seg[:, index * block : index * block + 1], seg[:, (index + 1) * block - 1 : (index + 1) * block]
        low = jnp.sum((keys < first).astype(F32), 1, keepdims=True).astype(jnp.int32) // 128 * 128
        high = (jnp.sum((keys <= last).astype(F32), 1, keepdims=True).astype(jnp.int32) + 127) // 128 * 128
        need = high - low
        kind = sum(((need > size).astype(jnp.int32) for size in sizes[:-1]), jnp.zeros_like(need))
        size = sum((jnp.where(kind == place, size, 0) for place, size in enumerate(sizes)), jnp.zeros_like(need))
        starts = jnp.where(lane == index, jnp.minimum(low, count - size), starts)
        kinds = jnp.where(lane == index, kind, kinds)
    return starts, kinds


def pack_rest_body(stage):
    for place in range(5):
        stage.second[place] = stage[place][...]
    for place in range(4):
        stage.third[place] = stage.expand[:, place * 256 : place * 256 + 256]
        stage.third[4 + place] = stage.shrink[place * 32 : place * 32 + 32, :]
    seg, source_seg = stage.seg[...], stage.source_seg[...]
    count = stage.key_seg.shape[1]
    stage.key_seg[...] = jnp.full(stage.key_seg.shape, -1, jnp.int32)
    stage.key_seg[:, : source_seg.shape[1]] = jnp.where(stage.source_keep[...] > 0, source_seg, -1)
    rows = (
        *find_windows(seg, seg, SELF_SIZES, SELF_BLOCK, seg.shape[1]),
        *find_windows(seg, source_seg, CROSS_SIZES, CROSS_BLOCK, count),
        *find_windows(seg, seg, BACK_SIZES, SELF_BLOCK, seg.shape[1]),
    )
    stage.window[...] = jnp.zeros(stage.window.shape, jnp.int32)
    for place, row in enumerate(rows):
        stage.window[place : place + 1, :] = row


def pack_rest(weights, expand, shrink, seg, source_seg, source_keep):
    ins = {
        **dict(enumerate(weights)),
        **dict(expand=expand, shrink=shrink, seg=seg, source_seg=source_seg, source_keep=source_keep),
    }
    outs = dict(
        second=((5, 32, 256), BF16), third=((8, 32, 256), BF16), window=((8, 128), jnp.int32),
        key_seg=((1, CROSS_SIZES[-1]), jnp.int32),
    )
    return staged("pack", pack_rest_body, {}, ins, outs, {})


def self_back_body(stage):
    query = stage.query
    key_acc, value_acc, query_back = stage.key_acc, stage.value_acc, stage.query_back
    attend_back(
        query, stage.key, stage.key_t, stage.value, stage.mixed_back, stage.mixed_t, stage.total, stage.seg,
        stage.seg, stage.window, query_back, key_acc, value_acc, stage.bias, BACK_SIZES, SELF_BLOCK, 4,
    )
    weight, affine = stage.weight, stage.affine
    key_back, value_back = stage.key_back, stage.value_back
    key_back[...] = (key_acc[...] * 0.125).astype(BF16)
    value_back[...] = value_acc[...].astype(BF16)
    stage.affine_back[...] = stage.affine_before[...]

    def run(rows, index):
        upstream = dot_nt(key_back[rows, :], weight[1]) + dot_nt(value_back[rows, :], weight[2])
        upstream = upstream + dot(weight[0], query_back[:, rows]).T
        grad, gain = standard_back(stage.target[rows, :].astype(F32), affine[0:1, :], upstream)
        add_affine(stage, 0, gain, upstream)
        stage.target_back[rows, :] = grad + stage.first_back[rows, :]
        stage.send.target_back(index)

    blocks_of_tokens(query.shape[0], run)
    width = query.shape[1]
    rows_of = width // 16 * 2
    square_grads(stage, 0, stage.normed_t, query_back, True)
    square_grads(stage, rows_of, stage.normed_t, key_back, False)
    square_grads(stage, 2 * rows_of, stage.normed_t, value_back, False)
    norms = stage.affine_back[...]
    norms = jnp.concatenate([norms, jnp.zeros_like(norms)], 0)
    for inner in range(2):
        low = (norms if inner == 0 else jnp.concatenate([norms[3:], norms[:3]], 0)).astype(BF16)
        for line in range(LINE):
            for result in (stage.keep, stage.send_):
                for outer in range(2):
                    result[outer * 2 + inner, line, 3 * rows_of :, :] = low[:, line * 128 : (line + 1) * 128]


def self_back(coords, window, ins):
    ins_ = types.SimpleNamespace(**ins)
    length, width = ins_.query.shape
    low, turned = ((length, width), BF16), ((width, length), BF16)
    part = ((4, LINE, 3 * width // 8 + AFFINE_ROWS, 128), BF16)
    return staged(
        "self_back", self_back_body, dict(coords=coords, window=window), ins,
        dict(send_=part, keep=part, target_back=Rows(((length, width), F32))),
        dict(
            key_acc=((length, width), F32), value_acc=((length, width), F32), query_back=turned, key_back=low,
            value_back=low, affine_back=((8, width), F32), bias=((BACK_SIZES[-1], SELF_BLOCK), F32),
        ),
        weight=20,
    )


def sums_body(jobs, stage):
    place = 0
    for index, job in enumerate(jobs):
        total = stage[place, index][...].astype(F32)
        for more in range(1, len(job)):
            total = total + stage[place + more, index][...].astype(F32)
        place += len(job)
        stage.outs[index][0][...] = total.astype(BF16)
        stage._send(index)


def sums(coords, jobs):
    ins = {}
    for index, job in enumerate(jobs):
        for part in job:
            ins[len(ins), index] = part
    outs = {index: (job[0].shape, BF16) for index, job in enumerate(jobs)}
    body = functools.partial(sums_body, jobs)
    return list(vars(staged("sums", body, dict(coords=coords), ins, outs, {}, limit=SMALL)).values())


def plane_part(array, step):
    def choose(ref, scalars):
        coords = scalars.coords
        return ref.at[(coords[1] ^ (step >> 1)) * 2 + (coords[3] ^ (step & 1))]

    return Part(array, array.shape[1:], choose)


def line_part(array, step):
    return Part(array, array.shape[1:], lambda ref, scalars: ref.at[(scalars.coords[0] + step) & 3])


ORDER = (1, 2, 3, 0)


def chip_jobs(keep, away):
    return [[plane_part(keep, step), plane_part(away, step)] for step in ORDER]


def plane_jobs(arrays):
    return [[line_part(array, step) for array in arrays] for step in ORDER]


def last_sums_body(hidden, squares, wide, stage):
    def total_of(first):
        parts = [stage[first + place][...].astype(F32) for place in range(4)]
        return parts[0] + parts[1] + (parts[2] + parts[3])

    results = [value[0] for value in stage.outs.values()]
    if hidden:
        total = total_of(0)
        half = total.shape[0] // 2
        rows = half // 8
        for chunk in range(8):
            results[0][:, chunk * 128 : (chunk + 1) * 128] = total[chunk * rows : (chunk + 1) * rows]
        results[1][...] = total[half:].T
        results = results[2:]
    first = 4 if hidden else 0
    for count in squares:
        total = total_of(first)
        first += 4
        for place in range(count):
            for chunk in range(2):
                row = (2 * place + chunk) * 32
                results[place][:, chunk * 128 : (chunk + 1) * 128] = total[row : row + 32]
        results = results[count:]
        if total.shape[0] > count * 64:
            lane = (stage.coords[1] * 2 + stage.coords[2]) * 32 + stage.coords[5]
            norms = pltpu.roll(total[count * 64 : count * 64 + 8], (128 - lane) & 127, 1)
            results[0][...] = norms[:3, :wide]
            results = results[1:]


def last_sums(coords, hidden, squares, wide):
    arrays = [array for group in ([hidden] if hidden else []) + squares for array in group]
    outs = {}
    if hidden:
        rows = hidden[0].shape[0]
        outs[(0,)] = ((rows // 16, 1024), F32)
        outs[(1,)] = ((128, rows // 2), F32)
    counts = []
    for group in squares:
        counts.append(group[0].shape[0] // 64)
        for _ in range(counts[-1]):
            outs[(len(outs),)] = ((32, 256), F32)
        if group[0].shape[0] % 64:
            outs[(len(outs),)] = ((3, wide), F32)
    body = functools.partial(last_sums_body, bool(hidden), counts, wide)
    result = staged("last_sums", body, dict(coords=coords), dict(enumerate(arrays)), outs, {}, limit=SMALL)
    return list(vars(result).values())


SWAP = [(0, 1), (1, 0)]
SHIFTS = [[(i, (i + k) % LINE) for i in range(LINE)] for k in range(LINE)]
CROSS = [[(i, i ^ k) for i in range(4)] for k in range(4)]
PLANE = ("b", "i")


def tie(*values):
    return lax.optimization_barrier(values)


def join(arrays):
    return jnp.concatenate(arrays, 0).reshape(len(arrays), *arrays[0].shape)


def along_line(array):
    return [array] + [lax.ppermute(array, "a", SHIFTS[k]) for k in (1, 2, 3)]


def along_plane(array):
    return [array] + [lax.ppermute(array, PLANE, CROSS[k]) for k in (1, 2, 3)]


def line_pair(array, step):
    return jnp.concatenate([array, lax.ppermute(array, "a", CROSS[step])], 0)


def across_cores(arrays):
    return arrays + [lax.ppermute(array, "c", SWAP) for array in arrays]


def swap_cores(array):
    return lax.ppermute(array, "c", SWAP)


def to_plane(arrays):
    return [lax.ppermute(array, PLANE, CROSS[k]) for array, k in zip(arrays, (1, 2, 3))] + arrays[3:4]


def to_line(arrays):
    return [lax.ppermute(array, "a", SHIFTS[k]) for array, k in zip(arrays, (1, 2, 3))] + arrays[3:4]


def shards(
    target,
    source,
    target_segment,
    source_segment,
    source_keep,
    self_query,
    self_key,
    self_value,
    self_output,
    cross_query,
    cross_key,
    cross_value,
    cross_output,
    expand_weight,
    shrink_weight,
    norm_affine,
    cotangent,
):
    src_length = source.shape[1]
    rest = lax.axis_size("r")
    wide = norm_affine.shape[1]
    a, b, c, r, i = (lax.axis_index(name) for name in "abcri")
    coords = jnp.stack([a, b, c, i, (((a * 2 + b) * 2 + c) * rest + r) * wide, r * wide]).astype(jnp.int32)

    def whole_rows(shard):
        return lax.all_gather(shard, "r", axis=0, tiled=True) if rest > 1 else shard

    shard_one = pack_first(coords, [whole_rows(w) for w in (self_query, self_key, self_value)], norm_affine)
    if rest > 1:
        norms = lax.psum(shard_one[6].astype(F32), "r").astype(BF16)
        shard_one = jnp.concatenate([shard_one[:6], norms[None]], 0)
    x, upstream, sent = target[0], cotangent[0], source[0]
    line_one = along_line(shard_one)
    others = [whole_rows(w) for w in (self_output, cross_query, cross_key, cross_value, cross_output)]
    rest_of = pack_rest(
        others, whole_rows(expand_weight), whole_rows(shrink_weight), target_segment, source_segment, source_keep
    )
    seg, key_seg, window = target_segment, rest_of.key_seg, rest_of.window
    near_one = along_plane(join(line_one))
    pair_two, pair_three = line_pair(rest_of.second, 1), line_pair(rest_of.third, 1)
    near_one[0], pair_two, pair_three = tie(near_one[0], pair_two, pair_three)
    joined_two = line_pair(pair_two, 2).reshape(4, 5, 32, -1)
    halves = (pair_three.reshape(2, 8, 32, -1), lax.ppermute(pair_three, "a", CROSS[2]).reshape(2, 8, 32, -1))
    parts = [jnp.concatenate([half[:, :4] for half in halves], 0), jnp.concatenate([half[:, 4:] for half in halves], 0)]
    pieces_one = across_cores(near_one)
    joined_two, pieces_one = tie(joined_two, pieces_one)
    stage_two = along_plane(joined_two)
    ready, *parts = tie(x, *parts)
    sides = [lax.ppermute(parts[0], "i", SWAP), lax.ppermute(parts[1], "b", SWAP)]
    one = self_forward(coords, window, ready, seg, pieces_one)
    sides[0], sides[1], stage_two[0], one.mixed = tie(*sides, stage_two[0], one.mixed)
    sides = [join([part, side]) for part, side in zip(parts, sides)]
    far = [lax.ppermute(sides[0], "b", SWAP), lax.ppermute(sides[1], "i", SWAP)]
    pieces_two = across_cores([tie(array, one.mixed)[0] for array in stage_two])
    two = cross_forward(coords, window, x, one.mixed, one.affine, sent, seg, key_seg, pieces_two)
    pieces_three = across_cores(
        [sides[0], tie(far[0], two.normed)[0], sides[1], tie(far[1], two.normed)[0]]
    )
    three = feed_forward(coords, two.normed, two.normed_t, two.second, upstream, pieces_three)
    away_three = swap_cores(three.send_)
    four = norm_back(one.affine, two.weight, two.second, three.normed_back, upstream)
    away_three, four.mixed_back = tie(away_three, four.mixed_back)
    chip_three = sums(coords, chip_jobs(three.keep, away_three))
    chip_three, four.mixed_back = tie(chip_three, four.mixed_back)
    plane_three = to_plane(chip_three)
    five = cross_back(
        coords,
        window,
        dict(
            query=two.query, key=two.key, seg=seg, key_seg=key_seg, mixed_t=two.mixed_t, total=two.total,
            value=two.value, mixed_back=four.mixed_back, key_t=two.key_t, weight=two.weight,
            affine=one.affine, affine_before=four.affine_back, first=two.first, second_back=four.second_back,
            mixed1_t=one.mixed_t, normed_t=two.normed2_t, source=sent, out_back=four.out_back,
        ),
        src_length,
    )
    five.send_, plane_three = tie(five.send_, plane_three)
    away_two = swap_cores(five.send_)
    line_three = to_line(sums(coords, plane_jobs(plane_three)))
    away_two, line_three[3] = tie(away_two, line_three[3])
    chip_two = sums(coords, chip_jobs(five.keep, away_two))
    chip_two, five.mixed1_back = tie(chip_two, five.mixed1_back)
    plane_two = to_plane(chip_two)
    six = self_back(
        coords,
        window,
        dict(
            query=one.query, key=one.key, seg=seg, total=one.total,
            value=one.value, mixed_back=five.mixed1_back, mixed_t=one.mixed_t, key_t=one.key_t,
            weight=one.weight, affine=one.affine, affine_before=five.affine_back, target=x,
            first_back=five.first_back, normed_t=one.normed_t,
        ),
    )
    six.send_, plane_two, line_three = tie(six.send_, plane_two, line_three)
    away_one = swap_cores(six.send_)
    tail = sums(coords, chip_jobs(six.keep, away_one) + plane_jobs(plane_two))
    plane_one = to_plane(tail[:4])
    line_two = to_line(tail[4:])
    line_three, line_two[3] = tie(line_three, line_two[3])
    hidden = last_sums(coords, line_three, [], wide)
    plane_one, hidden = tie(plane_one, hidden)
    line_one = to_line(sums(coords, plane_jobs(plane_one)))
    *squares, norms = last_sums(coords, [], [line_two, line_one], wide)
    if rest > 1:
        norms = lax.psum(norms, "r")

    def own_block(spread):
        return lax.psum_scatter(spread, "r", scatter_dimension=0, tiled=True) if rest > 1 else spread

    grads = [own_block(grad) for grad in (*squares[5:], *squares[:5], *hidden)]
    return (three.output[None], six.target_back[None], five.source_back[None], *grads, norms)


def solution(mesh):
    dp, inner = mesh.shape["dp"], mesh.shape["inner"]
    fine = Mesh(mesh.devices.reshape(4, 2, 2, dp // 16, inner), ("a", "b", "c", "r", "i"))
    split = ("a", "b", "c", "r")
    in_specs = (
        P((*split, "i"), None, None),
        P((*split, "i"), None, None),
        P((*split, "i"), None),
        P((*split, "i"), None),
        P((*split, "i"), None),
        P(split, "i"),
        P(split, "i"),
        P(split, "i"),
        P(split, "i"),
        P(split, "i"),
        P(split, "i"),
        P(split, "i"),
        P(split, "i"),
        P(split, "i"),
        P(split, "i"),
        P("i", split),
        P((*split, "i"), None, None),
    )
    out_specs = (
        P((*split, "i"), None, None),
        P((*split, "i"), None, None),
        P((*split, "i"), None, None),
        P(split, "i"),
        P(split, "i"),
        P(split, "i"),
        P(split, "i"),
        P(split, "i"),
        P(split, "i"),
        P(split, "i"),
        P(split, "i"),
        P(split, "i"),
        P(split, "i"),
        P("i", split),
    )
    return jax.shard_map(shards, mesh=fine, in_specs=in_specs, out_specs=out_specs, check_vma=False)
```

```python
import functools
import types

import jax
import jax.numpy as jnp
from jax import lax
from jax.experimental import pallas as pl
from jax.experimental.pallas import tpu as pltpu
from jax.sharding import Mesh
from jax.sharding import PartitionSpec as P

EPS = 1e-05
NEG = -1e30
SCALE = 0.125 * 1.4426950408889634
TOKENS = 256
LINE = 4
SELF_BLOCK = 256
SELF_SIZES = (384, 512, 768, 1024)
BACK_SIZES = (384, 512, 640, 768, 1024)
CROSS_BLOCK = 512
CROSS_SIZES = (128, 256, 384)
MIB = 1024 * 1024
BF16 = jnp.bfloat16
SPACE = pltpu.HBM
LARGE = 64
PAIRS = 4
SMALL = 64
F32 = jnp.float32


def dot(left, right):
    return jnp.dot(left, right, preferred_element_type=F32)


def dot_nt(left, right):
    return lax.dot_general(left, right, (((1,), (1,)), ((), ())), preferred_element_type=F32)


def tile(index, size):
    return pl.ds(pl.multiple_of(index * size, size), size)


class Named:
    def __init__(self, act):
        self._act = act

    def __getattr__(self, name):
        return functools.partial(self._act, name)


class Rows:
    def __init__(self, of):
        self.of = of


class Part:
    def __init__(self, array, shape, choose):
        self.array, self.shape, self.dtype, self.choose = array, shape, array.dtype, choose


class Stage:
    def __init__(self):
        self.scalars, self.own, self.ins, self.outs, self.raw = None, {}, {}, {}, []
        self.waited, self.sent = set(), {}
        self.at, self.send = Named(self._at), Named(self._send)

    def begin(self):
        for _, copies in self.ins.values():
            for copy in copies:
                copy.start()

    def _at(self, name, index):
        buffer, copies = self.ins[name]
        if (name, index) not in self.waited:
            self.waited.add((name, index))
            copies[index].wait()
        return buffer

    def __getitem__(self, name):
        if name in self.own:
            return self.own[name]
        if name in self.outs:
            return self.outs[name][0]
        for index in range(len(self.ins[name][1])):
            self._at(name, index)
        return self.ins[name][0]

    def __getattr__(self, name):
        return self[name]

    def _send(self, name, index=None):
        for place, copy in enumerate(self.outs[name][1]):
            if index in (None, place) and (name, place) not in self.sent:
                self.sent[name, place] = copy
                copy.start()

    def finish(self):
        for name in self.ins:
            self[name]
        for name in self.outs:
            self._send(name)
        for copy in self.sent.values():
            copy.wait()


def staged(name, body, scalars, ins, outs, scratch, raw=None, raw_sems=0, weight=0, limit=LARGE):
    raw = raw or []
    by_rows = [label for group in (ins, outs) for label, value in group.items() if isinstance(value, Rows)]
    ins = {label: value.of if isinstance(value, Rows) else value for label, value in ins.items()}
    outs = {label: value.of if isinstance(value, Rows) else value for label, value in outs.items()}

    def copies_of(label, source, target, sems):
        if label not in by_rows:
            return [pltpu.make_async_copy(source, target, sems.pop())]
        spans = [pl.ds(first, TOKENS) for first in range(0, target.shape[0], TOKENS)]
        return [pltpu.make_async_copy(source.at[span], target.at[span], sems.pop()) for span in spans]

    def count_of(label, shape):
        return shape[0] // TOKENS if label in by_rows else 1

    total = sum(count_of(n, v.shape) for n, v in ins.items()) + sum(count_of(n, v[0]) for n, v in outs.items())
    total += raw_sems

    def kernel(*refs):
        refs = list(refs)

        def take(count):
            head = refs[:count]
            del refs[:count]
            return head

        stage = Stage()
        stage.scalars = types.SimpleNamespace(**dict(zip(scalars, take(len(scalars)))))
        in_refs, stage.raw, out_refs = take(len(ins)), take(len(raw)), take(len(outs))
        in_vmem, out_vmem = take(len(ins)), take(len(outs))
        stage.own = dict(zip(scratch, take(len(scratch))))
        stage.own.update(vars(stage.scalars))
        sem_array = take(1)[0]
        sems = [sem_array.at[place] for place in range(total)]
        for label, source, target in zip(ins, in_refs, in_vmem):
            if isinstance(ins[label], Part):
                source = ins[label].choose(source, stage.scalars)
            stage.ins[label] = (target, copies_of(label, source, target, sems))
        for label, source, target in zip(outs, out_vmem, out_refs):
            stage.outs[label] = (source, copies_of(label, source, target, sems))
        stage.raw_sems = sems
        if not raw:
            stage.begin()
        body(stage)
        stage.finish()

    results = pl.pallas_call(
        kernel,
        out_shape=[jax.ShapeDtypeStruct(*shape) for shape in outs.values()],
        in_specs=[pl.BlockSpec(memory_space=pltpu.SMEM)] * len(scalars)
        + [pl.BlockSpec(memory_space=SPACE)] * (len(ins) + len(raw)),
        out_specs=[pl.BlockSpec(memory_space=SPACE)] * len(outs),
        scratch_shapes=[pltpu.VMEM(array.shape, array.dtype) for array in ins.values()]
        + [pltpu.VMEM(*shape) for shape in outs.values()]
        + [pltpu.VMEM(*shape) for shape in scratch.values()]
        + [pltpu.SemaphoreType.DMA((total,))],
        compiler_params=pltpu.CompilerParams(vmem_limit_bytes=limit * MIB),
        cost_estimate=pl.CostEstimate(
            flops=1000 + weight * 10**9, bytes_accessed=1000 + weight * 3 * 10**6, transcendentals=0
        ),
        name=name,
    )(
        *scalars.values(),
        *[array.array if isinstance(array, Part) else array for array in ins.values()],
        *raw,
    )
    return types.SimpleNamespace(**{str(label): result for label, result in zip(outs, results)})


def place_of(coords, doubled, part, entry):
    core, plane = part // 4, part % 4
    line = coords[0] ^ entry if doubled else (coords[0] - entry) & 3
    outer = coords[1] ^ (plane >> 1)
    inner = coords[3] ^ (plane & 1)
    return (line * 2 + outer) * 2 + (coords[2] ^ core), inner


def piece_copies(stage, pieces, sems, spot, doubled=False):
    copies = []
    for part in range(8):
        for entry in range(4):
            dp, inner = place_of(stage.coords, doubled, part, entry)
            for which, target in spot(dp, inner):
                copies.append(pltpu.make_async_copy(pieces[part].at[entry, which], target, sems[len(copies)]))
    for copy in copies:
        copy.start()
    return copies


def standard(value):
    centre = value - jnp.mean(value, -1, keepdims=True)
    rate = lax.rsqrt(jnp.mean(centre * centre, -1, keepdims=True) + EPS)
    return centre * rate, rate


def standard_back(value, gain, upstream):
    z, rate = standard(value)
    scaled = upstream * gain
    back = rate * (scaled - jnp.mean(scaled, -1, keepdims=True) - z * jnp.mean(scaled * z, -1, keepdims=True))
    return back, upstream * z


def blocks_of_tokens(length, run):
    for index in range(length // TOKENS):
        run(slice(index * TOKENS, (index + 1) * TOKENS), index)


def windowed(sizes, kind, run):
    for place, size in enumerate(sizes):
        pl.when(kind == place)(functools.partial(run, size))


def column_of(row):
    return jnp.broadcast_to(row.astype(F32), (128, row.shape[1])).T[:, :1]


def own_lanes(array, half):
    low = lax.broadcasted_iota(jnp.int32, array.shape, 1) < 64
    zero = jnp.zeros_like(array)
    return jnp.where(low, array, zero) if half == 0 else jnp.where(low, zero, array)


def attend(query, keys_t, values_t, query_seg, key_seg, window, mixed, mixed_t, total, bias, sums_t, sizes, block, first):
    length, width = query.shape
    heads = total.shape[0]
    lane = lax.broadcasted_iota(jnp.int32, (block, 128), 1)

    def one_block(index, carry):
        rows = tile(index, block)
        start = window[first, index]

        def run(size):
            span = pl.ds(pl.multiple_of(start, 128), size)
            bias[:, :size] = jnp.where(column_of(query_seg[:, rows]) == key_seg[:, span].astype(F32), 0.0, NEG)
            ones = jnp.ones((16, size), BF16)

            def one_pair(pair, tops):
                lanes = tile(pair, 128)
                q, k = query[rows, lanes], keys_t[lanes, span]
                for half in range(2):
                    scores = dot(own_lanes(q, half), k) * SCALE + bias[:, :size]
                    top = jnp.max(scores, -1, keepdims=True)
                    expo = jnp.exp2(scores - top).astype(BF16)
                    spot = pl.ds(pl.multiple_of(pair * 128 + half * 64, 64), 64)
                    parts = dot_nt(jnp.concatenate([values_t[spot, span], ones], 0), expo)
                    sums = parts[64:65]
                    mixed_t[spot, rows] = (parts[:64] * (1.0 / sums)).astype(BF16)
                    sums_t[pl.ds(pair * 2 + half, 1), :] = sums
                    tops = jnp.where(lane == pair * 2 + half, top, tops)
                return tops

            tops = lax.fori_loop(0, width // 128, one_pair, jnp.zeros((block, 128), F32), unroll=PAIRS)
            total[:, rows] = tops.T[:heads] + jnp.log2(sums_t[...])

        windowed(sizes, window[first + 1, index], run)
        mixed[rows, :] = mixed_t[:, rows].T
        return carry

    lax.fori_loop(0, length // block, one_block, 0)


def attend_back(query, keys, keys_t, values, back, mixed_t, total, query_seg, key_seg, window, query_back_t, key_acc, value_acc, bias, sizes, block, first):
    length, width = query.shape
    key_acc[...] = jnp.zeros(key_acc.shape, F32)
    value_acc[...] = jnp.zeros(value_acc.shape, F32)

    def one_block(index, carry):
        rows = tile(index, block)
        start = window[first, index]

        def run(size):
            span = pl.ds(pl.multiple_of(start, 128), size)
            bias[:size, :] = jnp.where(column_of(key_seg[:, span]) == query_seg[:, rows].astype(F32), 0.0, NEG)
            low = lax.broadcasted_iota(jnp.int32, (size, 128), 1) < 64

            def one_pair(pair, carried):
                lanes = tile(pair, 128)
                q, k, v, up = query[rows, lanes], keys[span, lanes], values[span, lanes], back[rows, lanes]
                q_t, up_t = q.T, up.T
                product = up_t.astype(F32) * mixed_t[lanes, rows].astype(F32)
                key_parts, value_parts = [], []
                for half in range(2):
                    scores = dot(own_lanes(k, half), q_t) * SCALE + bias[:size, :]
                    probs = jnp.exp2(scores - total[pl.ds(pair * 2 + half, 1), rows])
                    spread = dot(own_lanes(v, half), up_t)
                    delta = jnp.sum(product[half * 64 : half * 64 + 64], 0, keepdims=True)
                    scores_back = (probs * (spread - delta)).astype(BF16)
                    value_parts.append(dot(probs.astype(BF16), up))
                    key_parts.append(dot(scores_back, q))
                    spot = pl.ds(pl.multiple_of(pair * 128 + half * 64, 64), 64)
                    query_back_t[spot, rows] = (dot(keys_t[spot, span], scores_back) * 0.125).astype(BF16)
                value_acc[span, lanes] += jnp.where(low, *value_parts)
                key_acc[span, lanes] += jnp.where(low, *key_parts)
                return carried

            lax.fori_loop(0, width // 128, one_pair, 0, unroll=PAIRS)

        windowed(sizes, window[first + 1, index], run)
        return carry

    lax.fori_loop(0, length // block, one_block, 0)


def put_square(stage, grad, column, base):
    core = stage.coords[2]
    rows = grad.shape[0] // 16
    blocks = grad.astype(BF16).reshape(LINE, 2, 2, rows, grad.shape[1])
    for result, wanted in ((stage.keep, 0), (stage.send_, 1)):
        picked = jnp.where(core == wanted, blocks[:, :, 0], blocks[:, :, 1])
        for outer in range(2):
            for chunk in range(2):
                result[outer * 2 + column, :, base + chunk * rows : base + (chunk + 1) * rows, :] = picked[
                    :, outer, :, chunk * 128 : (chunk + 1) * 128
                ]


def self_forward_body(stage):
    affine, loose, weight = stage.affine, stage.loose, stage.weight
    copies = piece_copies(
        stage, stage.raw, stage.raw_sems, lambda dp, inner: [(slice(0, 7), loose.at[:, dp, :, tile(inner, 256)])]
    )
    stage.begin()
    for copy in copies:
        copy.wait()
    for w in range(3):
        for dp in range(16):
            for half in range(2):
                weight[w, dp * 32 + half * 16 : dp * 32 + half * 16 + 16, :] = loose[2 * w + half, dp]
    flat = jnp.sum(loose[6].astype(F32), 0)
    flat = flat[:, :256] + flat[:, 256:]
    affine[:, :256] = flat[:8]
    affine[:, 256:] = flat[8:]
    stage.send.weight()
    stage.send.affine()
    normed_t = stage.normed_t
    length = normed_t.shape[1]

    def project(rows, index):
        z, _ = standard(stage.at.target(index)[rows, :].astype(F32))
        n = (z * affine[0:1, :] + affine[1:2, :]).astype(BF16)
        normed_t[:, rows] = n.T
        query, key, value = (dot(n, weight[place]).astype(BF16) for place in range(3))
        stage.query[rows, :] = query
        stage.key[rows, :] = key
        stage.value[rows, :] = value
        stage.send.query(index)
        stage.send.key(index)
        stage.send.value(index)
        stage.key_t[:, rows] = key.T
        stage.value_t[:, rows] = value.T

    blocks_of_tokens(length, project)
    stage.send.normed_t()
    stage.send.key_t()
    attend(
        stage.query, stage.key_t, stage.value_t, stage.seg, stage.seg, stage.window, stage.mixed, stage.mixed_t,
        stage.total, stage.bias, stage.sums_t, SELF_SIZES, SELF_BLOCK, 0,
    )


def self_forward(coords, window, target, seg, pieces):
    length, width = target.shape
    low, turned = ((length, width), BF16), ((width, length), BF16)
    return staged(
        "self_forward", self_forward_body, dict(coords=coords, window=window), dict(target=Rows(target), seg=seg),
        dict(
            weight=((3, width, width), BF16), affine=((8, width), F32), query=Rows(low), key=Rows(low),
            value=Rows(low), key_t=turned, normed_t=turned, mixed=low, mixed_t=turned,
            total=((width // 64, length), F32),
        ),
        dict(
            loose=((7, 16, 16, width), BF16), value_t=turned, bias=((SELF_BLOCK, SELF_SIZES[-1]), F32),
            sums_t=((width // 64, SELF_BLOCK), F32),
        ),
        raw=pieces, raw_sems=32,
        weight=20,
    )


def cross_forward_body(stage):
    weight = stage.weight
    copies = piece_copies(
        stage,
        stage.raw,
        stage.raw_sems,
        lambda dp, inner: [(slice(0, 5), weight.at[:, tile(dp, 32), tile(inner, 256)])],
        doubled=True,
    )
    stage.begin()
    for copy in copies:
        copy.wait()
    stage.send.weight()
    source, affine = stage.source, stage.affine
    first = stage.first
    length = first.shape[0]
    padded = stage.padded
    count = source.shape[0]
    padded[...] = jnp.zeros(padded.shape, BF16)
    padded[:count, :] = source[...]
    stage.key[...] = dot(padded[...], weight[2]).astype(BF16)
    stage.value[...] = dot(padded[...], weight[3]).astype(BF16)
    stage.key_t[...] = stage.key[...].T
    stage.value_t[...] = stage.value[...].T
    stage.send.key()
    stage.send.key_t()
    stage.send.value()

    def project(rows, index):
        v = stage.at.target(index)[rows, :].astype(F32) + dot(stage.at.mixed1(index)[rows, :], weight[0])
        first[rows, :] = v
        stage.send.first(index)
        z, _ = standard(v)
        n = (z * affine[2:3, :] + affine[3:4, :]).astype(BF16)
        stage.normed2_t[:, rows] = n.T
        stage.query[rows, :] = dot(n, weight[1]).astype(BF16)
        stage.send.query(index)

    blocks_of_tokens(length, project)
    stage.send.normed2_t()
    attend(
        stage.query, stage.key_t, stage.value_t, stage.seg, stage.key_seg, stage.window, stage.mixed,
        stage.mixed_t, stage.total, stage.bias, stage.sums_t, CROSS_SIZES, CROSS_BLOCK, 2,
    )
    stage.send.mixed_t()
    stage.send.total()

    def finish(rows, index):
        m = stage.mixed[rows, :]
        v = first[rows, :] + dot(m, weight[4])
        stage.second[rows, :] = v
        z, _ = standard(v)
        n = (z * affine[4:5, :] + affine[5:6, :]).astype(BF16)
        stage.normed[rows, :] = n
        stage.normed_t[:, rows] = n.T
        stage.send.second(index)
        stage.send.normed(index)

    blocks_of_tokens(length, finish)


def cross_forward(coords, window, target, mixed1, affine, source, seg, key_seg, pieces):
    length, width = target.shape
    count = key_seg.shape[1]
    low, turned, full = ((length, width), BF16), ((width, length), BF16), ((length, width), F32)
    return staged(
        "cross_forward", cross_forward_body, dict(coords=coords, window=window),
        dict(
            mixed1=Rows(mixed1), target=Rows(target), affine=affine, source=source, seg=seg, key_seg=key_seg
        ),
        dict(
            weight=((5, width, width), BF16), key=((count, width), BF16), key_t=((width, count), BF16), value=((count, width), BF16),
            first=Rows(full), normed2_t=turned, query=Rows(low), mixed_t=turned,
            total=((width // 64, length), F32), second=Rows(full), normed=Rows(low), normed_t=turned,
        ),
        dict(
            bias=((CROSS_BLOCK, CROSS_SIZES[-1]), F32), sums_t=((width // 64, CROSS_BLOCK), F32),
            value_t=((width, count), BF16), mixed=low, padded=((count, width), BF16),
        ),
        raw=pieces, raw_sems=32,
        weight=20,
    )


FF_BLOCK = 256
FF_TOKENS = 512


def feed_forward_body(stage):
    expand, shrink, active, hidden_back = stage.expand, stage.shrink, stage.active, stage.hidden_back
    loose_expand, loose_shrink = stage.loose_expand, stage.loose_shrink
    coords, copies = stage.coords, []
    for part in range(8):
        core, kind = part // 4, part % 4
        for entry in range(8):
            first, line = entry // 4, coords[0] ^ (entry % 4)
            outer, inner = (kind, first) if kind < 2 else (first, kind - 2)
            outer, inner = coords[1] ^ outer, coords[3] ^ inner
            dp = (line * 2 + outer) * 2 + (coords[2] ^ core)
            if kind < 2:
                spot = loose_expand.at[tile(inner, 4), tile(dp, 32), :]
            else:
                spot = loose_shrink.at[inner, tile(dp, 4)]
            source = stage.raw[part].at[first, entry % 4]
            copies.append(pltpu.make_async_copy(source, spot, stage.raw_sems[len(copies)]))
            copies[-1].start()
    stage.begin()
    core = coords[2]
    width, hidden = expand.shape
    for copy in copies:
        copy.wait()
    for part in range(hidden // FF_BLOCK):
        expand[:, part * FF_BLOCK : (part + 1) * FF_BLOCK] = loose_expand[part]
    for side in range(2):
        shrink[:, side * width // 2 : (side + 1) * width // 2] = loose_shrink[side].reshape(hidden, width // 2)
    normed, back = stage.normed, stage.back
    normed_t, back_t = stage.normed_t, stage.back_t
    length = normed.shape[0]
    back_t[...] = back[...].T

    def one_part(part):
        lanes = slice(part * FF_BLOCK, (part + 1) * FF_BLOCK)
        for index in range(length // FF_TOKENS):
            rows = slice(index * FF_TOKENS, (index + 1) * FF_TOKENS)
            v = dot(normed[rows, :], expand[:, lanes])
            up = dot_nt(back[rows, :], shrink[lanes, :])
            square = v * v
            half = 0.5 + 0.5 * jnp.tanh(v * (0.7978845608028654 + 0.035677408136300125 * square))
            value = v * half
            slope = half + value * (1.0 - half) * (1.5957691216057308 + 0.21406444881780075 * square)
            active[rows, lanes] = value.astype(BF16)
            hidden_back[rows, lanes] = (up * slope).astype(BF16)
        grad = dot(normed_t[...], hidden_back[:, lanes]).astype(BF16)
        blocks = grad.reshape(LINE, 2, 2, width // 16, FF_BLOCK)
        inner, chunk = part // 4, part % 4 * 2
        for result, wanted in ((stage.keep, 0), (stage.send_, 1)):
            picked = jnp.where(core == wanted, blocks[:, :, 0], blocks[:, :, 1])
            for outer in range(2):
                for side in range(2):
                    first = (chunk + side) * width // 16
                    result[outer * 2 + inner, :, first : first + width // 16, :] = picked[
                        :, outer, :, side * 128 : (side + 1) * 128
                    ]
        grad = dot(back_t[...], active[:, lanes]).astype(BF16)
        line, outer = part // 2, part % 2
        for result, wanted in ((stage.keep, 0), (stage.send_, 1)):
            picked = jnp.where(core == wanted, grad[:, :128], grad[:, 128:])
            for side in range(2):
                result[outer * 2 + side, line, width // 2 :, :] = picked[side * width // 2 : (side + 1) * width // 2]

    for part in range(hidden // FF_BLOCK):
        one_part(part)
    stage.send.send_()
    stage.send.keep()

    def finish(rows, index):
        stage.normed_back[rows, :] = dot_nt(hidden_back[rows, :], expand[...])
        stage.send.normed_back(index)
        stage.output[rows, :] = (stage.at.second(index)[rows, :] + dot(active[rows, :], shrink[...])).astype(BF16)
        stage.send.output(index)

    blocks_of_tokens(length, finish)


def feed_forward(coords, normed, normed_t, second, back, pieces):
    length, width = normed.shape
    hidden = 4 * width
    part = ((4, LINE, width, 128), BF16)
    wide = ((length, hidden), BF16)
    return staged(
        "feed_forward", feed_forward_body, dict(coords=coords),
        dict(normed=normed, back=back, normed_t=normed_t, second=Rows(second)),
        dict(
            send_=part, keep=part, normed_back=Rows(((length, width), F32)), output=Rows(((length, width), BF16))
        ),
        dict(
            loose_expand=((hidden // FF_BLOCK, width, FF_BLOCK), BF16),
            loose_shrink=((2, hidden // 32, 32, width // 2), BF16),
            expand=((width, hidden), BF16), shrink=((hidden, width), BF16), active=wide, hidden_back=wide,
            back_t=((width, length), BF16),
        ),
        raw=pieces, raw_sems=64,
        weight=20,
    )


def add_affine(stage, row, gain, bias):
    stage.affine_back[row : row + 1, :] += jnp.sum(gain, 0, keepdims=True)
    stage.affine_back[row + 1 : row + 2, :] += jnp.sum(bias, 0, keepdims=True)


def norm_back_body(stage):
    affine = stage.affine
    stage.affine_back[...] = jnp.zeros(stage.affine_back.shape, F32)

    def run(rows, index):
        upstream = stage.at.normed_back(index)[rows, :]
        grad, gain = standard_back(stage.at.second(index)[rows, :], affine[4:5, :], upstream)
        add_affine(stage, 4, gain, upstream)
        grad = grad + stage.at.back(index)[rows, :].astype(F32)
        stage.second_back[rows, :] = grad
        stage.mixed_back[rows, :] = dot_nt(grad.astype(BF16), stage.weight[...]).astype(BF16)
        stage.send.second_back(index)
        stage.send.mixed_back(index)

    blocks_of_tokens(stage.second_back.shape[0], run)


def norm_back(affine, weight, second, normed_back, back):
    length, width = second.shape
    low, full = ((length, width), BF16), ((length, width), F32)
    return staged(
        "norm_back", norm_back_body, {},
        dict(
            affine=affine, normed_back=Rows(normed_back), second=Rows(second), back=Rows(back),
            weight=Part(weight, (width, width), lambda ref, scalars: ref.at[4]),
        ),
        dict(affine_back=((8, width), F32), mixed_back=Rows(low), second_back=Rows(full)),
        {},
        weight=3,
    )


def square_grads(stage, base, left_t, right, turned):
    for column in range(2):
        cols = slice(column * 256, (column + 1) * 256)
        grad = dot_nt(left_t[...], right[cols, :]) if turned else dot(left_t[...], right[:, cols])
        put_square(stage, grad, column, base)


def cross_back_body(stage):
    query = stage.query
    key_acc, value_acc, query_back = stage.key_acc, stage.value_acc, stage.query_back
    attend_back(
        query, stage.key, stage.key_t, stage.value, stage.mixed_back, stage.mixed_t, stage.total, stage.seg,
        stage.key_seg, stage.window, query_back, key_acc, value_acc, stage.bias, CROSS_SIZES, CROSS_BLOCK, 2,
    )
    affine, weight, key_back, value_back = stage.affine, stage.weight, stage.key_back, stage.value_back
    key_back[...] = (key_acc[...] * 0.125).astype(BF16)
    value_back[...] = value_acc[...].astype(BF16)
    source_back = dot_nt(key_back[...], weight[2]) + dot_nt(value_back[...], weight[3])
    stage.source_back[...] = source_back[: stage.source_back.shape[0]]
    stage.send.source_back()
    stage.affine_back[...] = stage.affine_before[...]
    first_low = stage.first_low

    def run(rows, index):
        upstream = dot(weight[1], query_back[:, rows]).T
        grad, gain = standard_back(stage.first[rows, :], affine[2:3, :], upstream)
        add_affine(stage, 2, gain, upstream)
        second_back = stage.second_back[rows, :]
        stage.out_low[rows, :] = second_back.astype(BF16)
        grad = grad + second_back
        stage.first_back[rows, :] = grad
        low = grad.astype(BF16)
        first_low[rows, :] = low
        stage.mixed1_back[rows, :] = dot_nt(low, weight[0]).astype(BF16)

    blocks_of_tokens(query.shape[0], run)
    stage.send.first_back()
    stage.send.mixed1_back()
    stage.send.affine_back()
    rows_of = weight.shape[1] // 16 * 2
    square_grads(stage, 0, stage.mixed1_t, first_low, False)
    square_grads(stage, rows_of, stage.normed_t, query_back, True)
    padded, source_t = stage.padded, stage.source_t
    padded[...] = jnp.zeros(padded.shape, BF16)
    padded[: stage.source.shape[0], :] = stage.source[...]
    source_t[...] = padded[...].T
    square_grads(stage, 2 * rows_of, source_t, key_back, False)
    square_grads(stage, 3 * rows_of, source_t, value_back, False)
    square_grads(stage, 4 * rows_of, stage.mixed_t, stage.out_low, False)


def cross_back(coords, window, ins, source_length):
    ins_ = types.SimpleNamespace(**ins)
    length, width = ins_.query.shape
    count = ins_.key.shape[0]
    low, full = ((length, width), BF16), ((length, width), F32)
    keyed = (count, width)
    part = ((4, LINE, 5 * width // 8, 128), BF16)
    return staged(
        "cross_back", cross_back_body, dict(coords=coords, window=window), ins,
        dict(
            keep=part, send_=part, first_back=full, mixed1_back=low, affine_back=((8, width), F32),
            source_back=((source_length, width), F32),
        ),
        dict(
            key_acc=(keyed, F32), value_acc=(keyed, F32), query_back=((width, length), BF16), first_low=low, out_low=low,
            key_back=(keyed, BF16), value_back=(keyed, BF16), bias=((CROSS_SIZES[-1], CROSS_BLOCK), F32),
            padded=(keyed, BF16), source_t=((width, count), BF16),
        ),
        weight=20,
    )


AFFINE_ROWS = 16


def pack_first_body(wide, stage):
    for place in range(3):
        for half in range(2):
            stage.packed[2 * place + half] = stage[place][half * 16 : half * 16 + 16, :]
    coords = stage.coords
    own = stage.norms[...]
    width = 2 * stage.packed.shape[2]
    row_at, from_row = (lax.broadcasted_iota(jnp.int32, (8, own.shape[0]), axis) for axis in range(2))
    from_lane, lane_at = (lax.broadcasted_iota(jnp.int32, (wide, width), axis) for axis in range(2))
    down = (row_at == coords[3] * 3 + from_row).astype(BF16)
    right = (lane_at == coords[4] + from_lane).astype(BF16)
    placed = dot(down, dot(own, right).astype(BF16)).astype(BF16)
    stage.packed[6] = jnp.concatenate([placed[:, : width // 2], placed[:, width // 2 :]], 0)


def pack_first(coords, weights, norms):
    ins = {**dict(enumerate(weights)), **dict(norms=norms)}
    outs = dict(packed=((7, 16, weights[0].shape[1]), BF16))
    body = functools.partial(pack_first_body, norms.shape[1])
    return staged("pack", body, dict(coords=coords), ins, outs, {}, limit=SMALL).packed


def join_pairs_body(stage):
    for place in range(4):
        result = stage.one if place < 2 else stage.two
        result[place % 2] = stage[place][...]
        if place == 1:
            stage.send.one()


def join_pairs(one, two):
    shape = (2, *one[0].shape)
    outs = dict(one=(shape, BF16), two=(shape, BF16))
    result = staged("join", join_pairs_body, {}, dict(enumerate([*one, *two])), outs, {}, limit=SMALL)
    return [result.one, result.two]


def find_windows(seg, keys, sizes, block, count):
    lane = lax.broadcasted_iota(jnp.int32, (1, 128), 1)
    starts, kinds = jnp.zeros((1, 128), jnp.int32), jnp.zeros((1, 128), jnp.int32)
    for index in range(seg.shape[1] // block):
        first, last = seg[:, index * block : index * block + 1], seg[:, (index + 1) * block - 1 : (index + 1) * block]
        low = jnp.sum((keys < first).astype(F32), 1, keepdims=True).astype(jnp.int32) // 128 * 128
        high = (jnp.sum((keys <= last).astype(F32), 1, keepdims=True).astype(jnp.int32) + 127) // 128 * 128
        need = high - low
        kind = sum(((need > size).astype(jnp.int32) for size in sizes[:-1]), jnp.zeros_like(need))
        size = sum((jnp.where(kind == place, size, 0) for place, size in enumerate(sizes)), jnp.zeros_like(need))
        starts = jnp.where(lane == index, jnp.minimum(low, count - size), starts)
        kinds = jnp.where(lane == index, kind, kinds)
    return starts, kinds


def pack_rest_body(stage):
    for place in range(5):
        stage.second[place] = stage[place][...]
    for place in range(4):
        stage.third[place] = stage.expand[:, place * 256 : place * 256 + 256]
        stage.third[4 + place] = stage.shrink[place * 32 : place * 32 + 32, :]
    seg, source_seg = stage.seg[...], stage.source_seg[...]
    count = stage.key_seg.shape[1]
    stage.key_seg[...] = jnp.full(stage.key_seg.shape, -1, jnp.int32)
    stage.key_seg[:, : source_seg.shape[1]] = jnp.where(stage.source_keep[...] > 0, source_seg, -1)
    rows = (
        *find_windows(seg, seg, SELF_SIZES, SELF_BLOCK, seg.shape[1]),
        *find_windows(seg, source_seg, CROSS_SIZES, CROSS_BLOCK, count),
        *find_windows(seg, seg, BACK_SIZES, SELF_BLOCK, seg.shape[1]),
    )
    stage.window[...] = jnp.zeros(stage.window.shape, jnp.int32)
    for place, row in enumerate(rows):
        stage.window[place : place + 1, :] = row


def pack_rest(weights, expand, shrink, seg, source_seg, source_keep):
    ins = {
        **dict(enumerate(weights)),
        **dict(expand=expand, shrink=shrink, seg=seg, source_seg=source_seg, source_keep=source_keep),
    }
    outs = dict(
        second=((5, 32, 256), BF16), third=((8, 32, 256), BF16), window=((8, 128), jnp.int32),
        key_seg=((1, CROSS_SIZES[-1]), jnp.int32),
    )
    return staged("pack", pack_rest_body, {}, ins, outs, {})


def self_back_body(stage):
    query = stage.query
    key_acc, value_acc, query_back = stage.key_acc, stage.value_acc, stage.query_back
    attend_back(
        query, stage.key, stage.key_t, stage.value, stage.mixed_back, stage.mixed_t, stage.total, stage.seg,
        stage.seg, stage.window, query_back, key_acc, value_acc, stage.bias, BACK_SIZES, SELF_BLOCK, 4,
    )
    weight, affine = stage.weight, stage.affine
    key_back, value_back = stage.key_back, stage.value_back
    key_back[...] = (key_acc[...] * 0.125).astype(BF16)
    value_back[...] = value_acc[...].astype(BF16)
    stage.affine_back[...] = stage.affine_before[...]

    def run(rows, index):
        upstream = dot_nt(key_back[rows, :], weight[1]) + dot_nt(value_back[rows, :], weight[2])
        upstream = upstream + dot(weight[0], query_back[:, rows]).T
        grad, gain = standard_back(stage.target[rows, :].astype(F32), affine[0:1, :], upstream)
        add_affine(stage, 0, gain, upstream)
        stage.target_back[rows, :] = grad + stage.first_back[rows, :]
        stage.send.target_back(index)

    blocks_of_tokens(query.shape[0], run)
    width = query.shape[1]
    rows_of = width // 16 * 2
    square_grads(stage, 0, stage.normed_t, query_back, True)
    square_grads(stage, rows_of, stage.normed_t, key_back, False)
    square_grads(stage, 2 * rows_of, stage.normed_t, value_back, False)
    norms = stage.affine_back[...]
    norms = jnp.concatenate([norms, jnp.zeros_like(norms)], 0)
    for inner in range(2):
        low = (norms if inner == 0 else jnp.concatenate([norms[3:], norms[:3]], 0)).astype(BF16)
        for line in range(LINE):
            for result in (stage.keep, stage.send_):
                for outer in range(2):
                    result[outer * 2 + inner, line, 3 * rows_of :, :] = low[:, line * 128 : (line + 1) * 128]


def self_back(coords, window, ins):
    ins_ = types.SimpleNamespace(**ins)
    length, width = ins_.query.shape
    low, turned = ((length, width), BF16), ((width, length), BF16)
    part = ((4, LINE, 3 * width // 8 + AFFINE_ROWS, 128), BF16)
    return staged(
        "self_back", self_back_body, dict(coords=coords, window=window), ins,
        dict(send_=part, keep=part, target_back=Rows(((length, width), F32))),
        dict(
            key_acc=((length, width), F32), value_acc=((length, width), F32), query_back=turned, key_back=low,
            value_back=low, affine_back=((8, width), F32), bias=((BACK_SIZES[-1], SELF_BLOCK), F32),
        ),
        weight=20,
    )


def sums_body(jobs, stage):
    place = 0
    for index, job in enumerate(jobs):
        total = stage[place, index][...].astype(F32)
        for more in range(1, len(job)):
            total = total + stage[place + more, index][...].astype(F32)
        place += len(job)
        stage.outs[index][0][...] = total.astype(BF16)
        stage._send(index)


def sums(coords, jobs):
    ins = {}
    for index, job in enumerate(jobs):
        for part in job:
            ins[len(ins), index] = part
    outs = {index: (job[0].shape, BF16) for index, job in enumerate(jobs)}
    body = functools.partial(sums_body, jobs)
    return list(vars(staged("sums", body, dict(coords=coords), ins, outs, {}, limit=SMALL)).values())


def plane_part(array, step):
    def choose(ref, scalars):
        coords = scalars.coords
        return ref.at[(coords[1] ^ (step >> 1)) * 2 + (coords[3] ^ (step & 1))]

    return Part(array, array.shape[1:], choose)


def line_part(array, step):
    return Part(array, array.shape[1:], lambda ref, scalars: ref.at[(scalars.coords[0] + step) & 3])


ORDER = (1, 2, 3, 0)


def chip_jobs(keep, away):
    return [[plane_part(keep, step), plane_part(away, step)] for step in ORDER]


def plane_jobs(arrays):
    return [[line_part(array, step) for array in arrays] for step in ORDER]


def last_sums_body(hidden, squares, wide, stage):
    def total_of(first):
        parts = [stage[first + place][...].astype(F32) for place in range(4)]
        return parts[0] + parts[1] + (parts[2] + parts[3])

    results = [value[0] for value in stage.outs.values()]
    if hidden:
        total = total_of(0)
        half = total.shape[0] // 2
        rows = half // 8
        for chunk in range(8):
            results[0][:, chunk * 128 : (chunk + 1) * 128] = total[chunk * rows : (chunk + 1) * rows]
        results[1][...] = total[half:].T
        results = results[2:]
    first = 4 if hidden else 0
    for count in squares:
        total = total_of(first)
        first += 4
        for place in range(count):
            for chunk in range(2):
                row = (2 * place + chunk) * 32
                results[place][:, chunk * 128 : (chunk + 1) * 128] = total[row : row + 32]
        results = results[count:]
        if total.shape[0] > count * 64:
            lane = (stage.coords[1] * 2 + stage.coords[2]) * 32 + stage.coords[5]
            norms = pltpu.roll(total[count * 64 : count * 64 + 8], (128 - lane) & 127, 1)
            results[0][...] = norms[:3, :wide]
            results = results[1:]


def last_sums(coords, hidden, squares, wide):
    arrays = [array for group in ([hidden] if hidden else []) + squares for array in group]
    outs = {}
    if hidden:
        rows = hidden[0].shape[0]
        outs[(0,)] = ((rows // 16, 1024), F32)
        outs[(1,)] = ((128, rows // 2), F32)
    counts = []
    for group in squares:
        counts.append(group[0].shape[0] // 64)
        for _ in range(counts[-1]):
            outs[(len(outs),)] = ((32, 256), F32)
        if group[0].shape[0] % 64:
            outs[(len(outs),)] = ((3, wide), F32)
    body = functools.partial(last_sums_body, bool(hidden), counts, wide)
    result = staged("last_sums", body, dict(coords=coords), dict(enumerate(arrays)), outs, {}, limit=SMALL)
    return list(vars(result).values())


SWAP = [(0, 1), (1, 0)]
SHIFTS = [[(i, (i + k) % LINE) for i in range(LINE)] for k in range(LINE)]
CROSS = [[(i, i ^ k) for i in range(4)] for k in range(4)]
PLANE = ("b", "i")


def tie(*values):
    return lax.optimization_barrier(values)


def join(arrays):
    return jnp.concatenate(arrays, 0).reshape(len(arrays), *arrays[0].shape)


def along_line(array):
    return [array] + [lax.ppermute(array, "a", SHIFTS[k]) for k in (1, 2, 3)]


def along_plane(array):
    return [array] + [lax.ppermute(array, PLANE, CROSS[k]) for k in (1, 2, 3)]


def line_pair(array, step):
    return jnp.concatenate([array, lax.ppermute(array, "a", CROSS[step])], 0)


def across_cores(arrays):
    return arrays + [lax.ppermute(array, "c", SWAP) for array in arrays]


def swap_cores(array):
    return lax.ppermute(array, "c", SWAP)


def to_plane(arrays):
    return [lax.ppermute(array, PLANE, CROSS[k]) for array, k in zip(arrays, (1, 2, 3))] + arrays[3:4]


def to_line(arrays):
    return [lax.ppermute(array, "a", SHIFTS[k]) for array, k in zip(arrays, (1, 2, 3))] + arrays[3:4]


def shards(
    target,
    source,
    target_segment,
    source_segment,
    source_keep,
    self_query,
    self_key,
    self_value,
    self_output,
    cross_query,
    cross_key,
    cross_value,
    cross_output,
    expand_weight,
    shrink_weight,
    norm_affine,
    cotangent,
):
    src_length = source.shape[1]
    rest = lax.axis_size("r")
    wide = norm_affine.shape[1]
    a, b, c, r, i = (lax.axis_index(name) for name in "abcri")
    coords = jnp.stack([a, b, c, i, (((a * 2 + b) * 2 + c) * rest + r) * wide, r * wide]).astype(jnp.int32)

    def whole_rows(shard):
        return lax.all_gather(shard, "r", axis=0, tiled=True) if rest > 1 else shard

    shard_one = pack_first(coords, [whole_rows(w) for w in (self_query, self_key, self_value)], norm_affine)
    if rest > 1:
        norms = lax.psum(shard_one[6].astype(F32), "r").astype(BF16)
        shard_one = jnp.concatenate([shard_one[:6], norms[None]], 0)
    x, upstream, sent = target[0], cotangent[0], source[0]
    line_one = along_line(shard_one)
    others = [whole_rows(w) for w in (self_output, cross_query, cross_key, cross_value, cross_output)]
    rest_of = pack_rest(
        others, whole_rows(expand_weight), whole_rows(shrink_weight), target_segment, source_segment, source_keep
    )
    seg, key_seg, window = target_segment, rest_of.key_seg, rest_of.window
    near_one = along_plane(join(line_one))
    pair_two, pair_three = line_pair(rest_of.second, 1), line_pair(rest_of.third, 1)
    near_one[0], pair_two, pair_three = tie(near_one[0], pair_two, pair_three)
    joined_two = line_pair(pair_two, 2).reshape(4, 5, 32, -1)
    halves = (pair_three.reshape(2, 8, 32, -1), lax.ppermute(pair_three, "a", CROSS[2]).reshape(2, 8, 32, -1))
    parts = [jnp.concatenate([half[:, :4] for half in halves], 0), jnp.concatenate([half[:, 4:] for half in halves], 0)]
    pieces_one = across_cores(near_one)
    joined_two, pieces_one = tie(joined_two, pieces_one)
    stage_two = along_plane(joined_two)
    ready, *parts = tie(x, *parts)
    sides = [lax.ppermute(parts[0], "i", SWAP), lax.ppermute(parts[1], "b", SWAP)]
    one = self_forward(coords, window, ready, seg, pieces_one)
    sides[0], sides[1], stage_two[0], one.mixed = tie(*sides, stage_two[0], one.mixed)
    sides = join_pairs(*zip(parts, sides))
    far = [lax.ppermute(sides[0], "b", SWAP), lax.ppermute(sides[1], "i", SWAP)]
    pieces_two = across_cores([tie(array, one.mixed)[0] for array in stage_two])
    two = cross_forward(coords, window, x, one.mixed, one.affine, sent, seg, key_seg, pieces_two)
    pieces_three = across_cores(
        [sides[0], tie(far[0], two.normed)[0], sides[1], tie(far[1], two.normed)[0]]
    )
    three = feed_forward(coords, two.normed, two.normed_t, two.second, upstream, pieces_three)
    away_three = swap_cores(three.send_)
    four = norm_back(one.affine, two.weight, two.second, three.normed_back, upstream)
    away_three, four.mixed_back = tie(away_three, four.mixed_back)
    chip_three = sums(coords, chip_jobs(three.keep, away_three))
    chip_three, four.mixed_back = tie(chip_three, four.mixed_back)
    plane_three = to_plane(chip_three)
    five = cross_back(
        coords,
        window,
        dict(
            query=two.query, key=two.key, seg=seg, key_seg=key_seg, mixed_t=two.mixed_t, total=two.total,
            value=two.value, mixed_back=four.mixed_back, key_t=two.key_t, weight=two.weight,
            affine=one.affine, affine_before=four.affine_back, first=two.first, second_back=four.second_back,
            mixed1_t=one.mixed_t, normed_t=two.normed2_t, source=sent,
        ),
        src_length,
    )
    five.send_, plane_three = tie(five.send_, plane_three)
    away_two = swap_cores(five.send_)
    line_three = to_line(sums(coords, plane_jobs(plane_three)))
    away_two, line_three[3] = tie(away_two, line_three[3])
    chip_two = sums(coords, chip_jobs(five.keep, away_two))
    chip_two, five.mixed1_back = tie(chip_two, five.mixed1_back)
    plane_two = to_plane(chip_two)
    six = self_back(
        coords,
        window,
        dict(
            query=one.query, key=one.key, seg=seg, total=one.total,
            value=one.value, mixed_back=five.mixed1_back, mixed_t=one.mixed_t, key_t=one.key_t,
            weight=one.weight, affine=one.affine, affine_before=five.affine_back, target=x,
            first_back=five.first_back, normed_t=one.normed_t,
        ),
    )
    six.send_, plane_two, line_three = tie(six.send_, plane_two, line_three)
    away_one = swap_cores(six.send_)
    tail = sums(coords, chip_jobs(six.keep, away_one) + plane_jobs(plane_two))
    plane_one = to_plane(tail[:4])
    line_two = to_line(tail[4:])
    line_three, line_two[3] = tie(line_three, line_two[3])
    hidden = last_sums(coords, line_three, [], wide)
    plane_one, hidden = tie(plane_one, hidden)
    line_one = to_line(sums(coords, plane_jobs(plane_one)))
    *squares, norms = last_sums(coords, [], [line_two, line_one], wide)
    if rest > 1:
        norms = lax.psum(norms, "r")

    def own_block(spread):
        return lax.psum_scatter(spread, "r", scatter_dimension=0, tiled=True) if rest > 1 else spread

    grads = [own_block(grad) for grad in (*squares[5:], *squares[:5], *hidden)]
    return (three.output[None], six.target_back[None], five.source_back[None], *grads, norms)


def solution(mesh):
    dp, inner = mesh.shape["dp"], mesh.shape["inner"]
    fine = Mesh(mesh.devices.reshape(4, 2, 2, dp // 16, inner), ("a", "b", "c", "r", "i"))
    split = ("a", "b", "c", "r")
    in_specs = (
        P((*split, "i"), None, None),
        P((*split, "i"), None, None),
        P((*split, "i"), None),
        P((*split, "i"), None),
        P((*split, "i"), None),
        P(split, "i"),
        P(split, "i"),
        P(split, "i"),
        P(split, "i"),
        P(split, "i"),
        P(split, "i"),
        P(split, "i"),
        P(split, "i"),
        P(split, "i"),
        P(split, "i"),
        P("i", split),
        P((*split, "i"), None, None),
    )
    out_specs = (
        P((*split, "i"), None, None),
        P((*split, "i"), None, None),
        P((*split, "i"), None, None),
        P(split, "i"),
        P(split, "i"),
        P(split, "i"),
        P(split, "i"),
        P(split, "i"),
        P(split, "i"),
        P(split, "i"),
        P(split, "i"),
        P(split, "i"),
        P(split, "i"),
        P("i", split),
    )
    return jax.shard_map(shards, mesh=fine, in_specs=in_specs, out_specs=out_specs, check_vma=False)
```

```python
import functools
import types

import jax
import jax.numpy as jnp
from jax import lax
from jax.experimental import pallas as pl
from jax.experimental.pallas import tpu as pltpu
from jax.sharding import Mesh
from jax.sharding import PartitionSpec as P

EPS = 1e-05
NEG = -1e30
SCALE = 0.125 * 1.4426950408889634
TOKENS = 256
LINE = 4
SELF_BLOCK = 256
SELF_SIZES = (384, 512, 768, 1024)
BACK_SIZES = (384, 512, 768, 1024)
CROSS_BLOCK = 256
CROSS_BACK_BLOCK = 512
CROSS_BACK_SIZES = (256, 384)
CROSS_SIZES = (128, 256, 384)
MIB = 1024 * 1024
BF16 = jnp.bfloat16
SPACE = pltpu.HBM
LARGE = 64
PAIRS = 4
SMALL = 64
F32 = jnp.float32


def dot(left, right):
    return jnp.dot(left, right, preferred_element_type=F32)


def dot_nt(left, right):
    return lax.dot_general(left, right, (((1,), (1,)), ((), ())), preferred_element_type=F32)


def tile(index, size):
    return pl.ds(pl.multiple_of(index * size, size), size)


class Named:
    def __init__(self, act):
        self._act = act

    def __getattr__(self, name):
        return functools.partial(self._act, name)


class Rows:
    def __init__(self, of):
        self.of = of


class Part:
    def __init__(self, array, shape, choose):
        self.array, self.shape, self.dtype, self.choose = array, shape, array.dtype, choose


class Stage:
    def __init__(self):
        self.scalars, self.own, self.ins, self.outs, self.raw = None, {}, {}, {}, []
        self.waited, self.sent = set(), {}
        self.at, self.send = Named(self._at), Named(self._send)

    def begin(self):
        for _, copies in self.ins.values():
            for copy in copies:
                copy.start()

    def _at(self, name, index):
        buffer, copies = self.ins[name]
        if (name, index) not in self.waited:
            self.waited.add((name, index))
            copies[index].wait()
        return buffer

    def __getitem__(self, name):
        if name in self.own:
            return self.own[name]
        if name in self.outs:
            return self.outs[name][0]
        for index in range(len(self.ins[name][1])):
            self._at(name, index)
        return self.ins[name][0]

    def __getattr__(self, name):
        return self[name]

    def _send(self, name, index=None):
        for place, copy in enumerate(self.outs[name][1]):
            if index in (None, place) and (name, place) not in self.sent:
                self.sent[name, place] = copy
                copy.start()

    def finish(self):
        for name in self.ins:
            self[name]
        for name in self.outs:
            self._send(name)
        for copy in self.sent.values():
            copy.wait()


def staged(name, body, scalars, ins, outs, scratch, raw=None, raw_sems=0, weight=0, limit=LARGE):
    raw = raw or []
    by_rows = [label for group in (ins, outs) for label, value in group.items() if isinstance(value, Rows)]
    ins = {label: value.of if isinstance(value, Rows) else value for label, value in ins.items()}
    outs = {label: value.of if isinstance(value, Rows) else value for label, value in outs.items()}

    def copies_of(label, source, target, sems):
        if label not in by_rows:
            return [pltpu.make_async_copy(source, target, sems.pop())]
        spans = [pl.ds(first, TOKENS) for first in range(0, target.shape[0], TOKENS)]
        return [pltpu.make_async_copy(source.at[span], target.at[span], sems.pop()) for span in spans]

    def count_of(label, shape):
        return shape[0] // TOKENS if label in by_rows else 1

    total = sum(count_of(n, v.shape) for n, v in ins.items()) + sum(count_of(n, v[0]) for n, v in outs.items())
    total += raw_sems

    def kernel(*refs):
        refs = list(refs)

        def take(count):
            head = refs[:count]
            del refs[:count]
            return head

        stage = Stage()
        stage.scalars = types.SimpleNamespace(**dict(zip(scalars, take(len(scalars)))))
        in_refs, stage.raw, out_refs = take(len(ins)), take(len(raw)), take(len(outs))
        in_vmem, out_vmem = take(len(ins)), take(len(outs))
        stage.own = dict(zip(scratch, take(len(scratch))))
        stage.own.update(vars(stage.scalars))
        sem_array = take(1)[0]
        sems = [sem_array.at[place] for place in range(total)]
        for label, source, target in zip(ins, in_refs, in_vmem):
            if isinstance(ins[label], Part):
                source = ins[label].choose(source, stage.scalars)
            stage.ins[label] = (target, copies_of(label, source, target, sems))
        for label, source, target in zip(outs, out_vmem, out_refs):
            stage.outs[label] = (source, copies_of(label, source, target, sems))
        stage.raw_sems = sems
        if not raw:
            stage.begin()
        body(stage)
        stage.finish()

    results = pl.pallas_call(
        kernel,
        out_shape=[jax.ShapeDtypeStruct(*shape) for shape in outs.values()],
        in_specs=[pl.BlockSpec(memory_space=pltpu.SMEM)] * len(scalars)
        + [pl.BlockSpec(memory_space=SPACE)] * (len(ins) + len(raw)),
        out_specs=[pl.BlockSpec(memory_space=SPACE)] * len(outs),
        scratch_shapes=[pltpu.VMEM(array.shape, array.dtype) for array in ins.values()]
        + [pltpu.VMEM(*shape) for shape in outs.values()]
        + [pltpu.VMEM(*shape) for shape in scratch.values()]
        + [pltpu.SemaphoreType.DMA((total,))],
        compiler_params=pltpu.CompilerParams(vmem_limit_bytes=limit * MIB),
        cost_estimate=pl.CostEstimate(
            flops=1000 + weight * 10**9, bytes_accessed=1000 + weight * 3 * 10**6, transcendentals=0
        ),
        name=name,
    )(
        *scalars.values(),
        *[array.array if isinstance(array, Part) else array for array in ins.values()],
        *raw,
    )
    return types.SimpleNamespace(**{str(label): result for label, result in zip(outs, results)})


def place_of(coords, doubled, part, entry):
    core, plane = part // 4, part % 4
    line = coords[0] ^ entry if doubled else (coords[0] - entry) & 3
    outer = coords[1] ^ (plane >> 1)
    inner = coords[3] ^ (plane & 1)
    return (line * 2 + outer) * 2 + (coords[2] ^ core), inner


def piece_copies(stage, pieces, sems, spot, doubled=False):
    copies = []
    for part in range(8):
        for entry in range(4):
            dp, inner = place_of(stage.coords, doubled, part, entry)
            for which, target in spot(dp, inner):
                copies.append(pltpu.make_async_copy(pieces[part].at[entry, which], target, sems[len(copies)]))
    for copy in copies:
        copy.start()
    return copies


def standard(value):
    centre = value - jnp.mean(value, -1, keepdims=True)
    rate = lax.rsqrt(jnp.mean(centre * centre, -1, keepdims=True) + EPS)
    return centre * rate, rate


def standard_back(value, gain, upstream):
    z, rate = standard(value)
    scaled = upstream * gain
    back = rate * (scaled - jnp.mean(scaled, -1, keepdims=True) - z * jnp.mean(scaled * z, -1, keepdims=True))
    return back, upstream * z


def blocks_of_tokens(length, run):
    for index in range(length // TOKENS):
        run(slice(index * TOKENS, (index + 1) * TOKENS), index)


def windowed(sizes, kind, run):
    for place, size in enumerate(sizes):
        pl.when(kind == place)(functools.partial(run, size))


def column_of(row):
    return jnp.broadcast_to(row.astype(F32), (128, row.shape[1])).T[:, :1]


def own_lanes(array, half):
    low = lax.broadcasted_iota(jnp.int32, array.shape, 1) < 64
    zero = jnp.zeros_like(array)
    return jnp.where(low, array, zero) if half == 0 else jnp.where(low, zero, array)


def attend(query, keys_t, values_t, query_seg, key_seg, window, mixed, mixed_t, total, bias, sums_t, sizes, block, first):
    length, width = query.shape
    heads = total.shape[0]
    lane = lax.broadcasted_iota(jnp.int32, (block, 128), 1)

    def one_block(index, carry):
        rows = tile(index, block)
        start = window[first, index]

        def run(size):
            span = pl.ds(pl.multiple_of(start, 128), size)
            bias[:, :size] = jnp.where(column_of(query_seg[:, rows]) == key_seg[:, span].astype(F32), 0.0, NEG)
            ones = jnp.ones((16, size), BF16)

            def one_pair(pair, tops):
                lanes = tile(pair, 128)
                q, k = query[rows, lanes], keys_t[lanes, span]
                for half in range(2):
                    scores = dot(own_lanes(q, half), k) * SCALE + bias[:, :size]
                    top = jnp.max(scores, -1, keepdims=True)
                    expo = jnp.exp2(scores - top).astype(BF16)
                    spot = pl.ds(pl.multiple_of(pair * 128 + half * 64, 64), 64)
                    parts = dot_nt(jnp.concatenate([values_t[spot, span], ones], 0), expo)
                    sums = parts[64:65]
                    mixed_t[spot, rows] = (parts[:64] * (1.0 / sums)).astype(BF16)
                    sums_t[pl.ds(pair * 2 + half, 1), :] = sums
                    tops = jnp.where(lane == pair * 2 + half, top, tops)
                return tops

            tops = lax.fori_loop(0, width // 128, one_pair, jnp.zeros((block, 128), F32), unroll=PAIRS)
            total[:, rows] = tops.T[:heads] + jnp.log2(sums_t[...])

        windowed(sizes, window[first + 1, index], run)
        mixed[rows, :] = mixed_t[:, rows].T
        return carry

    lax.fori_loop(0, length // block, one_block, 0)


def attend_back(query, keys, keys_t, values, back, mixed_t, total, query_seg, key_seg, window, query_back_t, key_acc, value_acc, bias, sizes, block, first):
    length, width = query.shape
    key_acc[...] = jnp.zeros(key_acc.shape, F32)
    value_acc[...] = jnp.zeros(value_acc.shape, F32)

    def one_block(index, carry):
        rows = tile(index, block)
        start = window[first, index]

        def run(size):
            span = pl.ds(pl.multiple_of(start, 128), size)
            bias[:size, :] = jnp.where(column_of(key_seg[:, span]) == query_seg[:, rows].astype(F32), 0.0, NEG)
            low = lax.broadcasted_iota(jnp.int32, (size, 128), 1) < 64

            def one_pair(pair, carried):
                lanes = tile(pair, 128)
                q, k, v, up = query[rows, lanes], keys[span, lanes], values[span, lanes], back[rows, lanes]
                q_t, up_t = q.T, up.T
                product = up_t.astype(F32) * mixed_t[lanes, rows].astype(F32)
                key_parts, value_parts = [], []
                for half in range(2):
                    scores = dot(own_lanes(k, half), q_t) * SCALE + bias[:size, :]
                    probs = jnp.exp2(scores - total[pl.ds(pair * 2 + half, 1), rows])
                    spread = dot(own_lanes(v, half), up_t)
                    delta = jnp.sum(product[half * 64 : half * 64 + 64], 0, keepdims=True)
                    scores_back = (probs * (spread - delta)).astype(BF16)
                    value_parts.append(dot(probs.astype(BF16), up))
                    key_parts.append(dot(scores_back, q))
                    spot = pl.ds(pl.multiple_of(pair * 128 + half * 64, 64), 64)
                    query_back_t[spot, rows] = (dot(keys_t[spot, span], scores_back) * 0.125).astype(BF16)
                value_acc[span, lanes] += jnp.where(low, *value_parts)
                key_acc[span, lanes] += jnp.where(low, *key_parts)
                return carried

            lax.fori_loop(0, width // 128, one_pair, 0, unroll=PAIRS)

        windowed(sizes, window[first + 1, index], run)
        return carry

    lax.fori_loop(0, length // block, one_block, 0)


def put_square(stage, grad, column, base):
    core = stage.coords[2]
    rows = grad.shape[0] // 16
    blocks = grad.astype(BF16).reshape(LINE, 2, 2, rows, grad.shape[1])
    for result, wanted in ((stage.keep, 0), (stage.send_, 1)):
        picked = jnp.where(core == wanted, blocks[:, :, 0], blocks[:, :, 1])
        for outer in range(2):
            for chunk in range(2):
                result[outer * 2 + column, :, base + chunk * rows : base + (chunk + 1) * rows, :] = picked[
                    :, outer, :, chunk * 128 : (chunk + 1) * 128
                ]


def self_forward_body(stage):
    affine, loose, weight = stage.affine, stage.loose, stage.weight
    copies = piece_copies(
        stage, stage.raw, stage.raw_sems, lambda dp, inner: [(slice(0, 7), loose.at[:, dp, :, tile(inner, 256)])]
    )
    stage.begin()
    for copy in copies:
        copy.wait()
    for w in range(3):
        for dp in range(16):
            for half in range(2):
                weight[w, dp * 32 + half * 16 : dp * 32 + half * 16 + 16, :] = loose[2 * w + half, dp]
    flat = jnp.sum(loose[6].astype(F32), 0)
    flat = flat[:, :256] + flat[:, 256:]
    affine[:, :256] = flat[:8]
    affine[:, 256:] = flat[8:]
    stage.send.weight()
    stage.send.affine()
    normed_t = stage.normed_t
    length = normed_t.shape[1]

    def project(rows, index):
        z, _ = standard(stage.at.target(index)[rows, :].astype(F32))
        n = (z * affine[0:1, :] + affine[1:2, :]).astype(BF16)
        normed_t[:, rows] = n.T
        query, key, value = (dot(n, weight[place]).astype(BF16) for place in range(3))
        stage.query[rows, :] = query
        stage.key[rows, :] = key
        stage.value[rows, :] = value
        stage.send.query(index)
        stage.send.key(index)
        stage.send.value(index)
        stage.key_t[:, rows] = key.T
        stage.value_t[:, rows] = value.T

    blocks_of_tokens(length, project)
    stage.send.normed_t()
    stage.send.key_t()
    attend(
        stage.query, stage.key_t, stage.value_t, stage.seg, stage.seg, stage.window, stage.mixed, stage.mixed_t,
        stage.total, stage.bias, stage.sums_t, SELF_SIZES, SELF_BLOCK, 0,
    )


def self_forward(coords, window, target, seg, pieces):
    length, width = target.shape
    low, turned = ((length, width), BF16), ((width, length), BF16)
    return staged(
        "self_forward", self_forward_body, dict(coords=coords, window=window), dict(target=Rows(target), seg=seg),
        dict(
            weight=((3, width, width), BF16), affine=((8, width), F32), query=Rows(low), key=Rows(low),
            value=Rows(low), key_t=turned, normed_t=turned, mixed=low, mixed_t=turned,
            total=((width // 64, length), F32),
        ),
        dict(
            loose=((7, 16, 16, width), BF16), value_t=turned, bias=((SELF_BLOCK, SELF_SIZES[-1]), F32),
            sums_t=((width // 64, SELF_BLOCK), F32),
        ),
        raw=pieces, raw_sems=32,
        weight=20,
    )


def cross_forward_body(stage):
    weight = stage.weight
    copies = piece_copies(
        stage,
        stage.raw,
        stage.raw_sems,
        lambda dp, inner: [(slice(0, 5), weight.at[:, tile(dp, 32), tile(inner, 256)])],
        doubled=True,
    )
    stage.begin()
    for copy in copies:
        copy.wait()
    stage.send.weight()
    source, affine = stage.source, stage.affine
    first = stage.first
    length = first.shape[0]
    padded = stage.padded
    count = source.shape[0]
    padded[...] = jnp.zeros(padded.shape, BF16)
    padded[:count, :] = source[...]
    stage.key[...] = dot(padded[...], weight[2]).astype(BF16)
    stage.value[...] = dot(padded[...], weight[3]).astype(BF16)
    stage.key_t[...] = stage.key[...].T
    stage.value_t[...] = stage.value[...].T
    stage.send.key()
    stage.send.key_t()
    stage.send.value()

    def project(rows, index):
        v = stage.at.target(index)[rows, :].astype(F32) + dot(stage.at.mixed1(index)[rows, :], weight[0])
        first[rows, :] = v
        stage.send.first(index)
        z, _ = standard(v)
        n = (z * affine[2:3, :] + affine[3:4, :]).astype(BF16)
        stage.normed2_t[:, rows] = n.T
        stage.query[rows, :] = dot(n, weight[1]).astype(BF16)
        stage.send.query(index)

    blocks_of_tokens(length, project)
    stage.send.normed2_t()
    attend(
        stage.query, stage.key_t, stage.value_t, stage.seg, stage.key_seg, stage.window, stage.mixed,
        stage.mixed_t, stage.total, stage.bias, stage.sums_t, CROSS_SIZES, CROSS_BLOCK, 2,
    )
    stage.send.mixed_t()
    stage.send.total()

    def finish(rows, index):
        m = stage.mixed[rows, :]
        v = first[rows, :] + dot(m, weight[4])
        stage.second[rows, :] = v
        z, _ = standard(v)
        n = (z * affine[4:5, :] + affine[5:6, :]).astype(BF16)
        stage.normed[rows, :] = n
        stage.normed_t[:, rows] = n.T
        stage.send.second(index)
        stage.send.normed(index)

    blocks_of_tokens(length, finish)


def cross_forward(coords, window, target, mixed1, affine, source, seg, key_seg, pieces):
    length, width = target.shape
    count = key_seg.shape[1]
    low, turned, full = ((length, width), BF16), ((width, length), BF16), ((length, width), F32)
    return staged(
        "cross_forward", cross_forward_body, dict(coords=coords, window=window),
        dict(
            mixed1=Rows(mixed1), target=Rows(target), affine=affine, source=source, seg=seg, key_seg=key_seg
        ),
        dict(
            weight=((5, width, width), BF16), key=((count, width), BF16), key_t=((width, count), BF16), value=((count, width), BF16),
            first=Rows(full), normed2_t=turned, query=Rows(low), mixed_t=turned,
            total=((width // 64, length), F32), second=Rows(full), normed=Rows(low), normed_t=turned,
        ),
        dict(
            bias=((CROSS_BLOCK, CROSS_SIZES[-1]), F32), sums_t=((width // 64, CROSS_BLOCK), F32),
            value_t=((width, count), BF16), mixed=low, padded=((count, width), BF16),
        ),
        raw=pieces, raw_sems=32,
        weight=20,
    )


FF_BLOCK = 256
FF_TOKENS = 512


def feed_forward_body(stage):
    expand, shrink, active, hidden_back = stage.expand, stage.shrink, stage.active, stage.hidden_back
    loose_expand, loose_shrink = stage.loose_expand, stage.loose_shrink
    coords, copies = stage.coords, []
    for part in range(8):
        core, kind = part // 4, part % 4
        for entry in range(8):
            first, line = entry // 4, coords[0] ^ (entry % 4)
            outer, inner = (kind, first) if kind < 2 else (first, kind - 2)
            outer, inner = coords[1] ^ outer, coords[3] ^ inner
            dp = (line * 2 + outer) * 2 + (coords[2] ^ core)
            if kind < 2:
                spot = loose_expand.at[tile(inner, 4), tile(dp, 32), :]
            else:
                spot = loose_shrink.at[inner, tile(dp, 4)]
            source = stage.raw[part].at[first, entry % 4]
            copies.append(pltpu.make_async_copy(source, spot, stage.raw_sems[len(copies)]))
            copies[-1].start()
    stage.begin()
    core = coords[2]
    width, hidden = expand.shape
    for copy in copies:
        copy.wait()
    for part in range(hidden // FF_BLOCK):
        expand[:, part * FF_BLOCK : (part + 1) * FF_BLOCK] = loose_expand[part]
    for side in range(2):
        shrink[:, side * width // 2 : (side + 1) * width // 2] = loose_shrink[side].reshape(hidden, width // 2)
    normed, back = stage.normed, stage.back
    normed_t, back_t = stage.normed_t, stage.back_t
    length = normed.shape[0]
    back_t[...] = back[...].T

    def one_part(part):
        lanes = slice(part * FF_BLOCK, (part + 1) * FF_BLOCK)
        for index in range(length // FF_TOKENS):
            rows = slice(index * FF_TOKENS, (index + 1) * FF_TOKENS)
            v = dot(normed[rows, :], expand[:, lanes])
            up = dot_nt(back[rows, :], shrink[lanes, :])
            square = v * v
            half = 0.5 + 0.5 * jnp.tanh(v * (0.7978845608028654 + 0.035677408136300125 * square))
            value = v * half
            slope = half + value * (1.0 - half) * (1.5957691216057308 + 0.21406444881780075 * square)
            active[rows, lanes] = value.astype(BF16)
            hidden_back[rows, lanes] = (up * slope).astype(BF16)
        grad = dot(normed_t[...], hidden_back[:, lanes]).astype(BF16)
        blocks = grad.reshape(LINE, 2, 2, width // 16, FF_BLOCK)
        inner, chunk = part // 4, part % 4 * 2
        for result, wanted in ((stage.keep, 0), (stage.send_, 1)):
            picked = jnp.where(core == wanted, blocks[:, :, 0], blocks[:, :, 1])
            for outer in range(2):
                for side in range(2):
                    first = (chunk + side) * width // 16
                    result[outer * 2 + inner, :, first : first + width // 16, :] = picked[
                        :, outer, :, side * 128 : (side + 1) * 128
                    ]
        grad = dot(back_t[...], active[:, lanes]).astype(BF16)
        line, outer = part // 2, part % 2
        for result, wanted in ((stage.keep, 0), (stage.send_, 1)):
            picked = jnp.where(core == wanted, grad[:, :128], grad[:, 128:])
            for side in range(2):
                result[outer * 2 + side, line, width // 2 :, :] = picked[side * width // 2 : (side + 1) * width // 2]

    for part in range(hidden // FF_BLOCK):
        one_part(part)
    stage.send.send_()
    stage.send.keep()

    def finish(rows, index):
        stage.normed_back[rows, :] = dot_nt(hidden_back[rows, :], expand[...])
        stage.send.normed_back(index)
        stage.output[rows, :] = (stage.at.second(index)[rows, :] + dot(active[rows, :], shrink[...])).astype(BF16)
        stage.send.output(index)

    blocks_of_tokens(length, finish)


def feed_forward(coords, normed, normed_t, second, back, pieces):
    length, width = normed.shape
    hidden = 4 * width
    part = ((4, LINE, width, 128), BF16)
    wide = ((length, hidden), BF16)
    return staged(
        "feed_forward", feed_forward_body, dict(coords=coords),
        dict(normed=normed, back=back, normed_t=normed_t, second=Rows(second)),
        dict(
            send_=part, keep=part, normed_back=Rows(((length, width), F32)), output=Rows(((length, width), BF16))
        ),
        dict(
            loose_expand=((hidden // FF_BLOCK, width, FF_BLOCK), BF16),
            loose_shrink=((2, hidden // 32, 32, width // 2), BF16),
            expand=((width, hidden), BF16), shrink=((hidden, width), BF16), active=wide, hidden_back=wide,
            back_t=((width, length), BF16),
        ),
        raw=pieces, raw_sems=64,
        weight=20,
    )


def add_affine(stage, row, gain, bias):
    stage.affine_back[row : row + 1, :] += jnp.sum(gain, 0, keepdims=True)
    stage.affine_back[row + 1 : row + 2, :] += jnp.sum(bias, 0, keepdims=True)


def norm_back_body(stage):
    affine = stage.affine
    stage.affine_back[...] = jnp.zeros(stage.affine_back.shape, F32)

    def run(rows, index):
        upstream = stage.at.normed_back(index)[rows, :]
        grad, gain = standard_back(stage.at.second(index)[rows, :], affine[4:5, :], upstream)
        add_affine(stage, 4, gain, upstream)
        grad = grad + stage.at.back(index)[rows, :].astype(F32)
        stage.second_back[rows, :] = grad
        stage.mixed_back[rows, :] = dot_nt(grad.astype(BF16), stage.weight[...]).astype(BF16)
        stage.send.second_back(index)
        stage.send.mixed_back(index)

    blocks_of_tokens(stage.second_back.shape[0], run)


def norm_back(affine, weight, second, normed_back, back):
    length, width = second.shape
    low, full = ((length, width), BF16), ((length, width), F32)
    return staged(
        "norm_back", norm_back_body, {},
        dict(
            affine=affine, normed_back=Rows(normed_back), second=Rows(second), back=Rows(back),
            weight=Part(weight, (width, width), lambda ref, scalars: ref.at[4]),
        ),
        dict(affine_back=((8, width), F32), mixed_back=Rows(low), second_back=Rows(full)),
        {},
        weight=3,
    )


def square_grads(stage, base, left_t, right, turned):
    for column in range(2):
        cols = slice(column * 256, (column + 1) * 256)
        grad = dot_nt(left_t[...], right[cols, :]) if turned else dot(left_t[...], right[:, cols])
        put_square(stage, grad, column, base)


def cross_back_body(stage):
    query = stage.query
    key_acc, value_acc, query_back = stage.key_acc, stage.value_acc, stage.query_back
    attend_back(
        query, stage.key, stage.key_t, stage.value, stage.mixed_back, stage.mixed_t, stage.total, stage.seg,
        stage.key_seg, stage.window, query_back, key_acc, value_acc, stage.bias, CROSS_BACK_SIZES, CROSS_BACK_BLOCK, 6,
    )
    affine, weight, key_back, value_back = stage.affine, stage.weight, stage.key_back, stage.value_back
    key_back[...] = (key_acc[...] * 0.125).astype(BF16)
    value_back[...] = value_acc[...].astype(BF16)
    source_back = dot_nt(key_back[...], weight[2]) + dot_nt(value_back[...], weight[3])
    stage.source_back[...] = source_back[: stage.source_back.shape[0]]
    stage.send.source_back()
    stage.affine_back[...] = stage.affine_before[...]
    first_low = stage.first_low

    def run(rows, index):
        upstream = dot(weight[1], query_back[:, rows]).T
        grad, gain = standard_back(stage.first[rows, :], affine[2:3, :], upstream)
        add_affine(stage, 2, gain, upstream)
        second_back = stage.second_back[rows, :]
        stage.out_low[rows, :] = second_back.astype(BF16)
        grad = grad + second_back
        stage.first_back[rows, :] = grad
        low = grad.astype(BF16)
        first_low[rows, :] = low
        stage.mixed1_back[rows, :] = dot_nt(low, weight[0]).astype(BF16)

    blocks_of_tokens(query.shape[0], run)
    stage.send.first_back()
    stage.send.mixed1_back()
    stage.send.affine_back()
    rows_of = weight.shape[1] // 16 * 2
    square_grads(stage, 0, stage.mixed1_t, first_low, False)
    square_grads(stage, rows_of, stage.normed_t, query_back, True)
    padded, source_t = stage.padded, stage.source_t
    padded[...] = jnp.zeros(padded.shape, BF16)
    padded[: stage.source.shape[0], :] = stage.source[...]
    source_t[...] = padded[...].T
    square_grads(stage, 2 * rows_of, source_t, key_back, False)
    square_grads(stage, 3 * rows_of, source_t, value_back, False)
    square_grads(stage, 4 * rows_of, stage.mixed_t, stage.out_low, False)


def cross_back(coords, window, ins, source_length):
    ins_ = types.SimpleNamespace(**ins)
    length, width = ins_.query.shape
    count = ins_.key.shape[0]
    low, full = ((length, width), BF16), ((length, width), F32)
    keyed = (count, width)
    part = ((4, LINE, 5 * width // 8, 128), BF16)
    return staged(
        "cross_back", cross_back_body, dict(coords=coords, window=window), ins,
        dict(
            keep=part, send_=part, first_back=full, mixed1_back=low, affine_back=((8, width), F32),
            source_back=((source_length, width), F32),
        ),
        dict(
            key_acc=(keyed, F32), value_acc=(keyed, F32), query_back=((width, length), BF16), first_low=low, out_low=low,
            key_back=(keyed, BF16), value_back=(keyed, BF16), bias=((CROSS_BACK_SIZES[-1], CROSS_BACK_BLOCK), F32),
            padded=(keyed, BF16), source_t=((width, count), BF16),
        ),
        weight=20,
    )


AFFINE_ROWS = 16


def pack_first_body(wide, stage):
    for place in range(3):
        for half in range(2):
            stage.packed[2 * place + half] = stage[place][half * 16 : half * 16 + 16, :]
    coords = stage.coords
    own = stage.norms[...]
    width = 2 * stage.packed.shape[2]
    row_at, from_row = (lax.broadcasted_iota(jnp.int32, (8, own.shape[0]), axis) for axis in range(2))
    from_lane, lane_at = (lax.broadcasted_iota(jnp.int32, (wide, width), axis) for axis in range(2))
    down = (row_at == coords[3] * 3 + from_row).astype(BF16)
    right = (lane_at == coords[4] + from_lane).astype(BF16)
    placed = dot(down, dot(own, right).astype(BF16)).astype(BF16)
    stage.packed[6] = jnp.concatenate([placed[:, : width // 2], placed[:, width // 2 :]], 0)


def pack_first(coords, weights, norms):
    ins = {**dict(enumerate(weights)), **dict(norms=norms)}
    outs = dict(packed=((7, 16, weights[0].shape[1]), BF16))
    body = functools.partial(pack_first_body, norms.shape[1])
    return staged("pack", body, dict(coords=coords), ins, outs, {}, limit=SMALL).packed


def join_pairs_body(stage):
    for place in range(4):
        result = stage.one if place < 2 else stage.two
        result[place % 2] = stage[place][...]
        if place == 1:
            stage.send.one()


def join_pairs(one, two):
    shape = (2, *one[0].shape)
    outs = dict(one=(shape, BF16), two=(shape, BF16))
    result = staged("join", join_pairs_body, {}, dict(enumerate([*one, *two])), outs, {}, limit=SMALL)
    return [result.one, result.two]


def find_windows(seg, keys, sizes, block, count):
    lane = lax.broadcasted_iota(jnp.int32, (1, 128), 1)
    starts, kinds = jnp.zeros((1, 128), jnp.int32), jnp.zeros((1, 128), jnp.int32)
    for index in range(seg.shape[1] // block):
        first, last = seg[:, index * block : index * block + 1], seg[:, (index + 1) * block - 1 : (index + 1) * block]
        low = jnp.sum((keys < first).astype(F32), 1, keepdims=True).astype(jnp.int32) // 128 * 128
        high = (jnp.sum((keys <= last).astype(F32), 1, keepdims=True).astype(jnp.int32) + 127) // 128 * 128
        need = high - low
        kind = sum(((need > size).astype(jnp.int32) for size in sizes[:-1]), jnp.zeros_like(need))
        size = sum((jnp.where(kind == place, size, 0) for place, size in enumerate(sizes)), jnp.zeros_like(need))
        starts = jnp.where(lane == index, jnp.minimum(low, count - size), starts)
        kinds = jnp.where(lane == index, kind, kinds)
    return starts, kinds


def pack_rest_body(stage):
    for place in range(5):
        stage.second[place] = stage[place][...]
    for place in range(4):
        stage.third[place] = stage.expand[:, place * 256 : place * 256 + 256]
        stage.third[4 + place] = stage.shrink[place * 32 : place * 32 + 32, :]
    seg, source_seg = stage.seg[...], stage.source_seg[...]
    count = stage.key_seg.shape[1]
    stage.key_seg[...] = jnp.full(stage.key_seg.shape, -1, jnp.int32)
    stage.key_seg[:, : source_seg.shape[1]] = jnp.where(stage.source_keep[...] > 0, source_seg, -1)
    rows = (
        *find_windows(seg, seg, SELF_SIZES, SELF_BLOCK, seg.shape[1]),
        *find_windows(seg, source_seg, CROSS_SIZES, CROSS_BLOCK, count),
        *find_windows(seg, seg, BACK_SIZES, SELF_BLOCK, seg.shape[1]),
        *find_windows(seg, source_seg, CROSS_BACK_SIZES, CROSS_BACK_BLOCK, count),
    )
    stage.window[...] = jnp.zeros(stage.window.shape, jnp.int32)
    for place, row in enumerate(rows):
        stage.window[place : place + 1, :] = row


def pack_rest(weights, expand, shrink, seg, source_seg, source_keep):
    ins = {
        **dict(enumerate(weights)),
        **dict(expand=expand, shrink=shrink, seg=seg, source_seg=source_seg, source_keep=source_keep),
    }
    outs = dict(
        second=((5, 32, 256), BF16), third=((8, 32, 256), BF16), window=((8, 128), jnp.int32),
        key_seg=((1, CROSS_SIZES[-1]), jnp.int32),
    )
    return staged("pack", pack_rest_body, {}, ins, outs, {})


def self_back_body(stage):
    query = stage.query
    key_acc, value_acc, query_back = stage.key_acc, stage.value_acc, stage.query_back
    attend_back(
        query, stage.key, stage.key_t, stage.value, stage.mixed_back, stage.mixed_t, stage.total, stage.seg,
        stage.seg, stage.window, query_back, key_acc, value_acc, stage.bias, BACK_SIZES, SELF_BLOCK, 4,
    )
    weight, affine = stage.weight, stage.affine
    key_back, value_back = stage.key_back, stage.value_back
    key_back[...] = (key_acc[...] * 0.125).astype(BF16)
    value_back[...] = value_acc[...].astype(BF16)
    stage.affine_back[...] = stage.affine_before[...]

    def run(rows, index):
        upstream = dot_nt(key_back[rows, :], weight[1]) + dot_nt(value_back[rows, :], weight[2])
        upstream = upstream + dot(weight[0], query_back[:, rows]).T
        grad, gain = standard_back(stage.target[rows, :].astype(F32), affine[0:1, :], upstream)
        add_affine(stage, 0, gain, upstream)
        stage.target_back[rows, :] = grad + stage.first_back[rows, :]
        stage.send.target_back(index)

    blocks_of_tokens(query.shape[0], run)
    width = query.shape[1]
    rows_of = width // 16 * 2
    square_grads(stage, 0, stage.normed_t, query_back, True)
    square_grads(stage, rows_of, stage.normed_t, key_back, False)
    square_grads(stage, 2 * rows_of, stage.normed_t, value_back, False)
    norms = stage.affine_back[...]
    norms = jnp.concatenate([norms, jnp.zeros_like(norms)], 0)
    for inner in range(2):
        low = (norms if inner == 0 else jnp.concatenate([norms[3:], norms[:3]], 0)).astype(BF16)
        for line in range(LINE):
            for result in (stage.keep, stage.send_):
                for outer in range(2):
                    result[outer * 2 + inner, line, 3 * rows_of :, :] = low[:, line * 128 : (line + 1) * 128]


def self_back(coords, window, ins):
    ins_ = types.SimpleNamespace(**ins)
    length, width = ins_.query.shape
    low, turned = ((length, width), BF16), ((width, length), BF16)
    part = ((4, LINE, 3 * width // 8 + AFFINE_ROWS, 128), BF16)
    return staged(
        "self_back", self_back_body, dict(coords=coords, window=window), ins,
        dict(send_=part, keep=part, target_back=Rows(((length, width), F32))),
        dict(
            key_acc=((length, width), F32), value_acc=((length, width), F32), query_back=turned, key_back=low,
            value_back=low, affine_back=((8, width), F32), bias=((BACK_SIZES[-1], SELF_BLOCK), F32),
        ),
        weight=20,
    )


def sums_body(jobs, stage):
    place = 0
    for index, job in enumerate(jobs):
        total = stage[place, index][...].astype(F32)
        for more in range(1, len(job)):
            total = total + stage[place + more, index][...].astype(F32)
        place += len(job)
        stage.outs[index][0][...] = total.astype(BF16)
        stage._send(index)


def sums(coords, jobs):
    ins = {}
    for index, job in enumerate(jobs):
        for part in job:
            ins[len(ins), index] = part
    outs = {index: (job[0].shape, BF16) for index, job in enumerate(jobs)}
    body = functools.partial(sums_body, jobs)
    return list(vars(staged("sums", body, dict(coords=coords), ins, outs, {}, limit=SMALL)).values())


def plane_part(array, step):
    def choose(ref, scalars):
        coords = scalars.coords
        return ref.at[(coords[1] ^ (step >> 1)) * 2 + (coords[3] ^ (step & 1))]

    return Part(array, array.shape[1:], choose)


def line_part(array, step):
    return Part(array, array.shape[1:], lambda ref, scalars: ref.at[(scalars.coords[0] + step) & 3])


ORDER = (1, 2, 3, 0)


def chip_jobs(keep, away):
    return [[plane_part(keep, step), plane_part(away, step)] for step in ORDER]


def plane_jobs(arrays):
    return [[line_part(array, step) for array in arrays] for step in ORDER]


def last_sums_body(hidden, squares, wide, stage):
    def total_of(first):
        parts = [stage[first + place][...].astype(F32) for place in range(4)]
        return parts[0] + parts[1] + (parts[2] + parts[3])

    results = [value[0] for value in stage.outs.values()]
    if hidden:
        total = total_of(0)
        half = total.shape[0] // 2
        rows = half // 8
        for chunk in range(8):
            results[0][:, chunk * 128 : (chunk + 1) * 128] = total[chunk * rows : (chunk + 1) * rows]
        results[1][...] = total[half:].T
        results = results[2:]
    first = 4 if hidden else 0
    for count in squares:
        total = total_of(first)
        first += 4
        for place in range(count):
            for chunk in range(2):
                row = (2 * place + chunk) * 32
                results[place][:, chunk * 128 : (chunk + 1) * 128] = total[row : row + 32]
        results = results[count:]
        if total.shape[0] > count * 64:
            lane = (stage.coords[1] * 2 + stage.coords[2]) * 32 + stage.coords[5]
            norms = pltpu.roll(total[count * 64 : count * 64 + 8], (128 - lane) & 127, 1)
            results[0][...] = norms[:3, :wide]
            results = results[1:]


def last_sums(coords, hidden, squares, wide):
    arrays = [array for group in ([hidden] if hidden else []) + squares for array in group]
    outs = {}
    if hidden:
        rows = hidden[0].shape[0]
        outs[(0,)] = ((rows // 16, 1024), F32)
        outs[(1,)] = ((128, rows // 2), F32)
    counts = []
    for group in squares:
        counts.append(group[0].shape[0] // 64)
        for _ in range(counts[-1]):
            outs[(len(outs),)] = ((32, 256), F32)
        if group[0].shape[0] % 64:
            outs[(len(outs),)] = ((3, wide), F32)
    body = functools.partial(last_sums_body, bool(hidden), counts, wide)
    result = staged("last_sums", body, dict(coords=coords), dict(enumerate(arrays)), outs, {}, limit=SMALL)
    return list(vars(result).values())


SWAP = [(0, 1), (1, 0)]
SHIFTS = [[(i, (i + k) % LINE) for i in range(LINE)] for k in range(LINE)]
CROSS = [[(i, i ^ k) for i in range(4)] for k in range(4)]
PLANE = ("b", "i")


def tie(*values):
    return lax.optimization_barrier(values)


def join(arrays):
    return jnp.concatenate(arrays, 0).reshape(len(arrays), *arrays[0].shape)


def along_line(array):
    return [array] + [lax.ppermute(array, "a", SHIFTS[k]) for k in (1, 2, 3)]


def along_plane(array):
    return [array] + [lax.ppermute(array, PLANE, CROSS[k]) for k in (1, 2, 3)]


def line_pair(array, step):
    return jnp.concatenate([array, lax.ppermute(array, "a", CROSS[step])], 0)


def across_cores(arrays):
    return arrays + [lax.ppermute(array, "c", SWAP) for array in arrays]


def swap_cores(array):
    return lax.ppermute(array, "c", SWAP)


def to_plane(arrays):
    return [lax.ppermute(array, PLANE, CROSS[k]) for array, k in zip(arrays, (1, 2, 3))] + arrays[3:4]


def to_line(arrays):
    return [lax.ppermute(array, "a", SHIFTS[k]) for array, k in zip(arrays, (1, 2, 3))] + arrays[3:4]


def shards(
    target,
    source,
    target_segment,
    source_segment,
    source_keep,
    self_query,
    self_key,
    self_value,
    self_output,
    cross_query,
    cross_key,
    cross_value,
    cross_output,
    expand_weight,
    shrink_weight,
    norm_affine,
    cotangent,
):
    src_length = source.shape[1]
    rest = lax.axis_size("r")
    wide = norm_affine.shape[1]
    a, b, c, r, i = (lax.axis_index(name) for name in "abcri")
    coords = jnp.stack([a, b, c, i, (((a * 2 + b) * 2 + c) * rest + r) * wide, r * wide]).astype(jnp.int32)

    def whole_rows(shard):
        return lax.all_gather(shard, "r", axis=0, tiled=True) if rest > 1 else shard

    shard_one = pack_first(coords, [whole_rows(w) for w in (self_query, self_key, self_value)], norm_affine)
    if rest > 1:
        norms = lax.psum(shard_one[6].astype(F32), "r").astype(BF16)
        shard_one = jnp.concatenate([shard_one[:6], norms[None]], 0)
    x, upstream, sent = target[0], cotangent[0], source[0]
    line_one = along_line(shard_one)
    others = [whole_rows(w) for w in (self_output, cross_query, cross_key, cross_value, cross_output)]
    rest_of = pack_rest(
        others, whole_rows(expand_weight), whole_rows(shrink_weight), target_segment, source_segment, source_keep
    )
    seg, key_seg, window = target_segment, rest_of.key_seg, rest_of.window
    near_one = along_plane(join(line_one))
    pair_two, pair_three = line_pair(rest_of.second, 1), line_pair(rest_of.third, 1)
    near_one[0], pair_two, pair_three = tie(near_one[0], pair_two, pair_three)
    joined_two = line_pair(pair_two, 2).reshape(4, 5, 32, -1)
    halves = (pair_three.reshape(2, 8, 32, -1), lax.ppermute(pair_three, "a", CROSS[2]).reshape(2, 8, 32, -1))
    parts = [jnp.concatenate([half[:, :4] for half in halves], 0), jnp.concatenate([half[:, 4:] for half in halves], 0)]
    pieces_one = across_cores(near_one)
    joined_two, pieces_one = tie(joined_two, pieces_one)
    stage_two = along_plane(joined_two)
    ready, *parts = tie(x, *parts)
    sides = [lax.ppermute(parts[0], "i", SWAP), lax.ppermute(parts[1], "b", SWAP)]
    one = self_forward(coords, window, ready, seg, pieces_one)
    sides[0], sides[1], stage_two[0], one.mixed = tie(*sides, stage_two[0], one.mixed)
    sides = join_pairs(*zip(parts, sides))
    far = [lax.ppermute(sides[0], "b", SWAP), lax.ppermute(sides[1], "i", SWAP)]
    pieces_two = across_cores([tie(array, one.mixed)[0] for array in stage_two])
    two = cross_forward(coords, window, x, one.mixed, one.affine, sent, seg, key_seg, pieces_two)
    pieces_three = across_cores(
        [sides[0], tie(far[0], two.normed)[0], sides[1], tie(far[1], two.normed)[0]]
    )
    three = feed_forward(coords, two.normed, two.normed_t, two.second, upstream, pieces_three)
    away_three = swap_cores(three.send_)
    four = norm_back(one.affine, two.weight, two.second, three.normed_back, upstream)
    away_three, four.mixed_back = tie(away_three, four.mixed_back)
    chip_three = sums(coords, chip_jobs(three.keep, away_three))
    chip_three, four.mixed_back = tie(chip_three, four.mixed_back)
    plane_three = to_plane(chip_three)
    five = cross_back(
        coords,
        window,
        dict(
            query=two.query, key=two.key, seg=seg, key_seg=key_seg, mixed_t=two.mixed_t, total=two.total,
            value=two.value, mixed_back=four.mixed_back, key_t=two.key_t, weight=two.weight,
            affine=one.affine, affine_before=four.affine_back, first=two.first, second_back=four.second_back,
            mixed1_t=one.mixed_t, normed_t=two.normed2_t, source=sent,
        ),
        src_length,
    )
    five.send_, plane_three = tie(five.send_, plane_three)
    away_two = swap_cores(five.send_)
    line_three = to_line(sums(coords, plane_jobs(plane_three)))
    away_two, line_three[3] = tie(away_two, line_three[3])
    chip_two = sums(coords, chip_jobs(five.keep, away_two))
    chip_two, five.mixed1_back = tie(chip_two, five.mixed1_back)
    plane_two = to_plane(chip_two)
    six = self_back(
        coords,
        window,
        dict(
            query=one.query, key=one.key, seg=seg, total=one.total,
            value=one.value, mixed_back=five.mixed1_back, mixed_t=one.mixed_t, key_t=one.key_t,
            weight=one.weight, affine=one.affine, affine_before=five.affine_back, target=x,
            first_back=five.first_back, normed_t=one.normed_t,
        ),
    )
    six.send_, plane_two, line_three = tie(six.send_, plane_two, line_three)
    away_one = swap_cores(six.send_)
    tail = sums(coords, chip_jobs(six.keep, away_one) + plane_jobs(plane_two))
    plane_one = to_plane(tail[:4])
    line_two = to_line(tail[4:])
    line_three, line_two[3] = tie(line_three, line_two[3])
    hidden = last_sums(coords, line_three, [], wide)
    plane_one, hidden = tie(plane_one, hidden)
    line_one = to_line(sums(coords, plane_jobs(plane_one)))
    *squares, norms = last_sums(coords, [], [line_two, line_one], wide)
    if rest > 1:
        norms = lax.psum(norms, "r")

    def own_block(spread):
        return lax.psum_scatter(spread, "r", scatter_dimension=0, tiled=True) if rest > 1 else spread

    grads = [own_block(grad) for grad in (*squares[5:], *squares[:5], *hidden)]
    return (three.output[None], six.target_back[None], five.source_back[None], *grads, norms)


def solution(mesh):
    dp, inner = mesh.shape["dp"], mesh.shape["inner"]
    fine = Mesh(mesh.devices.reshape(4, 2, 2, dp // 16, inner), ("a", "b", "c", "r", "i"))
    split = ("a", "b", "c", "r")
    in_specs = (
        P((*split, "i"), None, None),
        P((*split, "i"), None, None),
        P((*split, "i"), None),
        P((*split, "i"), None),
        P((*split, "i"), None),
        P(split, "i"),
        P(split, "i"),
        P(split, "i"),
        P(split, "i"),
        P(split, "i"),
        P(split, "i"),
        P(split, "i"),
        P(split, "i"),
        P(split, "i"),
        P(split, "i"),
        P("i", split),
        P((*split, "i"), None, None),
    )
    out_specs = (
        P((*split, "i"), None, None),
        P((*split, "i"), None, None),
        P((*split, "i"), None, None),
        P(split, "i"),
        P(split, "i"),
        P(split, "i"),
        P(split, "i"),
        P(split, "i"),
        P(split, "i"),
        P(split, "i"),
        P(split, "i"),
        P(split, "i"),
        P(split, "i"),
        P("i", split),
    )
    return jax.shard_map(shards, mesh=fine, in_specs=in_specs, out_specs=out_specs, check_vma=False)
```

```python
import functools
import types

import jax
import jax.numpy as jnp
from jax import lax
from jax.experimental import pallas as pl
from jax.experimental.pallas import tpu as pltpu
from jax.sharding import Mesh
from jax.sharding import PartitionSpec as P

EPS = 1e-05
NEG = -1e30
SCALE = 0.125 * 1.4426950408889634
TOKENS = 256
LINE = 4
SELF_BLOCK = 256
SELF_SIZES = (384, 512, 768, 1024)
BACK_SIZES = (384, 512, 768, 1024)
CROSS_BLOCK = 256
CROSS_BACK_BLOCK = 512
CROSS_BACK_SIZES = (256, 384)
CROSS_SIZES = (128, 256, 384)
MIB = 1024 * 1024
BF16 = jnp.bfloat16
SPACE = pltpu.HBM
LARGE = 64
PAIRS = 4
SMALL = 64
F32 = jnp.float32


def dot(left, right):
    return jnp.dot(left, right, preferred_element_type=F32)


def dot_nt(left, right):
    return lax.dot_general(left, right, (((1,), (1,)), ((), ())), preferred_element_type=F32)


def tile(index, size):
    return pl.ds(pl.multiple_of(index * size, size), size)


class Named:
    def __init__(self, act):
        self._act = act

    def __getattr__(self, name):
        return functools.partial(self._act, name)


class Rows:
    def __init__(self, of):
        self.of = of


class Part:
    def __init__(self, array, shape, choose):
        self.array, self.shape, self.dtype, self.choose = array, shape, array.dtype, choose


class Stage:
    def __init__(self):
        self.scalars, self.own, self.ins, self.outs, self.raw = None, {}, {}, {}, []
        self.waited, self.sent = set(), {}
        self.at, self.send = Named(self._at), Named(self._send)

    def begin(self):
        for _, copies in self.ins.values():
            for copy in copies:
                copy.start()

    def _at(self, name, index):
        buffer, copies = self.ins[name]
        if (name, index) not in self.waited:
            self.waited.add((name, index))
            copies[index].wait()
        return buffer

    def __getitem__(self, name):
        if name in self.own:
            return self.own[name]
        if name in self.outs:
            return self.outs[name][0]
        for index in range(len(self.ins[name][1])):
            self._at(name, index)
        return self.ins[name][0]

    def __getattr__(self, name):
        return self[name]

    def _send(self, name, index=None):
        for place, copy in enumerate(self.outs[name][1]):
            if index in (None, place) and (name, place) not in self.sent:
                self.sent[name, place] = copy
                copy.start()

    def finish(self):
        for name in self.ins:
            self[name]
        for name in self.outs:
            self._send(name)
        for copy in self.sent.values():
            copy.wait()


def staged(name, body, scalars, ins, outs, scratch, raw=None, raw_sems=0, weight=0, limit=LARGE):
    raw = raw or []
    by_rows = [label for group in (ins, outs) for label, value in group.items() if isinstance(value, Rows)]
    ins = {label: value.of if isinstance(value, Rows) else value for label, value in ins.items()}
    outs = {label: value.of if isinstance(value, Rows) else value for label, value in outs.items()}

    def copies_of(label, source, target, sems):
        if label not in by_rows:
            return [pltpu.make_async_copy(source, target, sems.pop())]
        spans = [pl.ds(first, TOKENS) for first in range(0, target.shape[0], TOKENS)]
        return [pltpu.make_async_copy(source.at[span], target.at[span], sems.pop()) for span in spans]

    def count_of(label, shape):
        return shape[0] // TOKENS if label in by_rows else 1

    total = sum(count_of(n, v.shape) for n, v in ins.items()) + sum(count_of(n, v[0]) for n, v in outs.items())
    total += raw_sems

    def kernel(*refs):
        refs = list(refs)

        def take(count):
            head = refs[:count]
            del refs[:count]
            return head

        stage = Stage()
        stage.scalars = types.SimpleNamespace(**dict(zip(scalars, take(len(scalars)))))
        in_refs, stage.raw, out_refs = take(len(ins)), take(len(raw)), take(len(outs))
        in_vmem, out_vmem = take(len(ins)), take(len(outs))
        stage.own = dict(zip(scratch, take(len(scratch))))
        stage.own.update(vars(stage.scalars))
        sem_array = take(1)[0]
        sems = [sem_array.at[place] for place in range(total)]
        for label, source, target in zip(ins, in_refs, in_vmem):
            if isinstance(ins[label], Part):
                source = ins[label].choose(source, stage.scalars)
            stage.ins[label] = (target, copies_of(label, source, target, sems))
        for label, source, target in zip(outs, out_vmem, out_refs):
            stage.outs[label] = (source, copies_of(label, source, target, sems))
        stage.raw_sems = sems
        if not raw:
            stage.begin()
        body(stage)
        stage.finish()

    results = pl.pallas_call(
        kernel,
        out_shape=[jax.ShapeDtypeStruct(*shape) for shape in outs.values()],
        in_specs=[pl.BlockSpec(memory_space=pltpu.SMEM)] * len(scalars)
        + [pl.BlockSpec(memory_space=SPACE)] * (len(ins) + len(raw)),
        out_specs=[pl.BlockSpec(memory_space=SPACE)] * len(outs),
        scratch_shapes=[pltpu.VMEM(array.shape, array.dtype) for array in ins.values()]
        + [pltpu.VMEM(*shape) for shape in outs.values()]
        + [pltpu.VMEM(*shape) for shape in scratch.values()]
        + [pltpu.SemaphoreType.DMA((total,))],
        compiler_params=pltpu.CompilerParams(vmem_limit_bytes=limit * MIB),
        cost_estimate=pl.CostEstimate(
            flops=1000 + weight * 10**9, bytes_accessed=1000 + weight * 3 * 10**6, transcendentals=0
        ),
        name=name,
    )(
        *scalars.values(),
        *[array.array if isinstance(array, Part) else array for array in ins.values()],
        *raw,
    )
    return types.SimpleNamespace(**{str(label): result for label, result in zip(outs, results)})


def place_of(coords, doubled, part, entry):
    core, plane = part // 4, part % 4
    line = coords[0] ^ entry if doubled else (coords[0] - entry) & 3
    outer = coords[1] ^ (plane >> 1)
    inner = coords[3] ^ (plane & 1)
    return (line * 2 + outer) * 2 + (coords[2] ^ core), inner


def piece_copies(stage, pieces, sems, spot, doubled=False):
    copies = []
    for part in range(8):
        for entry in range(4):
            dp, inner = place_of(stage.coords, doubled, part, entry)
            for which, target in spot(dp, inner):
                copies.append(pltpu.make_async_copy(pieces[part].at[entry, which], target, sems[len(copies)]))
    for copy in copies:
        copy.start()
    return copies


def standard(value):
    centre = value - jnp.mean(value, -1, keepdims=True)
    rate = lax.rsqrt(jnp.mean(centre * centre, -1, keepdims=True) + EPS)
    return centre * rate, rate


def standard_back(value, gain, upstream):
    z, rate = standard(value)
    scaled = upstream * gain
    back = rate * (scaled - jnp.mean(scaled, -1, keepdims=True) - z * jnp.mean(scaled * z, -1, keepdims=True))
    return back, upstream * z


def blocks_of_tokens(length, run):
    for index in range(length // TOKENS):
        run(slice(index * TOKENS, (index + 1) * TOKENS), index)


def windowed(sizes, kind, run):
    for place, size in enumerate(sizes):
        pl.when(kind == place)(functools.partial(run, size))


def column_of(row):
    return jnp.broadcast_to(row.astype(F32), (128, row.shape[1])).T[:, :1]


def own_lanes(array, half):
    low = lax.broadcasted_iota(jnp.int32, array.shape, 1) < 64
    zero = jnp.zeros_like(array)
    return jnp.where(low, array, zero) if half == 0 else jnp.where(low, zero, array)


def attend(query, keys_t, values_t, query_seg, key_seg, window, mixed, mixed_t, total, bias, sums_t, sizes, block, first):
    length, width = query.shape
    heads = total.shape[0]
    lane = lax.broadcasted_iota(jnp.int32, (block, 128), 1)

    def one_block(index, carry):
        rows = tile(index, block)
        start = window[first, index]

        def run(size):
            span = pl.ds(pl.multiple_of(start, 128), size)
            bias[:, :size] = jnp.where(column_of(query_seg[:, rows]) == key_seg[:, span].astype(F32), 0.0, NEG)
            ones = jnp.ones((16, size), BF16)

            def one_pair(pair, tops):
                lanes = tile(pair, 128)
                q, k = query[rows, lanes], keys_t[lanes, span]
                for half in range(2):
                    scores = dot(own_lanes(q, half), k) * SCALE + bias[:, :size]
                    top = jnp.max(scores, -1, keepdims=True)
                    expo = jnp.exp2(scores - top).astype(BF16)
                    spot = pl.ds(pl.multiple_of(pair * 128 + half * 64, 64), 64)
                    parts = dot_nt(jnp.concatenate([values_t[spot, span], ones], 0), expo)
                    sums = parts[64:65]
                    mixed_t[spot, rows] = (parts[:64] * (1.0 / sums)).astype(BF16)
                    sums_t[pl.ds(pair * 2 + half, 1), :] = sums
                    tops = jnp.where(lane == pair * 2 + half, top, tops)
                return tops

            tops = lax.fori_loop(0, width // 128, one_pair, jnp.zeros((block, 128), F32), unroll=PAIRS)
            total[:, rows] = tops.T[:heads] + jnp.log2(sums_t[...])

        windowed(sizes, window[first + 1, index], run)
        mixed[rows, :] = mixed_t[:, rows].T
        return carry

    lax.fori_loop(0, length // block, one_block, 0)


def attend_back(query, keys, keys_t, values, back, mixed_t, total, query_seg, key_seg, window, query_back_t, key_acc, value_acc, bias, sizes, block, first):
    length, width = query.shape
    key_acc[...] = jnp.zeros(key_acc.shape, F32)
    value_acc[...] = jnp.zeros(value_acc.shape, F32)

    def one_block(index, carry):
        rows = tile(index, block)
        start = window[first, index]

        def run(size):
            span = pl.ds(pl.multiple_of(start, 128), size)
            bias[:size, :] = jnp.where(column_of(key_seg[:, span]) == query_seg[:, rows].astype(F32), 0.0, NEG)
            low = lax.broadcasted_iota(jnp.int32, (size, 128), 1) < 64

            def one_pair(pair, carried):
                lanes = tile(pair, 128)
                q, k, v, up = query[rows, lanes], keys[span, lanes], values[span, lanes], back[rows, lanes]
                q_t, up_t = q.T, up.T
                product = up_t.astype(F32) * mixed_t[lanes, rows].astype(F32)
                key_parts, value_parts = [], []
                for half in range(2):
                    scores = dot(own_lanes(k, half), q_t) * SCALE + bias[:size, :]
                    probs = jnp.exp2(scores - total[pl.ds(pair * 2 + half, 1), rows])
                    spread = dot(own_lanes(v, half), up_t)
                    delta = jnp.sum(product[half * 64 : half * 64 + 64], 0, keepdims=True)
                    scores_back = (probs * (spread - delta)).astype(BF16)
                    value_parts.append(dot(probs.astype(BF16), up))
                    key_parts.append(dot(scores_back, q))
                    spot = pl.ds(pl.multiple_of(pair * 128 + half * 64, 64), 64)
                    query_back_t[spot, rows] = (dot(keys_t[spot, span], scores_back) * 0.125).astype(BF16)
                value_acc[span, lanes] += jnp.where(low, *value_parts)
                key_acc[span, lanes] += jnp.where(low, *key_parts)
                return carried

            lax.fori_loop(0, width // 128, one_pair, 0, unroll=PAIRS)

        windowed(sizes, window[first + 1, index], run)
        return carry

    lax.fori_loop(0, length // block, one_block, 0)


def put_square(stage, grad, column, base):
    core = stage.coords[2]
    rows = grad.shape[0] // 16
    blocks = grad.astype(BF16).reshape(LINE, 2, 2, rows, grad.shape[1])
    for result, wanted in ((stage.keep, 0), (stage.send_, 1)):
        picked = jnp.where(core == wanted, blocks[:, :, 0], blocks[:, :, 1])
        for outer in range(2):
            for chunk in range(2):
                result[outer * 2 + column, :, base + chunk * rows : base + (chunk + 1) * rows, :] = picked[
                    :, outer, :, chunk * 128 : (chunk + 1) * 128
                ]


def self_forward_body(stage):
    affine, loose, weight = stage.affine, stage.loose, stage.weight
    copies = piece_copies(
        stage, stage.raw, stage.raw_sems, lambda dp, inner: [(slice(0, 7), loose.at[:, dp, :, tile(inner, 256)])]
    )
    stage.begin()
    for copy in copies:
        copy.wait()
    for w in range(3):
        for dp in range(16):
            for half in range(2):
                weight[w, dp * 32 + half * 16 : dp * 32 + half * 16 + 16, :] = loose[2 * w + half, dp]
    flat = jnp.sum(loose[6].astype(F32), 0)
    flat = flat[:, :256] + flat[:, 256:]
    affine[:, :256] = flat[:8]
    affine[:, 256:] = flat[8:]
    stage.send.weight()
    stage.send.affine()
    normed_t = stage.normed_t
    length = normed_t.shape[1]

    def project(rows, index):
        z, _ = standard(stage.at.target(index)[rows, :].astype(F32))
        n = (z * affine[0:1, :] + affine[1:2, :]).astype(BF16)
        normed_t[:, rows] = n.T
        query, key, value = (dot(n, weight[place]).astype(BF16) for place in range(3))
        stage.query[rows, :] = query
        stage.key[rows, :] = key
        stage.value[rows, :] = value
        stage.send.query(index)
        stage.send.key(index)
        stage.send.value(index)
        stage.key_t[:, rows] = key.T
        stage.value_t[:, rows] = value.T

    blocks_of_tokens(length, project)
    stage.send.normed_t()
    stage.send.key_t()
    attend(
        stage.query, stage.key_t, stage.value_t, stage.seg, stage.seg, stage.window, stage.mixed, stage.mixed_t,
        stage.total, stage.bias, stage.sums_t, SELF_SIZES, SELF_BLOCK, 0,
    )


def self_forward(coords, window, target, seg, pieces):
    length, width = target.shape
    low, turned = ((length, width), BF16), ((width, length), BF16)
    return staged(
        "self_forward", self_forward_body, dict(coords=coords, window=window), dict(target=Rows(target), seg=seg),
        dict(
            weight=((3, width, width), BF16), affine=((8, width), F32), query=Rows(low), key=Rows(low),
            value=Rows(low), key_t=turned, normed_t=turned, mixed=low, mixed_t=turned,
            total=((width // 64, length), F32),
        ),
        dict(
            loose=((7, 16, 16, width), BF16), value_t=turned, bias=((SELF_BLOCK, SELF_SIZES[-1]), F32),
            sums_t=((width // 64, SELF_BLOCK), F32),
        ),
        raw=pieces, raw_sems=32,
        weight=20,
    )


def cross_forward_body(stage):
    weight = stage.weight
    copies = piece_copies(
        stage,
        stage.raw,
        stage.raw_sems,
        lambda dp, inner: [(slice(0, 5), weight.at[:, tile(dp, 32), tile(inner, 256)])],
        doubled=True,
    )
    stage.begin()
    for copy in copies:
        copy.wait()
    stage.send.weight()
    source, affine = stage.source, stage.affine
    first = stage.first
    length = first.shape[0]
    padded = stage.padded
    count = source.shape[0]
    padded[...] = jnp.zeros(padded.shape, BF16)
    padded[:count, :] = source[...]
    stage.key[...] = dot(padded[...], weight[2]).astype(BF16)
    stage.value[...] = dot(padded[...], weight[3]).astype(BF16)
    stage.key_t[...] = stage.key[...].T
    stage.value_t[...] = stage.value[...].T
    stage.send.key()
    stage.send.key_t()
    stage.send.value()

    def project(rows, index):
        v = stage.at.target(index)[rows, :].astype(F32) + dot(stage.at.mixed1(index)[rows, :], weight[0])
        first[rows, :] = v
        stage.send.first(index)
        z, _ = standard(v)
        n = (z * affine[2:3, :] + affine[3:4, :]).astype(BF16)
        stage.normed2_t[:, rows] = n.T
        stage.query[rows, :] = dot(n, weight[1]).astype(BF16)
        stage.send.query(index)

    blocks_of_tokens(length, project)
    stage.send.normed2_t()
    attend(
        stage.query, stage.key_t, stage.value_t, stage.seg, stage.key_seg, stage.window, stage.mixed,
        stage.mixed_t, stage.total, stage.bias, stage.sums_t, CROSS_SIZES, CROSS_BLOCK, 2,
    )
    stage.send.mixed_t()
    stage.send.total()

    def finish(rows, index):
        m = stage.mixed[rows, :]
        v = first[rows, :] + dot(m, weight[4])
        stage.second[rows, :] = v
        z, _ = standard(v)
        n = (z * affine[4:5, :] + affine[5:6, :]).astype(BF16)
        stage.normed[rows, :] = n
        stage.normed_t[:, rows] = n.T
        stage.send.second(index)
        stage.send.normed(index)

    blocks_of_tokens(length, finish)


def cross_forward(coords, window, target, mixed1, affine, source, seg, key_seg, pieces):
    length, width = target.shape
    count = key_seg.shape[1]
    low, turned, full = ((length, width), BF16), ((width, length), BF16), ((length, width), F32)
    return staged(
        "cross_forward", cross_forward_body, dict(coords=coords, window=window),
        dict(
            mixed1=Rows(mixed1), target=Rows(target), affine=affine, source=source, seg=seg, key_seg=key_seg
        ),
        dict(
            weight=((5, width, width), BF16), key=((count, width), BF16), key_t=((width, count), BF16), value=((count, width), BF16),
            first=Rows(full), normed2_t=turned, query=Rows(low), mixed_t=turned,
            total=((width // 64, length), F32), second=Rows(full), normed=Rows(low), normed_t=turned,
        ),
        dict(
            bias=((CROSS_BLOCK, CROSS_SIZES[-1]), F32), sums_t=((width // 64, CROSS_BLOCK), F32),
            value_t=((width, count), BF16), mixed=low, padded=((count, width), BF16),
        ),
        raw=pieces, raw_sems=32,
        weight=20,
    )


FF_BLOCK = 256
FF_TOKENS = 512


def feed_forward_body(stage):
    expand, shrink, active, hidden_back = stage.expand, stage.shrink, stage.active, stage.hidden_back
    loose_expand, loose_shrink = stage.loose_expand, stage.loose_shrink
    coords, copies = stage.coords, []
    for part in range(8):
        core, kind = part // 4, part % 4
        for entry in range(8):
            first, line = entry // 4, coords[0] ^ (entry % 4)
            outer, inner = (kind, first) if kind < 2 else (first, kind - 2)
            outer, inner = coords[1] ^ outer, coords[3] ^ inner
            dp = (line * 2 + outer) * 2 + (coords[2] ^ core)
            if kind < 2:
                spot = loose_expand.at[tile(inner, 4), tile(dp, 32), :]
            else:
                spot = loose_shrink.at[inner, tile(dp, 4)]
            source = stage.raw[part].at[first, entry % 4]
            copies.append(pltpu.make_async_copy(source, spot, stage.raw_sems[len(copies)]))
            copies[-1].start()
    stage.begin()
    core = coords[2]
    width, hidden = expand.shape
    for copy in copies:
        copy.wait()
    for part in range(hidden // FF_BLOCK):
        expand[:, part * FF_BLOCK : (part + 1) * FF_BLOCK] = loose_expand[part]
    for side in range(2):
        shrink[:, side * width // 2 : (side + 1) * width // 2] = loose_shrink[side].reshape(hidden, width // 2)
    normed, back = stage.normed, stage.back
    normed_t, back_t = stage.normed_t, stage.back_t
    length = normed.shape[0]
    back_t[...] = back[...].T

    def one_part(part):
        lanes = slice(part * FF_BLOCK, (part + 1) * FF_BLOCK)
        for index in range(length // FF_TOKENS):
            rows = slice(index * FF_TOKENS, (index + 1) * FF_TOKENS)
            v = dot(normed[rows, :], expand[:, lanes])
            up = dot_nt(back[rows, :], shrink[lanes, :])
            square = v * v
            half = 0.5 + 0.5 * jnp.tanh(v * (0.7978845608028654 + 0.035677408136300125 * square))
            value = v * half
            slope = half + value * (1.0 - half) * (1.5957691216057308 + 0.21406444881780075 * square)
            active[rows, lanes] = value.astype(BF16)
            hidden_back[rows, lanes] = (up * slope).astype(BF16)
        grad = dot(normed_t[...], hidden_back[:, lanes]).astype(BF16)
        blocks = grad.reshape(LINE, 2, 2, width // 16, FF_BLOCK)
        inner, chunk = part // 4, part % 4 * 2
        for result, wanted in ((stage.keep, 0), (stage.send_, 1)):
            picked = jnp.where(core == wanted, blocks[:, :, 0], blocks[:, :, 1])
            for outer in range(2):
                for side in range(2):
                    first = (chunk + side) * width // 16
                    result[outer * 2 + inner, :, first : first + width // 16, :] = picked[
                        :, outer, :, side * 128 : (side + 1) * 128
                    ]
        grad = dot(back_t[...], active[:, lanes]).astype(BF16)
        line, outer = part // 2, part % 2
        for result, wanted in ((stage.keep, 0), (stage.send_, 1)):
            picked = jnp.where(core == wanted, grad[:, :128], grad[:, 128:])
            for side in range(2):
                result[outer * 2 + side, line, width // 2 :, :] = picked[side * width // 2 : (side + 1) * width // 2]

    for part in range(hidden // FF_BLOCK):
        one_part(part)
    stage.send.send_()
    stage.send.keep()

    def finish(rows, index):
        stage.normed_back[rows, :] = dot_nt(hidden_back[rows, :], expand[...])
        stage.send.normed_back(index)
        stage.output[rows, :] = (stage.at.second(index)[rows, :] + dot(active[rows, :], shrink[...])).astype(BF16)
        stage.send.output(index)

    blocks_of_tokens(length, finish)


def feed_forward(coords, normed, normed_t, second, back, pieces):
    length, width = normed.shape
    hidden = 4 * width
    part = ((4, LINE, width, 128), BF16)
    wide = ((length, hidden), BF16)
    return staged(
        "feed_forward", feed_forward_body, dict(coords=coords),
        dict(normed=normed, back=back, normed_t=normed_t, second=Rows(second)),
        dict(
            send_=part, keep=part, normed_back=Rows(((length, width), F32)), output=Rows(((length, width), BF16))
        ),
        dict(
            loose_expand=((hidden // FF_BLOCK, width, FF_BLOCK), BF16),
            loose_shrink=((2, hidden // 32, 32, width // 2), BF16),
            expand=((width, hidden), BF16), shrink=((hidden, width), BF16), active=wide, hidden_back=wide,
            back_t=((width, length), BF16),
        ),
        raw=pieces, raw_sems=64,
        weight=20,
    )


def add_affine(stage, row, gain, bias):
    stage.affine_back[row : row + 1, :] += jnp.sum(gain, 0, keepdims=True)
    stage.affine_back[row + 1 : row + 2, :] += jnp.sum(bias, 0, keepdims=True)


def norm_back_body(stage):
    affine = stage.affine
    stage.affine_back[...] = jnp.zeros(stage.affine_back.shape, F32)

    def run(rows, index):
        upstream = stage.at.normed_back(index)[rows, :]
        grad, gain = standard_back(stage.at.second(index)[rows, :], affine[4:5, :], upstream)
        add_affine(stage, 4, gain, upstream)
        grad = grad + stage.at.back(index)[rows, :].astype(F32)
        stage.second_back[rows, :] = grad
        stage.mixed_back[rows, :] = dot_nt(grad.astype(BF16), stage.weight[...]).astype(BF16)
        stage.send.second_back(index)
        stage.send.mixed_back(index)

    blocks_of_tokens(stage.second_back.shape[0], run)


def norm_back(affine, weight, second, normed_back, back):
    length, width = second.shape
    low, full = ((length, width), BF16), ((length, width), F32)
    return staged(
        "norm_back", norm_back_body, {},
        dict(
            affine=affine, normed_back=Rows(normed_back), second=Rows(second), back=Rows(back),
            weight=Part(weight, (width, width), lambda ref, scalars: ref.at[4]),
        ),
        dict(affine_back=((8, width), F32), mixed_back=Rows(low), second_back=Rows(full)),
        {},
        weight=3,
    )


def square_grads(stage, base, left_t, right, turned):
    for column in range(2):
        cols = slice(column * 256, (column + 1) * 256)
        grad = dot_nt(left_t[...], right[cols, :]) if turned else dot(left_t[...], right[:, cols])
        put_square(stage, grad, column, base)


def cross_back_body(stage):
    query = stage.query
    key_acc, value_acc, query_back = stage.key_acc, stage.value_acc, stage.query_back
    attend_back(
        query, stage.key, stage.key_t, stage.value, stage.mixed_back, stage.mixed_t, stage.total, stage.seg,
        stage.key_seg, stage.window, query_back, key_acc, value_acc, stage.bias, CROSS_BACK_SIZES, CROSS_BACK_BLOCK, 6,
    )
    affine, weight, key_back, value_back = stage.affine, stage.weight, stage.key_back, stage.value_back
    key_back[...] = (key_acc[...] * 0.125).astype(BF16)
    value_back[...] = value_acc[...].astype(BF16)
    source_back = dot_nt(key_back[...], weight[2]) + dot_nt(value_back[...], weight[3])
    stage.source_back[...] = source_back[: stage.source_back.shape[0]]
    stage.send.source_back()
    stage.affine_back[...] = stage.affine_before[...]
    first_low = stage.first_low

    def run(rows, index):
        upstream = dot(weight[1], query_back[:, rows]).T
        grad, gain = standard_back(stage.first[rows, :], affine[2:3, :], upstream)
        add_affine(stage, 2, gain, upstream)
        second_back = stage.second_back[rows, :]
        stage.out_low[rows, :] = second_back.astype(BF16)
        grad = grad + second_back
        stage.first_back[rows, :] = grad
        low = grad.astype(BF16)
        first_low[rows, :] = low
        stage.mixed1_back[rows, :] = dot_nt(low, weight[0]).astype(BF16)

    blocks_of_tokens(query.shape[0], run)
    stage.send.first_back()
    stage.send.mixed1_back()
    stage.send.affine_back()
    rows_of = weight.shape[1] // 16 * 2
    square_grads(stage, 0, stage.mixed1_t, first_low, False)
    square_grads(stage, rows_of, stage.normed_t, query_back, True)
    padded, source_t = stage.padded, stage.source_t
    padded[...] = jnp.zeros(padded.shape, BF16)
    padded[: stage.source.shape[0], :] = stage.source[...]
    source_t[...] = padded[...].T
    square_grads(stage, 2 * rows_of, source_t, key_back, False)
    square_grads(stage, 3 * rows_of, source_t, value_back, False)
    square_grads(stage, 4 * rows_of, stage.mixed_t, stage.out_low, False)


def cross_back(coords, window, ins, source_length):
    ins_ = types.SimpleNamespace(**ins)
    length, width = ins_.query.shape
    count = ins_.key.shape[0]
    low, full = ((length, width), BF16), ((length, width), F32)
    keyed = (count, width)
    part = ((4, LINE, 5 * width // 8, 128), BF16)
    return staged(
        "cross_back", cross_back_body, dict(coords=coords, window=window), ins,
        dict(
            keep=part, send_=part, first_back=full, mixed1_back=low, affine_back=((8, width), F32),
            source_back=((source_length, width), F32),
        ),
        dict(
            key_acc=(keyed, F32), value_acc=(keyed, F32), query_back=((width, length), BF16), first_low=low, out_low=low,
            key_back=(keyed, BF16), value_back=(keyed, BF16), bias=((CROSS_BACK_SIZES[-1], CROSS_BACK_BLOCK), F32),
            padded=(keyed, BF16), source_t=((width, count), BF16),
        ),
        weight=20,
    )


AFFINE_ROWS = 16


def pack_first_body(wide, stage):
    for place in range(3):
        for half in range(2):
            stage.packed[2 * place + half] = stage[place][half * 16 : half * 16 + 16, :]
    coords = stage.coords
    own = stage.norms[...]
    width = 2 * stage.packed.shape[2]
    row_at, from_row = (lax.broadcasted_iota(jnp.int32, (8, own.shape[0]), axis) for axis in range(2))
    from_lane, lane_at = (lax.broadcasted_iota(jnp.int32, (wide, width), axis) for axis in range(2))
    down = (row_at == coords[3] * 3 + from_row).astype(BF16)
    right = (lane_at == coords[4] + from_lane).astype(BF16)
    placed = dot(down, dot(own, right).astype(BF16)).astype(BF16)
    stage.packed[6] = jnp.concatenate([placed[:, : width // 2], placed[:, width // 2 :]], 0)


def pack_first(coords, weights, norms):
    ins = {**dict(enumerate(weights)), **dict(norms=norms)}
    outs = dict(packed=((7, 16, weights[0].shape[1]), BF16))
    body = functools.partial(pack_first_body, norms.shape[1])
    return staged("pack", body, dict(coords=coords), ins, outs, {}, limit=SMALL).packed


def join_pairs_body(stage):
    for place in range(4):
        result = stage.one if place < 2 else stage.two
        result[place % 2] = stage[place][...]
        if place == 1:
            stage.send.one()


def join_pairs(one, two):
    shape = (2, *one[0].shape)
    outs = dict(one=(shape, BF16), two=(shape, BF16))
    result = staged("join", join_pairs_body, {}, dict(enumerate([*one, *two])), outs, {}, limit=SMALL)
    return [result.one, result.two]


def find_windows(seg, keys, sizes, block, count):
    lane = lax.broadcasted_iota(jnp.int32, (1, 128), 1)
    starts, kinds = jnp.zeros((1, 128), jnp.int32), jnp.zeros((1, 128), jnp.int32)
    for index in range(seg.shape[1] // block):
        first, last = seg[:, index * block : index * block + 1], seg[:, (index + 1) * block - 1 : (index + 1) * block]
        low = jnp.sum((keys < first).astype(F32), 1, keepdims=True).astype(jnp.int32) // 128 * 128
        high = (jnp.sum((keys <= last).astype(F32), 1, keepdims=True).astype(jnp.int32) + 127) // 128 * 128
        need = high - low
        kind = sum(((need > size).astype(jnp.int32) for size in sizes[:-1]), jnp.zeros_like(need))
        size = sum((jnp.where(kind == place, size, 0) for place, size in enumerate(sizes)), jnp.zeros_like(need))
        starts = jnp.where(lane == index, jnp.minimum(low, count - size), starts)
        kinds = jnp.where(lane == index, kind, kinds)
    return starts, kinds


def pack_rest_body(stage):
    for place in range(5):
        stage.second[place] = stage[place][...]
    for place in range(4):
        stage.third[place] = stage.expand[:, place * 256 : place * 256 + 256]
        stage.third[4 + place] = stage.shrink[place * 32 : place * 32 + 32, :]
    seg, source_seg = stage.seg[...], stage.source_seg[...]
    count = stage.key_seg.shape[1]
    stage.key_seg[...] = jnp.full(stage.key_seg.shape, -1, jnp.int32)
    stage.key_seg[:, : source_seg.shape[1]] = jnp.where(stage.source_keep[...] > 0, source_seg, -1)
    rows = (
        *find_windows(seg, seg, SELF_SIZES, SELF_BLOCK, seg.shape[1]),
        *find_windows(seg, source_seg, CROSS_SIZES, CROSS_BLOCK, count),
        *find_windows(seg, seg, BACK_SIZES, SELF_BLOCK, seg.shape[1]),
        *find_windows(seg, source_seg, CROSS_BACK_SIZES, CROSS_BACK_BLOCK, count),
    )
    stage.window[...] = jnp.zeros(stage.window.shape, jnp.int32)
    for place, row in enumerate(rows):
        stage.window[place : place + 1, :] = row


def pack_rest(weights, expand, shrink, seg, source_seg, source_keep):
    ins = {
        **dict(enumerate(weights)),
        **dict(expand=expand, shrink=shrink, seg=seg, source_seg=source_seg, source_keep=source_keep),
    }
    outs = dict(
        second=((5, 32, 256), BF16), third=((8, 32, 256), BF16), window=((8, 128), jnp.int32),
        key_seg=((1, CROSS_SIZES[-1]), jnp.int32),
    )
    return staged("pack", pack_rest_body, {}, ins, outs, {})


def self_back_body(stage):
    query = stage.query
    key_acc, value_acc, query_back = stage.key_acc, stage.value_acc, stage.query_back
    attend_back(
        query, stage.key, stage.key_t, stage.value, stage.mixed_back, stage.mixed_t, stage.total, stage.seg,
        stage.seg, stage.window, query_back, key_acc, value_acc, stage.bias, BACK_SIZES, SELF_BLOCK, 4,
    )
    weight, affine = stage.weight, stage.affine
    key_back, value_back = stage.key_back, stage.value_back
    key_back[...] = (key_acc[...] * 0.125).astype(BF16)
    value_back[...] = value_acc[...].astype(BF16)
    stage.affine_back[...] = stage.affine_before[...]

    def run(rows, index):
        upstream = dot_nt(key_back[rows, :], weight[1]) + dot_nt(value_back[rows, :], weight[2])
        upstream = upstream + dot(weight[0], query_back[:, rows]).T
        grad, gain = standard_back(stage.target[rows, :].astype(F32), affine[0:1, :], upstream)
        add_affine(stage, 0, gain, upstream)
        stage.target_back[rows, :] = grad + stage.first_back[rows, :]
        stage.send.target_back(index)

    blocks_of_tokens(query.shape[0], run)
    width = query.shape[1]
    rows_of = width // 16 * 2
    square_grads(stage, 0, stage.normed_t, query_back, True)
    square_grads(stage, rows_of, stage.normed_t, key_back, False)
    square_grads(stage, 2 * rows_of, stage.normed_t, value_back, False)
    norms = stage.affine_back[...]
    norms = jnp.concatenate([norms, jnp.zeros_like(norms)], 0)
    for inner in range(2):
        low = (norms if inner == 0 else jnp.concatenate([norms[3:], norms[:3]], 0)).astype(BF16)
        for line in range(LINE):
            for result in (stage.keep, stage.send_):
                for outer in range(2):
                    result[outer * 2 + inner, line, 3 * rows_of :, :] = low[:, line * 128 : (line + 1) * 128]


def self_back(coords, window, ins):
    ins_ = types.SimpleNamespace(**ins)
    length, width = ins_.query.shape
    low, turned = ((length, width), BF16), ((width, length), BF16)
    part = ((4, LINE, 3 * width // 8 + AFFINE_ROWS, 128), BF16)
    return staged(
        "self_back", self_back_body, dict(coords=coords, window=window), ins,
        dict(send_=part, keep=part, target_back=Rows(((length, width), F32))),
        dict(
            key_acc=((length, width), F32), value_acc=((length, width), F32), query_back=turned, key_back=low,
            value_back=low, affine_back=((8, width), F32), bias=((BACK_SIZES[-1], SELF_BLOCK), F32),
        ),
        weight=20,
    )


def sums_body(jobs, stage):
    place = 0
    for index, job in enumerate(jobs):
        total = stage[place, index][...].astype(F32)
        for more in range(1, len(job)):
            total = total + stage[place + more, index][...].astype(F32)
        place += len(job)
        stage.outs[index][0][...] = total.astype(BF16)
        stage._send(index)


def sums(coords, jobs):
    ins = {}
    for index, job in enumerate(jobs):
        for part in job:
            ins[len(ins), index] = part
    outs = {index: (job[0].shape, BF16) for index, job in enumerate(jobs)}
    body = functools.partial(sums_body, jobs)
    return list(vars(staged("sums", body, dict(coords=coords), ins, outs, {}, limit=SMALL)).values())


def plane_part(array, step):
    def choose(ref, scalars):
        coords = scalars.coords
        return ref.at[(coords[1] ^ (step >> 1)) * 2 + (coords[3] ^ (step & 1))]

    return Part(array, array.shape[1:], choose)


def line_part(array, step):
    return Part(array, array.shape[1:], lambda ref, scalars: ref.at[(scalars.coords[0] + step) & 3])


ORDER = (1, 2, 3, 0)


def chip_jobs(keep, away):
    return [[plane_part(keep, step), plane_part(away, step)] for step in ORDER]


def plane_jobs(arrays):
    return [[line_part(array, step) for array in arrays] for step in ORDER]


def last_sums_body(hidden, squares, wide, stage):
    def total_of(first):
        parts = [stage[first + place][...].astype(F32) for place in range(4)]
        return parts[0] + parts[1] + (parts[2] + parts[3])

    results = [value[0] for value in stage.outs.values()]
    if hidden:
        total = total_of(0)
        half = total.shape[0] // 2
        rows = half // 8
        for chunk in range(8):
            results[0][:, chunk * 128 : (chunk + 1) * 128] = total[chunk * rows : (chunk + 1) * rows]
        results[1][...] = total[half:].T
        results = results[2:]
    first = 4 if hidden else 0
    for count in squares:
        total = total_of(first)
        first += 4
        for place in range(count):
            for chunk in range(2):
                row = (2 * place + chunk) * 32
                results[place][:, chunk * 128 : (chunk + 1) * 128] = total[row : row + 32]
        results = results[count:]
        if total.shape[0] > count * 64:
            lane = (stage.coords[1] * 2 + stage.coords[2]) * 32 + stage.coords[5]
            norms = pltpu.roll(total[count * 64 : count * 64 + 8], (128 - lane) & 127, 1)
            results[0][...] = norms[:3, :wide]
            results = results[1:]


def last_sums(coords, hidden, squares, wide):
    arrays = [array for group in ([hidden] if hidden else []) + squares for array in group]
    outs = {}
    if hidden:
        rows = hidden[0].shape[0]
        outs[(0,)] = ((rows // 16, 1024), F32)
        outs[(1,)] = ((128, rows // 2), F32)
    counts = []
    for group in squares:
        counts.append(group[0].shape[0] // 64)
        for _ in range(counts[-1]):
            outs[(len(outs),)] = ((32, 256), F32)
        if group[0].shape[0] % 64:
            outs[(len(outs),)] = ((3, wide), F32)
    body = functools.partial(last_sums_body, bool(hidden), counts, wide)
    result = staged("last_sums", body, dict(coords=coords), dict(enumerate(arrays)), outs, {}, limit=SMALL)
    return list(vars(result).values())


SWAP = [(0, 1), (1, 0)]
SHIFTS = [[(i, (i + k) % LINE) for i in range(LINE)] for k in range(LINE)]
CROSS = [[(i, i ^ k) for i in range(4)] for k in range(4)]
PLANE = ("b", "i")


def tie(*values):
    return lax.optimization_barrier(values)


def join(arrays):
    return jnp.concatenate(arrays, 0).reshape(len(arrays), *arrays[0].shape)


def along_line(array):
    return [array] + [lax.ppermute(array, "a", SHIFTS[k]) for k in (1, 2, 3)]


def along_plane(array):
    return [array] + [lax.ppermute(array, PLANE, CROSS[k]) for k in (1, 2, 3)]


def line_pair(array, step):
    return jnp.concatenate([array, lax.ppermute(array, "a", CROSS[step])], 0)


def across_cores(arrays):
    return arrays + [lax.ppermute(array, "c", SWAP) for array in arrays]


def swap_cores(array):
    return lax.ppermute(array, "c", SWAP)


def to_plane(arrays):
    return [lax.ppermute(array, PLANE, CROSS[k]) for array, k in zip(arrays, (1, 2, 3))] + arrays[3:4]


def to_line(arrays):
    return [lax.ppermute(array, "a", SHIFTS[k]) for array, k in zip(arrays, (1, 2, 3))] + arrays[3:4]


def shards(
    target,
    source,
    target_segment,
    source_segment,
    source_keep,
    self_query,
    self_key,
    self_value,
    self_output,
    cross_query,
    cross_key,
    cross_value,
    cross_output,
    expand_weight,
    shrink_weight,
    norm_affine,
    cotangent,
):
    src_length = source.shape[1]
    rest = lax.axis_size("r")
    wide = norm_affine.shape[1]
    a, b, c, r, i = (lax.axis_index(name) for name in "abcri")
    coords = jnp.stack([a, b, c, i, (((a * 2 + b) * 2 + c) * rest + r) * wide, r * wide]).astype(jnp.int32)

    def whole_rows(shard):
        return lax.all_gather(shard, "r", axis=0, tiled=True) if rest > 1 else shard

    shard_one = pack_first(coords, [whole_rows(w) for w in (self_query, self_key, self_value)], norm_affine)
    if rest > 1:
        norms = lax.psum(shard_one[6].astype(F32), "r").astype(BF16)
        shard_one = jnp.concatenate([shard_one[:6], norms[None]], 0)
    x, upstream, sent = target[0], cotangent[0], source[0]
    line_one = along_line(shard_one)
    others = [whole_rows(w) for w in (self_output, cross_query, cross_key, cross_value, cross_output)]
    rest_of = pack_rest(
        others, whole_rows(expand_weight), whole_rows(shrink_weight), target_segment, source_segment, source_keep
    )
    seg, key_seg, window = target_segment, rest_of.key_seg, rest_of.window
    near_one = along_plane(join(line_one))
    pair_two, pair_three = line_pair(rest_of.second, 1), line_pair(rest_of.third, 1)
    near_one[0], pair_two, pair_three = tie(near_one[0], pair_two, pair_three)
    joined_two = line_pair(pair_two, 2).reshape(4, 5, 32, -1)
    halves = (pair_three.reshape(2, 8, 32, -1), lax.ppermute(pair_three, "a", CROSS[2]).reshape(2, 8, 32, -1))
    parts = [jnp.concatenate([half[:, :4] for half in halves], 0), jnp.concatenate([half[:, 4:] for half in halves], 0)]
    pieces_one = across_cores(near_one)
    joined_two, pieces_one = tie(joined_two, pieces_one)
    stage_two = along_plane(joined_two)
    ready, *parts = tie(x, *parts)
    sides = [lax.ppermute(parts[0], "i", SWAP), lax.ppermute(parts[1], "b", SWAP)]
    one = self_forward(coords, window, ready, seg, pieces_one)
    sides[0], sides[1], stage_two[0], one.mixed = tie(*sides, stage_two[0], one.mixed)
    sides = join_pairs(*zip(parts, sides))
    far = [lax.ppermute(sides[0], "b", SWAP), lax.ppermute(sides[1], "i", SWAP)]
    pieces_two = across_cores([tie(array, one.mixed)[0] for array in stage_two])
    two = cross_forward(coords, window, x, one.mixed, one.affine, sent, seg, key_seg, pieces_two)
    pieces_three = across_cores(
        [sides[0], tie(far[0], two.normed)[0], sides[1], tie(far[1], two.normed)[0]]
    )
    three = feed_forward(coords, two.normed, two.normed_t, two.second, upstream, pieces_three)
    away_three = swap_cores(three.send_)
    four = norm_back(one.affine, two.weight, two.second, three.normed_back, upstream)
    away_three, four.mixed_back = tie(away_three, four.mixed_back)
    chip_three = sums(coords, chip_jobs(three.keep, away_three))
    chip_three, four.mixed_back = tie(chip_three, four.mixed_back)
    plane_three = to_plane(chip_three)
    five = cross_back(
        coords,
        window,
        dict(
            query=two.query, key=two.key, seg=seg, key_seg=key_seg, mixed_t=two.mixed_t, total=two.total,
            value=two.value, mixed_back=four.mixed_back, key_t=two.key_t, weight=two.weight,
            affine=one.affine, affine_before=four.affine_back, first=two.first, second_back=four.second_back,
            mixed1_t=one.mixed_t, normed_t=two.normed2_t, source=sent,
        ),
        src_length,
    )
    five.send_, plane_three = tie(five.send_, plane_three)
    away_two = swap_cores(five.send_)
    line_three = to_line(sums(coords, plane_jobs(plane_three)))
    away_two, line_three[3] = tie(away_two, line_three[3])
    chip_two = sums(coords, chip_jobs(five.keep, away_two))
    chip_two, five.mixed1_back = tie(chip_two, five.mixed1_back)
    plane_two = to_plane(chip_two)
    six = self_back(
        coords,
        window,
        dict(
            query=one.query, key=one.key, seg=seg, total=one.total,
            value=one.value, mixed_back=five.mixed1_back, mixed_t=one.mixed_t, key_t=one.key_t,
            weight=one.weight, affine=one.affine, affine_before=five.affine_back, target=x,
            first_back=five.first_back, normed_t=one.normed_t,
        ),
    )
    six.send_, plane_two, line_three = tie(six.send_, plane_two, line_three)
    away_one = swap_cores(six.send_)
    tail = sums(coords, chip_jobs(six.keep, away_one) + plane_jobs(plane_two))
    plane_one = to_plane(tail[:4])
    line_two = to_line(tail[4:])
    plane_one, line_two[3] = tie(plane_one, line_two[3])
    own_one = sums(coords, plane_jobs(plane_one))
    line_one = to_line(own_one)
    line_three, line_one[3] = tie(line_three, line_one[3])
    hidden = last_sums(coords, line_three, [], wide)
    *squares, norms = last_sums(coords, [], [line_two, line_one], wide)
    if rest > 1:
        norms = lax.psum(norms, "r")

    def own_block(spread):
        return lax.psum_scatter(spread, "r", scatter_dimension=0, tiled=True) if rest > 1 else spread

    grads = [own_block(grad) for grad in (*squares[5:], *squares[:5], *hidden)]
    return (three.output[None], six.target_back[None], five.source_back[None], *grads, norms)


def solution(mesh):
    dp, inner = mesh.shape["dp"], mesh.shape["inner"]
    fine = Mesh(mesh.devices.reshape(4, 2, 2, dp // 16, inner), ("a", "b", "c", "r", "i"))
    split = ("a", "b", "c", "r")
    in_specs = (
        P((*split, "i"), None, None),
        P((*split, "i"), None, None),
        P((*split, "i"), None),
        P((*split, "i"), None),
        P((*split, "i"), None),
        P(split, "i"),
        P(split, "i"),
        P(split, "i"),
        P(split, "i"),
        P(split, "i"),
        P(split, "i"),
        P(split, "i"),
        P(split, "i"),
        P(split, "i"),
        P(split, "i"),
        P("i", split),
        P((*split, "i"), None, None),
    )
    out_specs = (
        P((*split, "i"), None, None),
        P((*split, "i"), None, None),
        P((*split, "i"), None, None),
        P(split, "i"),
        P(split, "i"),
        P(split, "i"),
        P(split, "i"),
        P(split, "i"),
        P(split, "i"),
        P(split, "i"),
        P(split, "i"),
        P(split, "i"),
        P(split, "i"),
        P("i", split),
    )
    return jax.shard_map(shards, mesh=fine, in_specs=in_specs, out_specs=out_specs, check_vma=False)
```
